32 devices in a mesh: region: 8 (over z, y), rep: 4 (over x, core).
Axes of the slice: x: 2, y: 2, z: 4, core: 2. Of those that a mesh axis runs over, the one named last changes fastest.
Arguments:
- initial_state: float32 [4, 8192, 227], P('rep', 'region'), may hold values from -6 to 6
- target_states: float32 [4, 2, 8192, 227], P('rep', None, 'region'), may hold values from -6 to 6
- var_means: float32 [227], replicated, may hold values from -6 to 6
- var_scales: float32 [227], replicated, may hold values from 0.5 to 2
- delta_scales: float32 [227], replicated, may hold values from 0.3 to 1
- edge_geometry: float32 [12288, 4], P('region'), may hold values from -6 to 6
- node_counts: int32 [8], P('region'), may hold values from 256 to 512, as said below
- edge_counts: int32 [8], P('region'), may hold values from 384 to 1536, as said below
- receivers: int32 [12288], P('region'), may hold values from 0 to 511, as said below
- senders: int32 [12288], P('region'), may hold values from 0 to 575
- send_lists: int32 [8, 8, 8], P('region'), may hold values from 0 to 511
- grid_nodes: int32 [8192], P('region'), may hold values from 0 to 511
- cell_area: float32 [8192], P('region')
- step_weights: int32 [2], replicated, may hold values from 1 to 4
- encoder_weight: float32 [227, 512], P(None, 'rep'), may hold values from -0.375 to 0.375
- encoder_moment: float32 [227, 512], P(None, 'rep'), may hold values from -4.7683716e-06 to 4.7683716e-06
- encoder_square: float32 [227, 512], P(None, 'rep'), may hold values from 2.972793e-12 to 1.1891172e-11
- embedder_weight: float32 [4, 512], P(None, 'rep'), may hold values from -3 to 3
- embedder_moment: float32 [4, 512], P(None, 'rep'), may hold values from -4.7683716e-06 to 4.7683716e-06
- embedder_square: float32 [4, 512], P(None, 'rep'), may hold values from 2.972793e-12 to 1.1891172e-11
- edge_weight: float32 [3, 1536, 512], P(None, None, 'rep'), may hold values from -0.15625 to 0.15625
- edge_moment: float32 [3, 1536, 512], P(None, None, 'rep'), may hold values from -4.7683716e-06 to 4.7683716e-06
- edge_square: float32 [3, 1536, 512], P(None, None, 'rep'), may hold values from 2.972793e-12 to 1.1891172e-11
- node_weight: float32 [3, 1024, 512], P(None, None, 'rep'), may hold values from -0.1875 to 0.1875
- node_moment: float32 [3, 1024, 512], P(None, None, 'rep'), may hold values from -4.7683716e-06 to 4.7683716e-06
- node_square: float32 [3, 1024, 512], P(None, None, 'rep'), may hold values from 2.972793e-12 to 1.1891172e-11
- decoder_weight: float32 [1024, 512], P(None, 'rep'), may hold values from -0.1875 to 0.1875
- decoder_moment: float32 [1024, 512], P(None, 'rep'), may hold values from -4.7683716e-06 to 4.7683716e-06
- decoder_square: float32 [1024, 512], P(None, 'rep'), may hold values from 2.972793e-12 to 1.1891172e-11
- inner_weight: float32 [9, 512, 512], P(None, None, 'rep'), may hold values from -0.25 to 0.25
- inner_moment: float32 [9, 512, 512], P(None, None, 'rep'), may hold values from -4.7683716e-06 to 4.7683716e-06
- inner_square: float32 [9, 512, 512], P(None, None, 'rep'), may hold values from 2.972793e-12 to 1.1891172e-11
- vector_weight: float32 [27, 512], P(None, 'rep')
- vector_moment: float32 [27, 512], P(None, 'rep'), may hold values from -2.670288e-05 to 2.670288e-05
- vector_square: float32 [27, 512], P(None, 'rep'), may hold values from 7.431983e-11 to 2.972793e-10
- head_weight: float32 [227, 512], P(None, 'rep'), may hold values from -0.25 to 0.25
- head_moment: float32 [227, 512], P(None, 'rep'), may hold values from -4.7683716e-06 to 4.7683716e-06
- head_square: float32 [227, 512], P(None, 'rep'), may hold values from 2.972793e-12 to 1.1891172e-11
Outputs:
- loss_total: float32 [], replicated
- weight_total: float32 [], replicated
- gradient_norm: float32 [], replicated
- encoder_first: float32 [227, 512], P(None, 'rep')
- encoder_second: float32 [227, 512], P(None, 'rep')
- encoder_master: float32 [227, 512], P(None, 'rep')
- embedder_first: float32 [4, 512], P(None, 'rep')
- embedder_second: float32 [4, 512], P(None, 'rep')
- embedder_master: float32 [4, 512], P(None, 'rep')
- edge_first: float32 [3, 1536, 512], P(None, None, 'rep')
- edge_second: float32 [3, 1536, 512], P(None, None, 'rep')
- edge_master: float32 [3, 1536, 512], P(None, None, 'rep')
- node_first: float32 [3, 1024, 512], P(None, None, 'rep')
- node_second: float32 [3, 1024, 512], P(None, None, 'rep')
- node_master: float32 [3, 1024, 512], P(None, None, 'rep')
- decoder_first: float32 [1024, 512], P(None, 'rep')
- decoder_second: float32 [1024, 512], P(None, 'rep')
- decoder_master: float32 [1024, 512], P(None, 'rep')
- inner_first: float32 [9, 512, 512], P(None, None, 'rep')
- inner_second: float32 [9, 512, 512], P(None, None, 'rep')
- inner_master: float32 [9, 512, 512], P(None, None, 'rep')
- vector_first: float32 [27, 512], P(None, 'rep')
- vector_second: float32 [27, 512], P(None, 'rep')
- vector_master: float32 [27, 512], P(None, 'rep')
- head_first: float32 [227, 512], P(None, 'rep')
- head_second: float32 [227, 512], P(None, 'rep')
- head_master: float32 [227, 512], P(None, 'rep')
- weight_copies: bfloat16 [4, 1766016], P('rep')
The draws below stay inside these ranges and needn't reach their ends.
Inputs may be any that keep to these rules, and one draw needn't show every extreme that they name: `node_counts`: 256 or more; one region holds exactly 512. `edge_counts`: 384 or more; one region holds exactly 1536. `receivers`: never falling along a region's edge slots and below that region's node count.
All inputs are finite; a program needn't handle non-finite values.
Results may differ from the reference program's by a relative error of at most 0.001.
The reference program's roundings to bfloat16 on the way count: a program that leaves them out, or rounds other values in their place, can miss the bound.
Values may be sent and summed in bfloat16 or wider, within the bound.
No kernel may reach another device: no remote copies, remote signals or barrier semaphores. Data moves between devices by JAX's collectives and lax.ppermute only.
A program may use at most 384 MiB of HBM per device.

```python
import math
import jax
import jax.numpy as jnp
from jax import lax

D = 512
VARS = 227
EF = 4
LAYERS = 3
STEPS = 2
STEP_COUNT = 10
NODE_CAP = 512
EDGE_CAP = 1536
SLOT = 8
GRID_DEV = 1024
SAMPLES = 4
EDGES = 12288
GRID = 8192
N_REGION = 8
N_REP = 4


def region_sizes(key):
    regions = EDGES // EDGE_CAP
    parts = jax.random.split(jax.random.fold_in(key, 101), 4)
    nodes = jax.random.randint(parts[0], (regions,), NODE_CAP // 2, NODE_CAP + 1)
    nodes = nodes.at[jax.random.randint(parts[1], (), 0, regions)].set(NODE_CAP)
    edges = jax.random.randint(parts[2], (regions,), EDGE_CAP // 4, EDGE_CAP + 1)
    edges = edges.at[jax.random.randint(parts[3], (), 0, regions)].set(EDGE_CAP)
    return (nodes.astype(jnp.int32), edges.astype(jnp.int32))


def draw_node_counts(key, part):
    return region_sizes(key)[0]


def draw_edge_counts(key, part):
    return region_sizes(key)[1]


def draw_receivers(key, part):
    nodes = region_sizes(key)[0]
    key = jax.random.fold_in(key, 7)
    regions = EDGES // EDGE_CAP
    raw = jax.random.randint(key, (regions, EDGE_CAP), 0, nodes[:, None])
    ordered = jnp.sort(raw, axis=1)
    ordered = ordered.at[:, EDGE_CAP - 1].set(nodes - 1)
    return ordered.reshape(-1).astype(jnp.int32)


def draw_cell_area(key, part):
    key = jax.random.fold_in(key, 9)
    regions = GRID // GRID_DEV
    place = (jnp.arange(GRID) // GRID_DEV).astype(jnp.float32) / max(regions - 1, 1)
    rise = 1.0 + 2.0 * place
    base = jax.random.uniform(key, (GRID,), jnp.float32, 0.5, 1.5)
    return rise * base


def draw_vector_weight(key, part):
    key = jax.random.fold_in(key, 5)
    first, second = jax.random.split(key)
    count = 9 + 6 * LAYERS
    column = jnp.arange(D, dtype=jnp.float32) / (D - 1)
    kind = jnp.arange(count) % 3
    rise = 0.5 + column
    spread = jax.random.uniform(second, (count, D), jnp.float32, 0.8, 1.2)
    noise = 0.3 * jax.random.normal(first, (count, D), jnp.float32)
    return jnp.where((kind == 1)[:, None], rise[None, :] * spread, noise)


def with_ends(entries, key, smallest, largest):
    index_at = [jax.random.randint(jax.random.fold_in(key, axis), (), 0, length) for axis, length in enumerate(entries.shape)]
    main_axis = entries.shape.index(max(entries.shape))
    beside = index_at[:main_axis] + [(index_at[main_axis] + 1) % entries.shape[main_axis]] + index_at[main_axis + 1:]
    return entries.at[tuple(index_at)].set(smallest).at[tuple(beside)].set(largest)


def levels(stream_key, dims, shards, least, top_value):
    factor_of, own = 1.0, jax.random.fold_in(stream_key, 6)
    for axis_at, blocks in shards:
        draws = jnp.exp(jax.random.uniform(jax.random.fold_in(own, axis_at), (blocks,), jnp.float32, least / len(shards), top_value / len(shards)))
        factor_of = factor_of * jnp.repeat(draws, dims[axis_at] // blocks).reshape([-1 if axis == axis_at else 1 for axis in range(len(dims))])
    return factor_of


def normal_values(own_key, extent, scale, most, cuts=(), kind=jnp.bfloat16):
    values = jax.random.normal(own_key, extent, jnp.float32) * scale
    if len(cuts) > 0:
        values = levels(own_key, extent, cuts, -0.22, 0.18) * values
    return jnp.clip(values, min=-most, max=most).astype(kind)


def setup_inputs(seed: int = 0) -> dict:
    splits = jax.random.split(jax.random.key(seed), 39)
    initial_state = normal_values(splits[0], (SAMPLES, GRID, VARS), 1.0, 6.0, ((0, 4), (1, 8)), jnp.float32)
    target_states = normal_values(splits[1], (SAMPLES, STEPS, GRID, VARS), 1.0, 6.0, ((0, 4), (2, 8)), jnp.float32)
    var_means = normal_values(splits[2], (VARS,), 1.0, 6.0, (), jnp.float32)
    var_scales = jnp.clip(jnp.exp(jax.random.uniform(splits[3], (VARS,), jnp.float32, math.log(0.5), math.log(2.0))), 0.5, 2.0)
    delta_scales = jnp.clip(jnp.exp(jax.random.uniform(splits[4], (VARS,), jnp.float32, math.log(0.3), math.log(1.0))), 0.3, 1.0)
    edge_geometry = normal_values(splits[5], (EDGES, EF), 1.0, 6.0, ((0, 8),), jnp.float32)
    node_counts = draw_node_counts(jax.random.fold_in(splits[38], 71), 0)
    edge_counts = draw_edge_counts(jax.random.fold_in(splits[38], 71), 0)
    receivers = draw_receivers(jax.random.fold_in(splits[38], 71), 0)
    senders = with_ends(jax.random.randint(splits[9], (EDGES,), 0, NODE_CAP + N_REGION * SLOT), jax.random.fold_in(splits[9], 1), 0, (NODE_CAP + N_REGION * SLOT) - 1).astype(jnp.int32)
    send_lists = with_ends(jax.random.randint(splits[10], (N_REGION, N_REGION, SLOT), 0, NODE_CAP), jax.random.fold_in(splits[10], 1), 0, NODE_CAP - 1).astype(jnp.int32)
    grid_nodes = with_ends(jax.random.randint(splits[11], (GRID,), 0, NODE_CAP), jax.random.fold_in(splits[11], 1), 0, NODE_CAP - 1).astype(jnp.int32)
    cell_area = draw_cell_area(jax.random.fold_in(splits[38], 71), 0)
    step_weights = jax.random.randint(splits[13], (STEPS,), 1, 5).astype(jnp.int32)
    encoder_weight = normal_values(splits[14], (VARS, D), VARS ** -0.5, 0.375, ((1, 4),), jnp.float32)
    encoder_moment = normal_values(splits[15], (VARS, D), (0.0022 / (2*VARS*D + EF*D + 5*LAYERS*D*D + 2*D*D + (3+2*LAYERS)*D*D + (9+6*LAYERS)*D) ** 0.5), 4.76837158203125e-06, ((1, 4),), jnp.float32)
    encoder_square = jnp.clip(jnp.exp(math.log(1.1891172074784961e-11) - 1.3862944 * jax.random.uniform(splits[16], (VARS, D), jnp.float32) ** levels(splits[16], (VARS, D), ((1, 4),), -0.2, 0.2)), 2.9727930186962404e-12, 1.1891172074784961e-11)
    embedder_weight = normal_values(splits[17], (EF, D), EF ** -0.5, 3.0, ((1, 4),), jnp.float32)
    embedder_moment = normal_values(splits[18], (EF, D), (0.0022 / (2*VARS*D + EF*D + 5*LAYERS*D*D + 2*D*D + (3+2*LAYERS)*D*D + (9+6*LAYERS)*D) ** 0.5), 4.76837158203125e-06, ((1, 4),), jnp.float32)
    embedder_square = jnp.clip(jnp.exp(math.log(1.1891172074784961e-11) - 1.3862944 * jax.random.uniform(splits[19], (EF, D), jnp.float32) ** levels(splits[19], (EF, D), ((1, 4),), -0.2, 0.2)), 2.9727930186962404e-12, 1.1891172074784961e-11)
    edge_weight = normal_values(splits[20], (LAYERS, 3 * D, D), (3 * D) ** -0.5, 0.15625, ((2, 4),), jnp.float32)
    edge_moment = normal_values(splits[21], (LAYERS, 3 * D, D), (0.0022 / (2*VARS*D + EF*D + 5*LAYERS*D*D + 2*D*D + (3+2*LAYERS)*D*D + (9+6*LAYERS)*D) ** 0.5), 4.76837158203125e-06, ((2, 4),), jnp.float32)
    edge_square = jnp.clip(jnp.exp(math.log(1.1891172074784961e-11) - 1.3862944 * jax.random.uniform(splits[22], (LAYERS, 3 * D, D), jnp.float32) ** levels(splits[22], (LAYERS, 3 * D, D), ((2, 4),), -0.2, 0.2)), 2.9727930186962404e-12, 1.1891172074784961e-11)
    node_weight = normal_values(splits[23], (LAYERS, 2 * D, D), (2 * D) ** -0.5, 0.1875, ((2, 4),), jnp.float32)
    node_moment = normal_values(splits[24], (LAYERS, 2 * D, D), (0.0022 / (2*VARS*D + EF*D + 5*LAYERS*D*D + 2*D*D + (3+2*LAYERS)*D*D + (9+6*LAYERS)*D) ** 0.5), 4.76837158203125e-06, ((2, 4),), jnp.float32)
    node_square = jnp.clip(jnp.exp(math.log(1.1891172074784961e-11) - 1.3862944 * jax.random.uniform(splits[25], (LAYERS, 2 * D, D), jnp.float32) ** levels(splits[25], (LAYERS, 2 * D, D), ((2, 4),), -0.2, 0.2)), 2.9727930186962404e-12, 1.1891172074784961e-11)
    decoder_weight = normal_values(splits[26], (2 * D, D), (2 * D) ** -0.5, 0.1875, ((1, 4),), jnp.float32)
    decoder_moment = normal_values(splits[27], (2 * D, D), (0.0022 / (2*VARS*D + EF*D + 5*LAYERS*D*D + 2*D*D + (3+2*LAYERS)*D*D + (9+6*LAYERS)*D) ** 0.5), 4.76837158203125e-06, ((1, 4),), jnp.float32)
    decoder_square = jnp.clip(jnp.exp(math.log(1.1891172074784961e-11) - 1.3862944 * jax.random.uniform(splits[28], (2 * D, D), jnp.float32) ** levels(splits[28], (2 * D, D), ((1, 4),), -0.2, 0.2)), 2.9727930186962404e-12, 1.1891172074784961e-11)
    inner_weight = normal_values(splits[29], (3 + 2 * LAYERS, D, D), D ** -0.5, 0.25, ((2, 4),), jnp.float32)
    inner_moment = normal_values(splits[30], (3 + 2 * LAYERS, D, D), (0.0022 / (2*VARS*D + EF*D + 5*LAYERS*D*D + 2*D*D + (3+2*LAYERS)*D*D + (9+6*LAYERS)*D) ** 0.5), 4.76837158203125e-06, ((2, 4),), jnp.float32)
    inner_square = jnp.clip(jnp.exp(math.log(1.1891172074784961e-11) - 1.3862944 * jax.random.uniform(splits[31], (3 + 2 * LAYERS, D, D), jnp.float32) ** levels(splits[31], (3 + 2 * LAYERS, D, D), ((2, 4),), -0.2, 0.2)), 2.9727930186962404e-12, 1.1891172074784961e-11)
    vector_weight = draw_vector_weight(jax.random.fold_in(splits[38], 71), 0)
    vector_moment = normal_values(splits[33], (9 + 6 * LAYERS, D), (0.011 / (2*VARS*D + EF*D + 5*LAYERS*D*D + 2*D*D + (3+2*LAYERS)*D*D + (9+6*LAYERS)*D) ** 0.5), 2.6702880859375e-05, ((1, 4),), jnp.float32)
    vector_square = jnp.clip(jnp.exp(math.log(2.972793122779649e-10) - 1.3862944 * jax.random.uniform(splits[34], (9 + 6 * LAYERS, D), jnp.float32) ** levels(splits[34], (9 + 6 * LAYERS, D), ((1, 4),), -0.2, 0.2)), 7.431982806949122e-11, 2.972793122779649e-10)
    head_weight = normal_values(splits[35], (VARS, D), D ** -0.5, 0.25, ((1, 4),), jnp.float32)
    head_moment = normal_values(splits[36], (VARS, D), (0.0022 / (2*VARS*D + EF*D + 5*LAYERS*D*D + 2*D*D + (3+2*LAYERS)*D*D + (9+6*LAYERS)*D) ** 0.5), 4.76837158203125e-06, ((1, 4),), jnp.float32)
    head_square = jnp.clip(jnp.exp(math.log(1.1891172074784961e-11) - 1.3862944 * jax.random.uniform(splits[37], (VARS, D), jnp.float32) ** levels(splits[37], (VARS, D), ((1, 4),), -0.2, 0.2)), 2.9727930186962404e-12, 1.1891172074784961e-11)
    return {"initial_state": initial_state, "target_states": target_states, "var_means": var_means, "var_scales": var_scales, "delta_scales": delta_scales, "edge_geometry": edge_geometry, "node_counts": node_counts, "edge_counts": edge_counts, "receivers": receivers, "senders": senders, "send_lists": send_lists, "grid_nodes": grid_nodes, "cell_area": cell_area, "step_weights": step_weights, "encoder_weight": encoder_weight, "encoder_moment": encoder_moment, "encoder_square": encoder_square, "embedder_weight": embedder_weight, "embedder_moment": embedder_moment, "embedder_square": embedder_square, "edge_weight": edge_weight, "edge_moment": edge_moment, "edge_square": edge_square, "node_weight": node_weight, "node_moment": node_moment, "node_square": node_square, "decoder_weight": decoder_weight, "decoder_moment": decoder_moment, "decoder_square": decoder_square, "inner_weight": inner_weight, "inner_moment": inner_moment, "inner_square": inner_square, "vector_weight": vector_weight, "vector_moment": vector_moment, "vector_square": vector_square, "head_weight": head_weight, "head_moment": head_moment, "head_square": head_square}


@jax.custom_vjp
def low(v):
    return lax.optimization_barrier(v.astype(jnp.bfloat16)).astype(jnp.float32)

@jax.custom_vjp
def low_back(v):
    return v

def low_keep(v):
    return (low(v), None)

def low_pass(kept, grad):
    return (grad,)

def back_keep(v):
    return (v, None)

def back_low(kept, grad):
    return (low(grad),)
low.defvjp(low_keep, low_pass)
low_back.defvjp(back_keep, back_low)
norm_eps = 1e-05
beta_first = 0.9
beta_second = 0.95
adam_eps = 1e-08
decay_weight = 0.1
learn_rate = 0.05
clip_limit = 0.02

def matmul(left, right):
    return jnp.matmul(left, right, precision=lax.Precision.HIGHEST)

def layer_norm(values, gain, shift):
    centred = values - lax.optimization_barrier(jnp.mean(values, axis=-1, keepdims=True))
    spread = lax.optimization_barrier(jnp.mean(centred * centred, axis=-1, keepdims=True))
    return centred * lax.rsqrt(spread + norm_eps) * gain + shift

def block(inputs, first, second, vectors, index):
    hidden = low_back(matmul(inputs, first) + vectors[3 * index])
    mixed = low_back(matmul(low(jax.nn.silu(hidden)), second[index]))
    return layer_norm(mixed, vectors[3 * index + 1], vectors[3 * index + 2])

def take_rows(table, index):
    return jax.vmap(lambda rows, where: jnp.take(rows, where, axis=0))(table, index)

def gather_sum(values, index):
    return jax.vmap(lambda rows, where: jax.ops.segment_sum(rows, where, NODE_CAP))(values, index)

def halo_rows(rounded, picks):
    regions = picks.shape[0]
    taken = rounded[jnp.arange(regions)[:, None, None], picks]
    return jnp.swapaxes(taken, 0, 1).reshape(regions, -1, rounded.shape[-1])

def one_step(state, edges0, weights, graph, norms):
    w_enc, w_embed, w_edge, w_node, w_dec, w_second, vectors, w_head = weights
    means, scales, resid = norms
    recv, send_from, edge_live, picks, assign = graph
    grid_lat = block(low((state - means) / scales), w_enc, w_second, vectors, 0)
    grid_low = low(grid_lat)
    nodes = gather_sum(grid_low, assign)
    edges = edges0
    for layer in range(LAYERS):
        node_low = low(nodes)
        table = jnp.concatenate([node_low, halo_rows(node_low, picks)], 1)
        joined = jnp.concatenate([low(edges), take_rows(table, send_from), take_rows(node_low, recv)], -1)
        edges = edges + block(joined, w_edge[layer], w_second, vectors, 2 + layer)
        total = gather_sum(edges * edge_live[..., None], recv)
        node_in = jnp.concatenate([node_low, low(total)], -1)
        nodes = nodes + block(node_in, w_node[layer], w_second, vectors, 2 + LAYERS + layer)
    node_low = low(nodes)
    dec_in = jnp.concatenate([grid_low, take_rows(node_low, assign)], -1)
    decoded = block(dec_in, w_dec, w_second, vectors, 2 + 2 * LAYERS)
    update = low_back(matmul(low(grid_lat + decoded), w_head.T))
    return state + resid * update

def objective(weights, inputs, targets, geometry, graph, norms, area, plan):
    rounded = tuple((low(w) for w in weights))
    total = jnp.zeros((), jnp.float32)
    for sample in range(inputs.shape[0]):
        edges0 = block(low(geometry), rounded[1], rounded[5], rounded[6], 1)
        state = inputs[sample]
        for step in range(STEPS):
            state = one_step(state, edges0, rounded, graph, norms)
            miss = (state - targets[sample, step]) / norms[2]
            total = total + plan[step] * jnp.sum(area[..., None] * miss * miss)
    return total

def adam(master, moment, square, grad):
    first = beta_first * moment + (1 - beta_first) * grad
    second = beta_second * square + (1 - beta_second) * grad * grad
    ratio = first / (1 - beta_first ** STEP_COUNT) / (jnp.sqrt(second / (1 - beta_second ** STEP_COUNT)) + adam_eps)
    return (first, second, master - learn_rate * (ratio + decay_weight * master))

def shard_rows(weight):
    split = weight.reshape(weight.shape[:-1] + (N_REP, weight.shape[-1] // N_REP))
    return jnp.moveaxis(split, -2, 0).reshape(N_REP, -1)

def reference(initial_state, target_states, var_means, var_scales, delta_scales, edge_geometry, node_counts, edge_counts, receivers, senders, send_lists, grid_nodes, cell_area, step_weights, encoder_weight, encoder_moment, encoder_square, embedder_weight, embedder_moment, embedder_square, edge_weight, edge_moment, edge_square, node_weight, node_moment, node_square, decoder_weight, decoder_moment, decoder_square, inner_weight, inner_moment, inner_square, vector_weight, vector_moment, vector_square, head_weight, head_moment, head_square):
    regions = node_counts.shape[0]
    counts = node_counts[:, None]
    recv = receivers.reshape(regions, -1)
    raw = senders.reshape(regions, -1)
    send_from = jnp.where(raw < NODE_CAP, raw % counts, raw)
    edge_live = (jnp.arange(recv.shape[1])[None, :] < edge_counts[:, None]).astype(jnp.float32)
    picks = send_lists % node_counts[:, None, None]
    assign = grid_nodes.reshape(regions, -1) % counts
    graph = (recv, send_from, edge_live, picks, assign)
    norms = (var_means, var_scales, delta_scales)
    inputs = initial_state.reshape(initial_state.shape[0], regions, -1, initial_state.shape[-1])
    targets = target_states.reshape(target_states.shape[0], target_states.shape[1], regions, -1, target_states.shape[-1])
    geometry = edge_geometry.reshape(regions, -1, edge_geometry.shape[-1])
    area = cell_area.reshape(regions, -1)
    plan = step_weights.astype(jnp.float32)
    masters = (encoder_weight, embedder_weight, edge_weight, node_weight, decoder_weight, inner_weight, vector_weight, head_weight)
    moments = (encoder_moment, embedder_moment, edge_moment, node_moment, decoder_moment, inner_moment, vector_moment, head_moment)
    squares = (encoder_square, embedder_square, edge_square, node_square, decoder_square, inner_square, vector_square, head_square)
    loss_total, pullback = jax.vjp(lambda *w: objective(w, inputs, targets, geometry, graph, norms, area, plan), *masters)
    weight_total = jnp.sum(plan) * jnp.sum(area) * inputs.shape[0] * inputs.shape[-1]
    grads = pullback(1.0 / weight_total)
    gradient_norm = jnp.sqrt(sum((jnp.sum(g * g) for g in grads)))
    factor = jnp.minimum(1.0, clip_limit / gradient_norm)
    new = [adam(masters[i], moments[i], squares[i], grads[i] * factor) for i in range(8)]
    weight_copies = jnp.concatenate([shard_rows(n[2]) for n in new], 1).astype(jnp.bfloat16)
    return (loss_total, weight_total, gradient_norm, new[0][0], new[0][1], new[0][2], new[1][0], new[1][1], new[1][2], new[2][0], new[2][1], new[2][2], new[3][0], new[3][1], new[3][2], new[4][0], new[4][1], new[4][2], new[5][0], new[5][1], new[5][2], new[6][0], new[6][1], new[6][2], new[7][0], new[7][1], new[7][2], weight_copies)
```

```python
import jax
import jax.numpy as jnp
from jax import lax
from jax.experimental import pallas as pl
from jax.experimental.pallas import tpu as pltpu
from jax.sharding import PartitionSpec as P

LAYERS = 3
STEPS = 2
STEP_COUNT = 10
NODE_CAP = 512
D = 512
BLOCK = 128
BLOCKS = D // BLOCK
TILE = 512
CODED = 32
CODE_TOP = 32000.0

norm_eps = 1e-05
beta_first = 0.9
beta_second = 0.95
adam_eps = 1e-08
decay_weight = 0.1
learn_rate = 0.05
clip_limit = 0.02

N_ACT = "act"
N_AREA = "area"
N_ASSIGN = "assign"
N_BEFORE = "before"
N_D_EDGES = "d_edges"
N_D_FIRST = "d_first"
N_D_GRID = "d_grid"
N_D_HALO = "d_halo"
N_D_HIDDEN = "d_hidden"
N_D_MIXED = "d_mixed"
N_D_NEXT = "d_next"
N_D_NODES = "d_nodes"
N_D_SECOND = "d_second"
N_D_STATE = "d_state"
N_DEC = "dec"
N_DELTA = "delta"
N_EDGE_FIRST = "edge_first"
N_EDGE_INNER = "edge_inner"
N_EDGES = "edges"
N_EDGES_LOW = "edges_low"
N_EMBED_GRADS = "embed_grads"
N_ENC = "enc"
N_FEATS = "feats"
N_FINAL = "final"
N_FIRST = "first"
N_FROM_RECV = "from_recv"
N_FROM_SEND = "from_send"
N_GEOMETRY = "geometry"
N_GRADS = "grads"
N_H = "h"
N_HALO = "halo"
N_HALO_HIGH = "halo_high"
N_HALO_REST = "halo_rest"
N_HEAD = "head"
N_HIDDEN = "hidden"
N_INNER = "inner"
N_INVERSE = "inverse"
N_LATENT = "latent"
N_LOCAL = "local"
N_LOW = "low"
N_MISS = "miss"
N_NODE_ACT = "node_act"
N_NODE_D_HIDDEN = "node_d_hidden"
N_NODE_D_MIXED = "node_d_mixed"
N_NODE_FIRST = "node_first"
N_NODE_HIDDEN = "node_hidden"
N_NODE_INNER = "node_inner"
N_NODE_INVERSE = "node_inverse"
N_NODE_LOW = "node_low"
N_NODE_NORMED = "node_normed"
N_NODES = "nodes"
N_NORMED = "normed"
N_OUTGOING = "outgoing"
N_PICKS = "picks"
N_PICKS_ROW = "picks_row"
N_PLAN = "plan"
N_RECV = "recv"
N_RECV_ROW = "recv_row"
N_REGION = "region"
N_REP = "rep"
N_RETURNED = "returned"
N_S = "s"
N_SCALES = "scales"
N_SEND = "send"
N_SEND_ROW = "send_row"
N_STATE = "state"
N_SUMS = "sums"
N_SUMS_ = "sums_"
N_TARGET = "target"
N_TOTAL = "total"
N_V = "v"
N_VECTORS = "vectors"
N_W = "w"

f32 = jnp.float32
bf16 = jnp.bfloat16


def up_to(rows, unit):
    return (rows + unit - 1) // unit * unit


class Env:
    pass


def cost_of(micros):
    return pl.CostEstimate(flops=int(micros * 1.15e9), bytes_accessed=0, transcendentals=0)


def launch(body, ins, outs, scratch=(), micros=0, swap=None, after=()):
    in_specs, operands, scratch_shapes, names = [], [], [], []
    loads = {}
    total_sems = 0
    for item in ins:
        name, array, kind = item[:3]
        operands.append(array)
        if kind == N_V:
            in_specs.append(pl.BlockSpec(memory_space=pltpu.VMEM))
        elif kind == N_S:
            in_specs.append(pl.BlockSpec(memory_space=pltpu.SMEM))
        elif kind == N_H:
            index, parts = item[3]
            in_specs.append(pl.BlockSpec(memory_space=pl.ANY))
            shape = array.shape[len(index) :]
            loads[name] = (N_H, index, parts, shape, total_sems)
            total_sems += parts
            names.append(name)
            scratch_shapes.append(pltpu.VMEM(shape, array.dtype))
        else:
            first, rows = item[3]
            in_specs.append(pl.BlockSpec(memory_space=pl.ANY))
            loads[name] = (N_W, first, rows, None, total_sems)
            total_sems += BLOCKS
            names.append(name)
            scratch_shapes.append(pltpu.VMEM((rows, D), array.dtype))
    out_specs, out_shape = [], []
    flushes = {}
    out_sems = 0
    for name, shape, dtype, kind, parts in outs:
        out_shape.append(jax.ShapeDtypeStruct(shape, dtype))
        if kind == N_V:
            out_specs.append(pl.BlockSpec(memory_space=pltpu.VMEM))
        elif kind == N_S:
            out_specs.append(pl.BlockSpec(memory_space=pltpu.SMEM))
        else:
            out_specs.append(pl.BlockSpec(memory_space=pl.ANY))
            flushes[name] = (parts, shape, out_sems)
            out_sems += parts
            if name not in names:
                names.append(name)
                scratch_shapes.append(pltpu.VMEM(shape, dtype))
    if swap is not None:
        for _ in range(BLOCKS):
            out_shape.append(jax.ShapeDtypeStruct((swap[1], BLOCK), f32))
            out_specs.append(pl.BlockSpec(memory_space=pl.ANY))
        operands.append(swap[0])
        in_specs.append(pl.BlockSpec(memory_space=pltpu.SMEM))
    for array in after:
        operands.append(array)
        in_specs.append(pl.BlockSpec(memory_space=pl.ANY))
    for name, shape, dtype in scratch:
        names.append(name)
        scratch_shapes.append(pltpu.VMEM(shape, dtype))
    scratch_shapes.append(pltpu.SemaphoreType.DMA((max(total_sems, 1),)))
    scratch_shapes.append(pltpu.SemaphoreType.DMA((max(out_sems, 1),)))
    if swap is not None:
        scratch_shapes.append(pltpu.SemaphoreType.DMA((BLOCKS,)))

    def kernel(*refs):
        k = Env()
        in_refs = refs[: len(ins)]
        out_refs = refs[len(operands) : len(operands) + len(out_shape)]
        rest = refs[len(operands) + len(out_shape) :]
        for name, ref in zip(names, rest):
            setattr(k, name, ref)
        sem_in, sem_out = rest[len(names) : len(names) + 2]
        sources, targets = {}, {}
        for item, ref in zip(ins, in_refs):
            if item[2] in (N_V, N_S):
                setattr(k, item[0], ref)
            else:
                sources[item[0]] = ref
        for item, ref in zip(outs, out_refs):
            if item[3] in (N_V, N_S):
                setattr(k, item[0], ref)
            else:
                targets[item[0]] = ref

        def load(name, part):
            kind, first, parts, shape, base = loads[name]
            src, dst = sources[name], getattr(k, name)
            if kind == N_H:
                for i in first:
                    src = src.at[i]
                if parts > 1:
                    step = shape[0] // parts
                    rows = pl.ds(pl.multiple_of(part * step, step), step)
                    src, dst = src.at[rows], dst.at[rows]
            else:
                src = src.at[part, pl.ds(first, parts)]
                dst = dst.at[:, pl.ds(part * BLOCK, BLOCK)]
            return pltpu.make_async_copy(src, dst, sem_in.at[base + part])

        def send(name, part):
            parts, shape, base = flushes[name]
            src, dst = getattr(k, name), targets[name]
            if parts > 1:
                step = shape[0] // parts
                rows = pl.ds(pl.multiple_of(part * step, step), step)
                src, dst = src.at[rows], dst.at[rows]
            return pltpu.make_async_copy(src, dst, sem_out.at[base + part])

        def wait(name, part=None):
            if name not in loads:
                return
            if part is not None:
                load(name, part).wait()
                return
            count = BLOCKS if loads[name][0] == N_W else loads[name][2]
            for i in range(count):
                load(name, i).wait()

        def flush(name, part=None):
            if part is not None:
                send(name, part).start()
                return
            for i in range(flushes[name][0]):
                send(name, i).start()

        def swap_copy(other):
            place = refs[len(ins)]
            source = k.grads.at[lax.bitwise_xor(place[0], other)]
            return pltpu.make_async_copy(source, out_refs[len(outs) + other], rest[-1].at[other])

        def flush_swap():
            for other in range(BLOCKS):
                swap_copy(other).start()

        k.wait, k.flush, k.flush_swap = wait, flush, flush_swap
        for item in ins:
            if item[0] in loads:
                count = BLOCKS if item[2] == N_W else loads[item[0]][2]
                for i in range(count):
                    load(item[0], i).start()
        body(k)
        for name in flushes:
            for i in range(flushes[name][0]):
                send(name, i).wait()
        if swap is not None:
            for other in range(BLOCKS):
                swap_copy(other).wait()

    return pl.pallas_call(
        kernel,
        out_shape=out_shape,
        in_specs=in_specs,
        out_specs=out_specs,
        scratch_shapes=scratch_shapes,
        compiler_params=pltpu.CompilerParams(
            vmem_limit_bytes=56 * 2**20
        ),
        cost_estimate=cost_of(micros),
    )(*operands)


def dense(left, right):
    return jnp.dot(left, right, preferred_element_type=f32)


def dense_left(left, right):
    return lax.dot_general(left, right, (((0,), (0,)), ((), ())), preferred_element_type=f32)


def dense_right(left, right):
    return lax.dot_general(left, right, (((1,), (1,)), ((), ())), preferred_element_type=f32)


def halves(value):
    high = value.astype(bf16)
    return high, (value - high.astype(f32)).astype(bf16)


def rows_hot(column, width):
    spots = lax.broadcasted_iota(jnp.int32, (column.shape[0], width), 1)
    return jnp.where(column == spots, 1.0, 0.0).astype(bf16)


def cols_hot(row, height, first=0):
    spots = lax.broadcasted_iota(jnp.int32, (height, row.shape[1]), 0) + first
    return jnp.where(row == spots, 1.0, 0.0).astype(bf16)


def sigmoid(value):
    return 0.5 * jnp.tanh(0.5 * value) + 0.5


def normalise(mixed):
    centred = mixed - jnp.mean(mixed, -1, keepdims=True)
    inverse = lax.rsqrt(jnp.mean(centred * centred, -1, keepdims=True) + norm_eps)
    return centred * inverse, inverse


def vec(k, block, row):
    at = 3 * block + row
    return k.vectors[at : at + 1, :]


def row_tile(t, size):
    return pl.ds(pl.multiple_of(t * size, size), size)


def loop(count, step, most=1):
    unroll = max(n for n in range(1, most + 1) if count % n == 0)
    lax.fori_loop(0, count, lambda t, carry: (step(t), carry)[1], 0, unroll=unroll)


def forward_rows(k, block, hidden, inner):
    act = (hidden * sigmoid(hidden)).astype(bf16)
    normed, inverse = normalise(dense(act, inner))
    return normed * vec(k, block, 1) + vec(k, block, 2), normed, inverse


def backward_rows(k, block, upstream, hidden, normed, inverse, inner, sums, at):
    sums[at + 1 : at + 2, :] += jnp.sum(upstream * normed, 0, keepdims=True)
    sums[at + 2 : at + 3, :] += jnp.sum(upstream, 0, keepdims=True)
    scaled = upstream * vec(k, block, 1)
    d_mixed = inverse * (
        scaled
        - jnp.mean(scaled, -1, keepdims=True)
        - normed * jnp.mean(scaled * normed, -1, keepdims=True)
    )
    d_mixed = d_mixed.astype(bf16)
    sigma = sigmoid(hidden)
    act = (hidden * sigma).astype(bf16)
    d_act = dense_right(d_mixed, inner)
    d_hidden = (d_act * (sigma * (1.0 + hidden * (1.0 - sigma)))).astype(bf16)
    sums[at : at + 1, :] += jnp.sum(d_hidden.astype(f32), 0, keepdims=True)
    return act, d_mixed, d_hidden


def add_grad(k, first, value):
    rows = value.shape[0]
    for c in range(BLOCKS):
        k.grads[c, first : first + rows, :] += value[:, c * BLOCK : (c + 1) * BLOCK]


def set_grad(k, first, value):
    rows = value.shape[0]
    for c in range(BLOCKS):
        k.grads[c, first : first + rows, :] = value[:, c * BLOCK : (c + 1) * BLOCK]


def put_grad(k, fresh, first, value):
    (set_grad if fresh else add_grad)(k, first, value)


def weight_grad(k, fresh, first, left, right, pieces=2):
    width = left.shape[1]
    step = width // pieces
    for i in range(pieces):
        part = dense_left(left[:, i * step : (i + 1) * step], right[...])
        put_grad(k, fresh, first + i * step, part)


def start_sums(k, fresh):
    if fresh:
        k.sums[...] = jnp.zeros(k.sums.shape, f32)
    else:
        k.wait(N_SUMS)


def embed_forward(geometry, first, inner, at_inner, vectors):
    edges = geometry.shape[1]

    def body(k):
        k.wait(N_FIRST)
        k.wait(N_INNER)

        def tile(t):
            rows = row_tile(t, TILE)
            hidden = dense_left(k.geometry[:, rows], k.first[...]) + vec(k, 1, 0)
            k.hidden[rows] = hidden
            out, normed, inverse = forward_rows(k, 1, hidden, k.inner[...])
            k.normed[rows] = normed
            k.inverse[rows] = inverse
            k.edges[rows] = out
            k.edges_low[rows] = out.astype(bf16)
            for name in (N_HIDDEN, N_NORMED, N_INVERSE, N_EDGES, N_EDGES_LOW):
                k.flush(name, t)

        loop(edges // TILE, tile)

    parts = edges // TILE
    return launch(
        body,
        [
            (N_GEOMETRY, geometry, N_V),
            (N_VECTORS, vectors, N_V),
            (N_FIRST,) + first,
            (N_INNER,) + inner,
        ],
        [
            (N_EDGES, (edges, D), f32, N_H, parts),
            (N_EDGES_LOW, (edges, D), bf16, N_H, parts),
            (N_HIDDEN, (edges, D), f32, N_H, parts),
            (N_NORMED, (edges, D), f32, N_H, parts),
            (N_INVERSE, (edges, 1), f32, N_H, parts),
        ],
        micros=5,
    )


def encoder_forward(state, means, scales, first, inner, vectors, assign, picks):
    depth, grid = state.shape
    out_rows = picks.shape[0]

    def body(k):
        k.wait(N_STATE)
        k.feats[...] = ((k.state[...] - k.means[...]) / k.scales[...]).astype(bf16)
        k.flush(N_FEATS)
        k.wait(N_FIRST)
        k.wait(N_INNER)

        def tile(t):
            rows = row_tile(t, TILE)
            hidden = dense_left(k.feats[:, rows], k.first[...]) + vec(k, 0, 0)
            k.hidden[rows] = hidden
            out, normed, inverse = forward_rows(k, 0, hidden, k.inner[...])
            k.normed[rows] = normed
            k.inverse[rows] = inverse
            k.latent[rows] = out
            k.low[rows] = out.astype(bf16)
            for name in (N_HIDDEN, N_NORMED, N_INVERSE, N_LATENT, N_LOW):
                k.flush(name, t)

        loop(grid // TILE, tile)
        nodes = dense(cols_hot(k.assign[...], NODE_CAP), k.low[...])
        k.nodes[...] = nodes
        k.node_low[...] = nodes.astype(bf16)
        k.outgoing[...] = dense(rows_hot(k.picks[...], NODE_CAP), k.node_low[...]).astype(bf16)

    parts = grid // TILE
    return launch(
        body,
        [
            (N_STATE, state, N_H, ((), 1)),
            ("means", means, N_V),
            (N_SCALES, scales, N_V),
            (N_ASSIGN, assign, N_V),
            (N_PICKS, picks, N_V),
            (N_VECTORS, vectors, N_V),
            (N_FIRST,) + first,
            (N_INNER,) + inner,
        ],
        [
            (N_NODES, (NODE_CAP, D), f32, N_V, 1),
            (N_NODE_LOW, (NODE_CAP, D), bf16, N_V, 1),
            (N_OUTGOING, (out_rows, D), bf16, N_V, 1),
            (N_LATENT, (grid, D), f32, N_H, parts),
            (N_LOW, (grid, D), bf16, N_H, parts),
            (N_FEATS, (depth, grid), bf16, N_H, 1),
            (N_HIDDEN, (grid, D), f32, N_H, parts),
            (N_NORMED, (grid, D), f32, N_H, parts),
            (N_INVERSE, (grid, 1), f32, N_H, parts),
        ],
        micros=5,
    )


def layer_local(layer, edges_low, node_low, edge_first, vectors, send, recv):
    count = edges_low.shape[0]
    at = 2 + layer

    def body(k):
        k.wait(N_EDGE_FIRST)

        def tile(t):
            rows = row_tile(t, TILE)
            sent = dense(rows_hot(k.send[rows], NODE_CAP), k.node_low[...]).astype(bf16)
            got = dense(rows_hot(k.recv[rows], NODE_CAP), k.node_low[...]).astype(bf16)
            k.wait(N_EDGES_LOW, t)
            joined = jnp.concatenate([k.edges_low[rows], sent, got], 1)
            k.local[rows] = dense(joined, k.edge_first[...]) + vec(k, at, 0)
            k.flush(N_LOCAL, t)

        loop(count // TILE, tile)

    parts = count // TILE
    return launch(
        body,
        [
            (N_NODE_LOW, node_low, N_V),
            (N_SEND, send, N_V),
            (N_RECV, recv, N_V),
            (N_VECTORS, vectors, N_V),
            (N_EDGE_FIRST,) + edge_first,
            (N_EDGES_LOW, edges_low, N_H, ((), parts)),
        ],
        [(N_LOCAL, (count, D), f32, N_H, parts)],
        micros=8,
    )[0]


def layer_forward(
    layer, local, edges, nodes, node_low, halo, weights, vectors, send, recv_row, picks, last
):
    count = edges.shape[0]
    halo_rows = halo.shape[0]
    from_send, edge_inner, node_first, node_inner = weights
    at_edge, at_node = 2 + layer, 2 + LAYERS + layer

    def body(k):
        k.wait(N_FROM_SEND)
        high, rest = halves(dense(k.halo[...], k.from_send[...]))
        k.table[:, 0:D] = high
        k.table[:, D : 2 * D] = rest
        k.wait(N_EDGE_INNER)

        def tile(t):
            rows = row_tile(t, TILE)
            both = dense(rows_hot(k.send[rows] - NODE_CAP, halo_rows), k.table[...])
            k.wait(N_HIDDEN, t)
            hidden = k.hidden[rows] + (both[:, 0:D] + both[:, D : 2 * D])
            k.hidden[rows] = hidden
            out, normed, inverse = forward_rows(k, at_edge, hidden, k.edge_inner[...])
            k.normed[rows] = normed
            k.inverse[rows] = inverse
            k.wait(N_EDGES, t)
            edge = k.edges[rows] + out
            k.edges[rows] = edge
            high, rest = halves(edge)
            k.edges_low[rows] = high
            k.rest[rows] = rest
            for name in (N_HIDDEN, N_NORMED, N_INVERSE):
                k.flush(name, t)
            if not last:
                k.flush(N_EDGES, t)
                k.flush(N_EDGES_LOW, t)

        loop(count // TILE, tile)
        k.wait(N_NODE_FIRST)
        k.wait(N_NODE_INNER)
        k.wait(N_NODES)

        def node_tile(t):
            rows = row_tile(t, TILE)
            hot = cols_hot(k.recv_row[...], TILE, t * TILE)
            total = (dense(hot, k.edges_low[...]) + dense(hot, k.rest[...])).astype(bf16)
            k.total[rows] = total
            node_in = jnp.concatenate([k.node_low[rows], total], 1)
            hidden = dense(node_in, k.node_first[...]) + vec(k, at_node, 0)
            k.node_hidden[rows] = hidden
            out, normed, inverse = forward_rows(k, at_node, hidden, k.node_inner[...])
            k.node_normed[rows] = normed
            k.node_inverse[rows] = inverse
            node = k.nodes[rows] + out
            k.nodes[rows] = node
            k.new_low[rows] = node.astype(bf16)
            for name in (N_TOTAL, N_NODE_HIDDEN, N_NODE_NORMED, N_NODE_INVERSE):
                k.flush(name, t)
            if not last:
                k.flush(N_NODES, t)

        loop(NODE_CAP // TILE, node_tile)
        if not last:
            k.outgoing[...] = dense(rows_hot(k.picks[...], NODE_CAP), k.new_low[...]).astype(bf16)

    parts = count // TILE
    node_parts = NODE_CAP // TILE
    ins = [
        (N_NODE_LOW, node_low, N_V),
        (N_HALO, halo, N_V),
        (N_SEND, send, N_V),
        (N_RECV_ROW, recv_row, N_V),
        (N_VECTORS, vectors, N_V),
        (N_FROM_SEND,) + from_send,
        (N_EDGE_INNER,) + edge_inner,
        (N_HIDDEN, local, N_H, ((), parts)),
        (N_EDGES, edges, N_H, ((), parts)),
        (N_NODE_FIRST,) + node_first,
        (N_NODE_INNER,) + node_inner,
        (N_NODES, nodes, N_H, ((), 1)),
    ]
    outs = [
        ("new_low", (NODE_CAP, D), bf16, N_V, 1),
        (N_HIDDEN, (count, D), f32, N_H, parts),
        (N_NORMED, (count, D), f32, N_H, parts),
        (N_INVERSE, (count, 1), f32, N_H, parts),
        (N_TOTAL, (NODE_CAP, D), bf16, N_H, node_parts),
        (N_NODE_HIDDEN, (NODE_CAP, D), f32, N_H, node_parts),
        (N_NODE_NORMED, (NODE_CAP, D), f32, N_H, node_parts),
        (N_NODE_INVERSE, (NODE_CAP, 1), f32, N_H, node_parts),
    ]
    scratch = [("table", (halo_rows, 2 * D), bf16), ("rest", (count, D), bf16)]
    if last:
        scratch.append((N_EDGES_LOW, (count, D), bf16))
    else:
        ins.append((N_PICKS, picks, N_V))
        outs += [
            (N_EDGES, (count, D), f32, N_H, parts),
            (N_NODES, (NODE_CAP, D), f32, N_H, node_parts),
            (N_OUTGOING, (halo_rows, D), bf16, N_V, 1),
            (N_EDGES_LOW, (count, D), bf16, N_H, parts),
        ]
    out = launch(body, ins, outs, scratch, micros=13)
    kept = {
        N_NODE_LOW: node_low,
        N_HALO: halo,
        N_HIDDEN: out[1],
        N_NORMED: out[2],
        N_INVERSE: out[3],
        N_TOTAL: out[4],
        N_NODE_HIDDEN: out[5],
        N_NODE_NORMED: out[6],
        N_NODE_INVERSE: out[7],
    }
    if last:
        return None, None, None, out[0], None, kept
    return out[8], out[11], out[9], out[0], out[10], kept


def decoder_forward(
    step, state, target, latent, low, node_low, weights, vectors, assign, delta, area, plan
):
    depth, grid = state.shape
    first, inner, head = weights
    at = 2 + 2 * LAYERS

    def body(k):
        k.wait(N_FIRST)
        k.wait(N_INNER)

        def tile(t):
            rows = row_tile(t, TILE)
            k.wait(N_LOW, t)
            got = dense(rows_hot(k.assign[rows], NODE_CAP), k.node_low[...]).astype(bf16)
            joined = jnp.concatenate([k.low[rows], got], 1)
            hidden = dense(joined, k.first[...]) + vec(k, at, 0)
            k.hidden[rows] = hidden
            out, normed, inverse = forward_rows(k, at, hidden, k.inner[...])
            k.normed[rows] = normed
            k.inverse[rows] = inverse
            k.wait(N_LATENT, t)
            k.final[rows] = (k.latent[rows] + out).astype(bf16)
            for name in (N_HIDDEN, N_NORMED, N_INVERSE, N_FINAL):
                k.flush(name, t)

        loop(grid // TILE, tile)
        k.wait(N_HEAD)
        k.wait(N_STATE)
        k.wait(N_TARGET)
        update = dense_right(k.head[...], k.final[...])
        new_state = k.state[...] + k.delta[...] * update
        k.new_state[...] = new_state
        miss = (new_state - k.target[...]) / k.delta[...]
        k.miss[...] = miss
        weight = k.plan[step].astype(f32)
        k.loss[...] = weight * jnp.sum(k.area[...] * miss * miss, keepdims=True)

    parts = grid // TILE
    out = launch(
        body,
        [
            (N_NODE_LOW, node_low, N_V),
            (N_ASSIGN, assign, N_V),
            (N_VECTORS, vectors, N_V),
            (N_DELTA, delta, N_V),
            (N_AREA, area, N_V),
            (N_PLAN, plan, N_S),
            (N_FIRST,) + first,
            (N_LOW, low, N_H, ((), parts)),
            (N_INNER,) + inner,
            (N_LATENT, latent, N_H, ((), parts)),
            (N_HEAD,) + head,
            (N_STATE, state, N_H, ((), 1)),
            (N_TARGET, target, N_H, ((step,), 1)),
        ],
        [
            ("new_state", (depth, grid), f32, N_V, 1),
            (N_MISS, (depth, grid), f32, N_V, 1),
            ("loss", (1, 1), f32, N_V, 1),
            (N_HIDDEN, (grid, D), f32, N_H, parts),
            (N_NORMED, (grid, D), f32, N_H, parts),
            (N_INVERSE, (grid, 1), f32, N_H, parts),
            (N_FINAL, (grid, D), bf16, N_H, parts),
        ],
        micros=7,
    )
    kept = {
        N_MISS: out[1],
        N_HIDDEN: out[3],
        N_NORMED: out[4],
        N_INVERSE: out[5],
        N_FINAL: out[6],
        N_LOW: low,
        N_NODE_LOW: node_low,
    }
    return out[0], out[2], kept


def grads_io(outs, scratch, grads, rows, swap):
    shape = (BLOCKS, rows, BLOCK)
    if swap is None:
        outs.append((N_GRADS, shape, f32, N_H, BLOCKS))
    elif grads is None:
        scratch.append((N_GRADS, shape, f32))


def flush_grads(k, swap):
    if swap is None:
        k.flush(N_GRADS)
    else:
        k.flush_swap()


def decoder_backward(
    step, regions, d_state, kept, weights, vectors, assign_row, delta, area, plan, inverse_total, grads, sums,
    swap,
):
    miss = kept[N_MISS]
    depth, grid = miss.shape
    first, inner, head = weights
    at = 2 + 2 * LAYERS
    fresh = grads is None
    more = d_state is not None
    keep_state = step > 0
    rows_all = up_to(3 * D + depth, CODED * regions)

    def body(k):
        k.wait(N_MISS)
        coefficient = 2.0 * k.inverse_total[0, 0] * k.plan[step].astype(f32)
        d_next = coefficient * k.area[...] * k.miss[...] / k.delta[...]
        if more:
            k.wait(N_D_STATE)
            d_next = k.d_state[...] + d_next
        if keep_state:
            k.d_next[...] = d_next
            k.flush(N_D_NEXT)
        k.d_update[...] = (d_next * k.delta[...]).astype(bf16)
        start_sums(k, fresh)
        k.wait(N_HEAD)
        k.wait(N_INNER)
        k.wait(N_FIRST)

        def tile(t):
            rows = row_tile(t, TILE)
            for name in (N_HIDDEN, N_NORMED, N_INVERSE):
                k.wait(name, t)
            d_final = dense_left(k.d_update[:, rows], k.head[...])
            act, d_mixed, d_hidden = backward_rows(
                k, at, d_final, k.hidden[rows], k.normed[rows], k.inverse[rows],
                k.inner[...], k.sums, 0,
            )
            k.act[rows] = act
            k.d_mixed[rows] = d_mixed
            k.d_hidden[rows] = d_hidden
            k.d_grid[rows] = d_final + dense_right(d_hidden, k.first[0:D])
            k.flush(N_D_GRID, t)

        loop(grid // TILE, tile)
        k.flush(N_SUMS)
        gathered = dense(cols_hot(k.assign_row[...], NODE_CAP), k.d_hidden[...])
        high, rest = halves(gathered)
        k.d_nodes[...] = dense_right(high, k.first[D : 2 * D]) + dense_right(rest, k.first[D : 2 * D])
        if not fresh:
            k.wait(N_GRADS)
        k.wait(N_LOW)
        k.wait(N_FINAL)
        weight_grad(k, fresh, 0, k.low, k.d_hidden)
        put_grad(k, fresh, D, dense_left(k.node_low[...], high) + dense_left(k.node_low[...], rest))
        weight_grad(k, fresh, 2 * D, k.act, k.d_mixed)
        put_grad(k, fresh, 3 * D, dense(k.d_update[...], k.final[...]))
        if fresh and rows_all > 3 * D + depth:
            k.grads[:, 3 * D + depth :, :] = jnp.zeros(
                (BLOCKS, rows_all - 3 * D - depth, BLOCK), f32
            )
        flush_grads(k, swap)

    parts = grid // TILE
    ins = [
        (N_MISS, miss, N_H, ((), 1)),
        (N_AREA, area, N_V),
        (N_DELTA, delta, N_V),
        ("assign_row", assign_row, N_V),
        (N_VECTORS, vectors, N_V),
        (N_NODE_LOW, kept[N_NODE_LOW], N_V),
        (N_PLAN, plan, N_S),
        ("inverse_total", inverse_total, N_S),
    ]
    if more:
        ins.append((N_D_STATE, d_state, N_H, ((), 1)))
    ins += [
        (N_HEAD,) + head,
        (N_HIDDEN, kept[N_HIDDEN], N_H, ((), parts)),
        (N_NORMED, kept[N_NORMED], N_H, ((), parts)),
        (N_INVERSE, kept[N_INVERSE], N_H, ((), parts)),
        (N_INNER,) + inner,
        (N_FIRST,) + first,
        (N_LOW, kept[N_LOW], N_H, ((), 1)),
        (N_FINAL, kept[N_FINAL], N_H, ((), 1)),
    ]
    outs = [
        (N_D_NODES, (NODE_CAP, D), f32, N_V, 1),
        (N_D_GRID, (grid, D), f32, N_H, parts),
    ]
    if keep_state:
        outs.append((N_D_NEXT, (depth, grid), f32, N_H, 1))
    scratch = [
        ("d_update", (depth, grid), bf16),
        (N_ACT, (grid, D), bf16),
        (N_D_MIXED, (grid, D), bf16),
        (N_D_HIDDEN, (grid, D), bf16),
    ]
    if not fresh:
        ins += [(N_SUMS, sums, N_H, ((), 1)), (N_GRADS, grads, N_H, ((), BLOCKS))]
    outs.append((N_SUMS, (8, D), f32, N_H, 1))
    grads_io(outs, scratch, grads, rows_all, swap)
    out = launch(
        body, ins, outs, scratch, micros=13, swap=swap
    )
    if keep_state:
        return out[0], out[1], out[2], out[3], out[4:]
    return out[0], out[1], None, out[2], out[3:]


def layer_backward(
    layer, d_nodes, returned, d_edges, kept, weights, vectors, send_row, recv, picks_row,
    sums, after,
):
    count = kept[N_HIDDEN].shape[0]
    halo_rows = kept[N_HALO].shape[0]
    edge_first, edge_inner, node_first, node_inner = weights
    at_edge, at_node = 2 + layer, 2 + LAYERS + layer
    top = d_edges is None

    def body(k):
        start_sums(k, sums is None)
        k.wait(N_D_NODES)
        if not top:
            high, rest = halves(k.returned[...])
            hot = cols_hot(k.picks_row[...], NODE_CAP)
            k.d_nodes[...] += dense(hot, high) + dense(hot, rest)
        for name in (N_NODE_HIDDEN, N_NODE_NORMED, N_NODE_INVERSE, N_NODE_INNER, N_NODE_FIRST):
            k.wait(name)

        def node_tile(t):
            rows = row_tile(t, TILE)
            act, d_mixed, d_hidden = backward_rows(
                k, at_node, k.d_nodes[rows], k.node_hidden[rows], k.node_normed[rows],
                k.node_inverse[rows], k.node_inner[...], k.sums, 3,
            )
            k.node_act[rows] = act
            k.node_d_mixed[rows] = d_mixed
            k.node_d_hidden[rows] = d_hidden
            d_in = dense_right(d_hidden, k.node_first[...])
            k.d_nodes[rows] += d_in[:, 0:D]
            high, rest = halves(d_in[:, D : 2 * D])
            k.d_total[rows, 0:D] = high
            k.d_total[rows, D : 2 * D] = rest

        loop(NODE_CAP // TILE, node_tile)
        for name in (N_D_NODES, N_NODE_ACT, N_NODE_D_MIXED, N_NODE_D_HIDDEN):
            k.flush(name)
        k.wait(N_EDGE_INNER)
        k.wait(N_EDGE_FIRST)

        def tile(t):
            rows = row_tile(t, TILE)
            both = dense(rows_hot(k.recv[rows], NODE_CAP), k.d_total[...])
            upstream = both[:, 0:D] + both[:, D : 2 * D]
            if not top:
                k.wait(N_D_EDGES, t)
                upstream = k.d_edges[rows] + upstream
            for name in (N_HIDDEN, N_NORMED, N_INVERSE):
                k.wait(name, t)
            act, d_mixed, d_hidden = backward_rows(
                k, at_edge, upstream, k.hidden[rows], k.normed[rows], k.inverse[rows],
                k.edge_inner[...], k.sums, 0,
            )
            k.act[rows] = act
            k.d_mixed[rows] = d_mixed
            k.d_hidden[rows] = d_hidden
            k.d_edges[rows] = upstream + dense_right(d_hidden, k.edge_first[0:D])
            for name in (N_ACT, N_D_MIXED, N_D_HIDDEN, N_D_EDGES):
                k.flush(name, t)

        loop(count // TILE, tile)
        k.flush(N_SUMS)
        to_halo = dense(cols_hot(k.send_row[...], halo_rows, NODE_CAP), k.d_hidden[...])
        high, rest = halves(to_halo)
        from_send = k.edge_first[D : 2 * D]
        k.d_halo[...] = dense_right(high, from_send) + dense_right(rest, from_send)
        k.halo_high[...] = high
        k.halo_rest[...] = rest

    parts = count // TILE
    ins = [
        (N_RECV, recv, N_V),
        (N_SEND_ROW, send_row, N_V),
        (N_VECTORS, vectors, N_V),
    ]
    if not top:
        ins += [(N_RETURNED, returned, N_V), (N_PICKS_ROW, picks_row, N_V)]
    ins += [
        (N_D_NODES, d_nodes, N_H, ((), 1)),
        (N_NODE_HIDDEN, kept[N_NODE_HIDDEN], N_H, ((), 1)),
        (N_NODE_NORMED, kept[N_NODE_NORMED], N_H, ((), 1)),
        (N_NODE_INVERSE, kept[N_NODE_INVERSE], N_H, ((), 1)),
        (N_NODE_INNER,) + node_inner,
        (N_NODE_FIRST,) + node_first,
        (N_EDGE_INNER,) + edge_inner,
        (N_EDGE_FIRST,) + edge_first,
    ]
    if sums is not None:
        ins.append((N_SUMS, sums, N_H, ((), 1)))
    if not top:
        ins.append((N_D_EDGES, d_edges, N_H, ((), parts)))
    ins += [
        (N_HIDDEN, kept[N_HIDDEN], N_H, ((), parts)),
        (N_NORMED, kept[N_NORMED], N_H, ((), parts)),
        (N_INVERSE, kept[N_INVERSE], N_H, ((), parts)),
    ]
    outs = [
        (N_D_HALO, (halo_rows, D), f32, N_V, 1),
        (N_HALO_HIGH, (halo_rows, D), bf16, N_V, 1),
        (N_HALO_REST, (halo_rows, D), bf16, N_V, 1),
        (N_D_NODES, (NODE_CAP, D), f32, N_H, 1),
        (N_NODE_ACT, (NODE_CAP, D), bf16, N_H, 1),
        (N_NODE_D_MIXED, (NODE_CAP, D), bf16, N_H, 1),
        (N_NODE_D_HIDDEN, (NODE_CAP, D), bf16, N_H, 1),
        (N_ACT, (count, D), bf16, N_H, parts),
        (N_D_MIXED, (count, D), bf16, N_H, parts),
        (N_D_HIDDEN, (count, D), bf16, N_H, parts),
        (N_D_EDGES, (count, D), f32, N_H, parts),
        (N_SUMS, (8, D), f32, N_H, 1),
    ]
    scratch = [("d_total", (NODE_CAP, 2 * D), bf16)]
    out = launch(body, ins, outs, scratch, micros=14, after=after)
    names = [item[0] for item in outs]
    return dict(zip(names, out))


def layer_grads(found, kept, edge_first, send_row, recv_row, rows_all, grads, swap, after):
    count = kept[N_HIDDEN].shape[0]
    halo_rows = kept[N_HALO].shape[0]
    fresh = grads is None

    def body(k):
        k.wait(N_D_HIDDEN)
        k.wait(N_FROM_SEND)
        k.wait(N_FROM_RECV)
        to_recv = dense(cols_hot(k.recv_row[...], NODE_CAP), k.d_hidden[...])
        to_send = dense(cols_hot(k.send_row[...], NODE_CAP), k.d_hidden[...])
        recv_high, recv_rest = halves(to_recv)
        send_high, send_rest = halves(to_send)
        from_send, from_recv = k.from_send[...], k.from_recv[...]
        k.wait(N_D_NODES)
        k.d_nodes[...] += (
            dense_right(send_high, from_send)
            + dense_right(send_rest, from_send)
            + dense_right(recv_high, from_recv)
            + dense_right(recv_rest, from_recv)
        )
        k.flush(N_D_NODES)
        if not fresh:
            k.wait(N_GRADS)
        low = k.node_low[...]
        put_grad(
            k, fresh, D,
            dense_left(low, send_high)
            + dense_left(low, send_rest)
            + dense_left(k.halo[...], k.halo_high[...])
            + dense_left(k.halo[...], k.halo_rest[...]),
        )
        put_grad(k, fresh, 2 * D, dense_left(low, recv_high) + dense_left(low, recv_rest))
        k.wait(N_EDGES_LOW)
        weight_grad(k, fresh, 0, k.edges_low, k.d_hidden)
        k.wait(N_ACT)
        k.wait(N_D_MIXED)
        weight_grad(k, fresh, 3 * D, k.act, k.d_mixed)
        k.wait(N_TOTAL)
        k.wait(N_NODE_D_HIDDEN)
        weight_grad(k, fresh, 4 * D, k.node_low, k.node_d_hidden)
        weight_grad(k, fresh, 5 * D, k.total, k.node_d_hidden)
        k.wait(N_NODE_ACT)
        k.wait(N_NODE_D_MIXED)
        weight_grad(k, fresh, 6 * D, k.node_act, k.node_d_mixed)
        if fresh and rows_all > 7 * D:
            k.grads[:, 7 * D :, :] = jnp.zeros((BLOCKS, rows_all - 7 * D, BLOCK), f32)
        flush_grads(k, swap)

    source, _, (first, _) = edge_first
    ins = [
        (N_NODE_LOW, kept[N_NODE_LOW], N_V),
        (N_HALO, kept[N_HALO], N_V),
        (N_HALO_HIGH, found[N_HALO_HIGH], N_V),
        (N_HALO_REST, found[N_HALO_REST], N_V),
        (N_RECV_ROW, recv_row, N_V),
        (N_SEND_ROW, send_row, N_V),
        (N_D_HIDDEN, found[N_D_HIDDEN], N_H, ((), 1)),
        (N_FROM_SEND, source, N_W, (first + D, D)),
        (N_FROM_RECV, source, N_W, (first + 2 * D, D)),
        (N_D_NODES, found[N_D_NODES], N_H, ((), 1)),
    ]
    if not fresh:
        ins.append((N_GRADS, grads, N_H, ((), BLOCKS)))
    ins += [
        (N_EDGES_LOW, kept[N_EDGES_LOW], N_H, ((), 1)),
        (N_ACT, found[N_ACT], N_H, ((), 1)),
        (N_D_MIXED, found[N_D_MIXED], N_H, ((), 1)),
        (N_TOTAL, kept[N_TOTAL], N_H, ((), 1)),
        (N_NODE_D_HIDDEN, found[N_NODE_D_HIDDEN], N_H, ((), 1)),
        (N_NODE_ACT, found[N_NODE_ACT], N_H, ((), 1)),
        (N_NODE_D_MIXED, found[N_NODE_D_MIXED], N_H, ((), 1)),
    ]
    outs = [(N_D_NODES, (NODE_CAP, D), f32, N_H, 1)]
    scratch = []
    grads_io(outs, scratch, grads, rows_all, swap)
    out = launch(body, ins, outs, scratch, micros=14, swap=swap, after=after)
    return out[0], out[1:]


def encoder_backward(
    step, d_grid, d_nodes, returned, d_next, kept, weights, vectors, assign, picks_row, scales,
    grads, sums, others, swap, after,
):
    feats = kept[N_FEATS]
    depth, grid = feats.shape
    first, inner = weights
    fresh = grads is None
    keep_state = step > 0
    rows_all = depth + D
    if others is not None:
        embed_grads, all_sums = others
        embed_rows = embed_grads.shape[1]
        at_vectors = depth + D + embed_rows
        rows_all = swap[1]

    def body(k):
        start_sums(k, fresh)
        k.wait(N_D_NODES)
        high, rest = halves(k.returned[...])
        hot = cols_hot(k.picks_row[...], NODE_CAP)
        nodes = k.d_nodes[...] + dense(hot, high) + dense(hot, rest)
        high, rest = halves(nodes)
        k.both[:, 0:D] = high
        k.both[:, D : 2 * D] = rest
        k.wait(N_INNER)

        def tile(t):
            rows = row_tile(t, TILE)
            for name in (N_HIDDEN, N_NORMED, N_INVERSE, N_D_GRID):
                k.wait(name, t)
            both = dense(rows_hot(k.assign[rows], NODE_CAP), k.both[...])
            upstream = k.d_grid[rows] + both[:, 0:D] + both[:, D : 2 * D]
            act, d_mixed, d_hidden = backward_rows(
                k, 0, upstream, k.hidden[rows], k.normed[rows], k.inverse[rows],
                k.inner[...], k.sums, 0,
            )
            k.act[rows] = act
            k.d_mixed[rows] = d_mixed
            k.d_hidden[rows] = d_hidden

        loop(grid // TILE, tile)
        if keep_state:
            k.wait(N_FIRST)
            k.wait(N_D_NEXT)
            k.d_state[...] = (
                k.d_next[...] + dense_right(k.first[...], k.d_hidden[...]) / k.scales[...]
            )
            k.flush(N_D_STATE)
        k.wait(N_FEATS)
        if others is None:
            k.flush(N_SUMS)
            put_grad(k, True, 0, dense(k.feats[...], k.d_hidden[...]))
            weight_grad(k, True, depth, k.act, k.d_mixed)
            k.flush(N_GRADS)
            return
        k.wait(N_BEFORE)
        k.grads[:, 0 : depth + D, :] = k.before[...]
        put_grad(k, False, 0, dense(k.feats[...], k.d_hidden[...]))
        weight_grad(k, False, depth, k.act, k.d_mixed)
        k.wait(N_EMBED_GRADS)
        k.grads[:, depth + D : at_vectors, :] = k.embed_grads[...]
        k.grads[:, at_vectors:, :] = jnp.zeros((BLOCKS, rows_all - at_vectors, BLOCK), f32)
        sources = [(k.sums, 0), (k.sums_embed, 0)]
        sources += [(getattr(k, N_SUMS_ + str(l)), 0) for l in range(LAYERS)]
        sources += [(getattr(k, N_SUMS_ + str(l)), 3) for l in range(LAYERS)]
        sources += [(k.sums_dec, 0)]
        for i, (source, at) in enumerate(sources):
            set_grad(k, at_vectors + 3 * i, source[at : at + 3, :])
        k.flush_swap()

    parts = grid // TILE
    ins = [
        (N_RETURNED, returned, N_V),
        (N_PICKS_ROW, picks_row, N_V),
        (N_ASSIGN, assign, N_V),
        (N_SCALES, scales, N_V),
        (N_VECTORS, vectors, N_V),
        (N_D_NODES, d_nodes, N_H, ((), 1)),
        (N_INNER,) + inner,
        (N_D_GRID, d_grid, N_H, ((), parts)),
        (N_HIDDEN, kept[N_HIDDEN], N_H, ((), parts)),
        (N_NORMED, kept[N_NORMED], N_H, ((), parts)),
        (N_INVERSE, kept[N_INVERSE], N_H, ((), parts)),
        (N_FEATS, feats, N_H, ((), 1)),
    ]
    outs = []
    if keep_state:
        ins += [(N_FIRST,) + first, (N_D_NEXT, d_next, N_H, ((), 1))]
        outs.append((N_D_STATE, (depth, grid), f32, N_H, 1))
    scratch = [
        ("both", (NODE_CAP, 2 * D), bf16),
        (N_ACT, (grid, D), bf16),
        (N_D_MIXED, (grid, D), bf16),
        (N_D_HIDDEN, (grid, D), bf16),
    ]
    if not fresh:
        ins.append((N_SUMS, sums, N_H, ((), 1)))
    if others is None:
        outs.append((N_SUMS, (8, D), f32, N_H, 1))
        outs.append((N_GRADS, (BLOCKS, rows_all, BLOCK), f32, N_H, BLOCKS))
    else:
        ins.append((N_BEFORE, grads, N_H, ((), BLOCKS)))
        ins.append((N_EMBED_GRADS, embed_grads, N_H, ((), BLOCKS)))
        ins += [(N_SUMS_ + str(name), value, N_V) for name, value in all_sums.items()]
        scratch.append((N_GRADS, (BLOCKS, rows_all, BLOCK), f32))
    out = launch(body, ins, outs, scratch, micros=10, swap=swap, after=after)
    if others is not None:
        return out
    return out if keep_state else (None, out[0], out[1])


def embed_backward(d_first, d_second, kept, geometry, inner, vectors, after):
    count = kept[N_HIDDEN].shape[0]
    features = geometry.shape[0]

    def body(k):
        start_sums(k, True)
        k.wait(N_INNER)

        def tile(t):
            rows = row_tile(t, TILE)
            for name in (N_D_FIRST, N_D_SECOND, N_HIDDEN, N_NORMED, N_INVERSE):
                k.wait(name, t)
            act, d_mixed, d_hidden = backward_rows(
                k, 1, k.d_first[rows] + k.d_second[rows], k.hidden[rows], k.normed[rows],
                k.inverse[rows], k.inner[...], k.sums, 0,
            )
            k.act[rows] = act
            k.d_mixed[rows] = d_mixed
            k.d_hidden[rows] = d_hidden

        loop(count // TILE, tile)
        k.flush(N_SUMS)
        set_grad(k, 0, dense(k.geometry[...], k.d_hidden[...]))
        weight_grad(k, True, features, k.act, k.d_mixed)
        k.flush(N_GRADS)

    parts = count // TILE
    ins = [
        (N_GEOMETRY, geometry, N_V),
        (N_VECTORS, vectors, N_V),
        (N_INNER,) + inner,
        (N_D_FIRST, d_first, N_H, ((), parts)),
        (N_D_SECOND, d_second, N_H, ((), parts)),
        (N_HIDDEN, kept[N_HIDDEN], N_H, ((), parts)),
        (N_NORMED, kept[N_NORMED], N_H, ((), parts)),
        (N_INVERSE, kept[N_INVERSE], N_H, ((), parts)),
    ]
    return launch(
        body,
        ins,
        [
            (N_SUMS, (8, D), f32, N_H, 1),
            (N_GRADS, (BLOCKS, features + D, BLOCK), f32, N_H, BLOCKS),
        ],
        [
            (N_ACT, (count, D), bf16),
            (N_D_MIXED, (count, D), bf16),
            (N_D_HIDDEN, (count, D), bf16),
        ],
        micros=11,
        after=after,
    )


def coded_rows(rows):
    return rows + up_to(rows // CODED, 16)


def encode(source, first, rows, target, scale):
    scale[...] = jnp.zeros(scale.shape, f32)

    def step(t):
        value = source[pl.ds(pl.multiple_of(first + t * CODED, CODED), CODED)]
        top = jnp.maximum(jnp.max(jnp.abs(value), 0, keepdims=True), 1e-30)
        exponent = jnp.ceil(jnp.log2(top))
        scale[pl.ds(t, 1), :] = exponent
        value = jnp.round(value * (CODE_TOP * jnp.exp2(-exponent)))
        target[row_tile(t, CODED)] = value.astype(jnp.int32).astype(jnp.int16)

    loop(rows // CODED, step, 8)
    more = coded_rows(rows) - rows
    target[rows : rows + more] = scale[0:more].astype(jnp.int32).astype(jnp.int16)


def scales_of(coded, rows, scale):
    more = coded_rows(rows) - rows
    exponent = coded[rows : rows + more].astype(jnp.int32).astype(f32)
    scale[0:more] = jnp.exp2(exponent) * (1.0 / CODE_TOP)


def decoded(coded, scale, t):
    return coded[row_tile(t, CODED)].astype(jnp.int32).astype(f32) * scale[pl.ds(t, 1), :]


def difference(p, order):
    return sum(bit for i, bit in enumerate(reversed(order)) if p >> i & 1)


CORES, OVER_X, TURN, JOIN = range(4)


def combine(jobs, order, place, after):
    regions = 2 ** len(order)
    operands, out_shape, scratch_shapes, plans = [], [], [], []
    squares = False

    def buffer(shape, dtype):
        scratch_shapes.append(pltpu.VMEM(shape, dtype))
        return len(scratch_shapes) - 1

    def output(shape, dtype):
        out_shape.append(jax.ShapeDtypeStruct(shape, dtype))
        return len(out_shape) - 1

    for kind, arrays, ways in jobs:
        loads, stores = [], []
        for array in arrays:
            loads.append((len(operands), buffer(array.shape, array.dtype)))
            operands.append(array)
        blocks, size = 1, 0
        if kind == CORES:
            size = arrays[0].shape[0]
            stores.append((output((size, BLOCK), f32), loads[0][1], None))
        elif kind == JOIN:
            shape = arrays[0].shape
            at = output((len(arrays) * shape[0],) + shape[1:], jnp.int16)
            stores = [(at, item[1], i * shape[0]) for i, item in enumerate(loads)]
        else:
            rows = arrays[0].shape[0]
            if kind == OVER_X:
                size = rows // regions
            else:
                code = arrays[1].shape[1]
                size = max(r for r in range(CODED, code, CODED) if coded_rows(r) == code)
            blocks = rows // size // ways
            if ways > 1:
                at = output((blocks * size, BLOCK), f32)
                stores.append((at, buffer((blocks * size, BLOCK), f32), None))
            else:
                squares = True
        if kind != JOIN:
            for _ in range(max(ways - 1, 1)):
                shape = (blocks, coded_rows(size), BLOCK)
                stores.append((output(shape, jnp.int16), buffer(shape, jnp.int16), None))
        work = None
        if kind != JOIN:
            rows = arrays[0].shape[0]
            work = (buffer((rows, BLOCK), f32), buffer((up_to(rows // CODED, 16), BLOCK), f32))
        plans.append((kind, ways, blocks, size, loads, stores, work))
    count = len(out_shape)
    if squares:
        out_shape.append(jax.ShapeDtypeStruct((CODED, BLOCK), f32))
    most = max(len(plan[5]) for plan in plans)

    def kernel(*refs):
        region = refs[0][1]
        ins = refs[1 : 1 + len(operands)]
        outs = refs[1 + len(operands) + len(after) :][: len(out_shape)]
        rest = refs[1 + len(operands) + len(after) + len(out_shape) :]
        sem_in, sem_out = rest[-2:]

        def load(at, kept):
            return pltpu.make_async_copy(ins[at], rest[kept], sem_in.at[at])

        def store(job, i):
            at, kept, first = plans[job][5][i]
            target = outs[at]
            if first is not None:
                target = target.at[pl.ds(first, rest[kept].shape[0])]
            return pltpu.make_async_copy(rest[kept], target, sem_out.at[job, i])

        for plan in plans:
            for item in plan[4]:
                load(*item).start()
        if squares:
            outs[-1][...] = jnp.zeros((CODED, BLOCK), f32)
        for job, (kind, ways, blocks, size, loads, stores, work) in enumerate(plans):
            for item in loads:
                load(*item).wait()
            values = [rest[item[1]] for item in loads]
            results = [rest[item[1]] for item in stores]
            if kind == CORES:
                total, scale = rest[work[0]], rest[work[1]]

                def step(t):
                    at = row_tile(t, 256)
                    values[0][at] += values[1][at]
                    total[at] = values[2][at] + values[3][at]

                loop(size // 256, step)
                encode(total, 0, size, results[1].at[0], scale)
            elif kind != JOIN:
                total, scale = rest[work[0]], rest[work[1]]
                mine = values[0]
                if kind == OVER_X:
                    rows = size * regions
                    scales_of(values[1].at[0], rows, scale)

                    def step(t):
                        at = row_tile(t, CODED)
                        total[at] = mine[at] + decoded(values[1].at[0], scale, t)

                    loop(rows // CODED, step, 8)
                else:
                    for i in range(blocks * ways):
                        for j, coded in enumerate(values[1:]):
                            scales_of(coded.at[i], size, scale)

                            def step(t):
                                at = pl.ds(pl.multiple_of(i * size + t * CODED, CODED), CODED)
                                value = total[at] if j else mine[at]
                                total[at] = value + decoded(coded.at[i], scale, t)

                            loop(size // CODED, step, 8)

                def first_row(p):
                    if kind == OVER_X:
                        return lax.bitwise_xor(region, difference(p, order)) * size
                    return p * size

                for p in range(blocks * ways):
                    way, i = p // blocks, p % blocks
                    if ways > 1 and way == 0:

                        def step(t):
                            at = pl.ds(pl.multiple_of(first_row(p) + t * CODED, CODED), CODED)
                            to = pl.ds(pl.multiple_of(i * size + t * CODED, CODED), CODED)
                            results[0][to] = total[at]

                        loop(size // CODED, step, 8)
                    else:
                        encode(total, first_row(p), size, results[way].at[i], scale)
                if ways == 1:

                    def square(t):
                        value = total[row_tile(t, CODED)]
                        outs[-1][...] += value * value

                    loop(size // CODED, square, 8)
            for i in range(len(stores)):
                store(job, i).start()
        for job in range(len(plans)):
            for i in range(len(plans[job][5])):
                store(job, i).wait()

    any_space = pl.BlockSpec(memory_space=pl.ANY)
    out_specs = [any_space] * count
    if squares:
        out_specs.append(pl.BlockSpec(memory_space=pltpu.VMEM))
    out = pl.pallas_call(
        kernel,
        out_shape=out_shape,
        in_specs=[pl.BlockSpec(memory_space=pltpu.SMEM)]
        + [any_space] * (len(operands) + len(after)),
        out_specs=out_specs,
        scratch_shapes=scratch_shapes
        + [
            pltpu.SemaphoreType.DMA((len(operands),)),
            pltpu.SemaphoreType.DMA((len(jobs), most)),
        ],
        compiler_params=pltpu.CompilerParams(vmem_limit_bytes=56 * 2**20),
        cost_estimate=cost_of(5),
    )(place, *operands, *after)
    parts = []
    for plan in plans:
        found = []
        for item in plan[5]:
            if item[0] not in found:
                found.append(item[0])
        parts.append([out[i] for i in found])
    return parts, (out[-1] if squares else None)


def update_weights(factor, place, order, groups, masters, moments, squares, chunks):
    count = len(masters)
    rows_of = [c[3] for c in chunks]
    half = groups[0][0].shape[0]
    places = 2 * half
    block_rows = []
    for group in groups:
        code = group[0].shape[1]
        block_rows.append(max(r for r in range(CODED, code, CODED) if coded_rows(r) == code))

    def kernel(*refs):
        scale = refs[0][0, 0]
        region = refs[1][1]
        group_refs = refs[2 : 2 + 2 * len(groups)]
        at = 2 + 2 * len(groups)
        param_refs = refs[at : at + 3 * count]
        out_refs = refs[at + 3 * count : at + 6 * count]
        rest = refs[at + 6 * count :]
        sem_in, sem_out, sem_grad = rest[-3:]
        factors = rest[-4]
        coded_refs = rest[3 * len(chunks) : 3 * len(chunks) + 2 * len(groups)]
        grad_refs = rest[3 * len(chunks) + 2 * len(groups) : 3 * len(chunks) + 3 * len(groups)]

        def grad_copies(g):
            return [
                pltpu.make_async_copy(group_refs[i], coded_refs[i], sem_grad.at[i])
                for i in (2 * g, 2 * g + 1)
            ]

        def decode(g):
            rows = block_rows[g]

            for p in range(places):
                coded = coded_refs[2 * g + p // half].at[p % half]
                first = lax.bitwise_xor(region, difference(p, order)) * rows
                scales_of(coded, rows, factors)

                def step(t):
                    at = pl.ds(pl.multiple_of(first + t * CODED, CODED), CODED)
                    grad_refs[g][at] = decoded(coded, factors, t)

                loop(rows // CODED, step, 8)

        def piece(ref, chunk):
            for i in chunk[1]:
                ref = ref.at[i]
            if chunk[3] < ref.shape[0]:
                ref = ref.at[pl.ds(chunk[2], chunk[3])]
            return ref

        def copies(i):
            chunk = chunks[i]
            w = chunk[0]
            found = []
            for j in range(3):
                found.append(
                    pltpu.make_async_copy(
                        piece(param_refs[3 * w + j], chunk), rest[3 * i + j], sem_in.at[3 * i + j]
                    )
                )
            return found

        def stores(i):
            chunk = chunks[i]
            return [
                pltpu.make_async_copy(
                    rest[3 * i + (j + 1) % 3],
                    piece(out_refs[3 * chunk[0] + j], chunk),
                    sem_out.at[3 * i + j],
                )
                for j in range(3)
            ]

        started = set()
        for i in range(len(chunks)):
            if chunks[i][4] not in started:
                started.add(chunks[i][4])
                for copy in grad_copies(chunks[i][4]):
                    copy.start()
            for copy in copies(i):
                copy.start()
        for i in range(len(chunks)):
            if chunks[i][4] in started:
                started.remove(chunks[i][4])
                for copy in grad_copies(chunks[i][4]):
                    copy.wait()
                decode(chunks[i][4])
            for copy in copies(i):
                copy.wait()
            master_ref, moment_ref, square_ref = rest[3 * i : 3 * i + 3]
            grad_ref, first_row = grad_refs[chunks[i][4]], chunks[i][5]

            def rows_step(rows, grad_rows):
                first, second, master = adam(
                    master_ref[rows],
                    moment_ref[rows],
                    square_ref[rows],
                    grad_ref[grad_rows] * scale,
                )
                moment_ref[rows] = first
                square_ref[rows] = second
                master_ref[rows] = master

            if rows_of[i] % 128 == 0:
                loop(
                    rows_of[i] // 128,
                    lambda t: rows_step(
                        row_tile(t, 128), pl.ds(pl.multiple_of(first_row + t * 128, 8), 128)
                    ),
                )
            else:
                rows_step(slice(0, rows_of[i]), slice(first_row, first_row + rows_of[i]))
            for copy in stores(i):
                copy.start()
        for i in range(len(chunks)):
            for copy in stores(i):
                copy.wait()

    any_space = pl.BlockSpec(memory_space=pl.ANY)
    scratch_shapes = []
    for rows in rows_of:
        scratch_shapes += [pltpu.VMEM((rows, BLOCK), f32)] * 3
    coded_parts = [part for group in groups for part in group]
    scratch_shapes += [pltpu.VMEM(part.shape, part.dtype) for part in coded_parts]
    scratch_shapes += [pltpu.VMEM((places * rows, BLOCK), f32) for rows in block_rows]
    scratch_shapes.append(pltpu.VMEM((up_to(max(block_rows) // CODED, 16), BLOCK), f32))
    scratch_shapes.append(pltpu.SemaphoreType.DMA((3 * len(chunks),)))
    scratch_shapes.append(pltpu.SemaphoreType.DMA((3 * len(chunks),)))
    scratch_shapes.append(pltpu.SemaphoreType.DMA((2 * len(groups),)))
    params = [value for item in zip(masters, moments, squares) for value in item]
    return pl.pallas_call(
        kernel,
        out_shape=[jax.ShapeDtypeStruct(p.shape, f32) for p in params],
        in_specs=[pl.BlockSpec(memory_space=pltpu.SMEM)] * 2
        + [any_space] * (len(coded_parts) + len(params)),
        out_specs=[any_space] * len(params),
        scratch_shapes=scratch_shapes,
        compiler_params=pltpu.CompilerParams(vmem_limit_bytes=56 * 2**20),
        cost_estimate=cost_of(0),
    )(factor, place, *coded_parts, *params)


def adam(master, moment, square, grad):
    first = beta_first * moment + (1 - beta_first) * grad
    second = beta_second * square + (1 - beta_second) * grad * grad
    ratio = (
        first
        / (1 - beta_first**STEP_COUNT)
        / (jnp.sqrt(second / (1 - beta_second**STEP_COUNT)) + adam_eps)
    )
    return (first, second, master - learn_rate * (ratio + decay_weight * master))


def pad_rows(value, rows):
    return jnp.pad(value, ((0, rows - value.shape[0]), (0, 0)))


def body(
    initial_state,
    target_states,
    var_means,
    var_scales,
    delta_scales,
    edge_geometry,
    node_counts,
    edge_counts,
    receivers,
    senders,
    send_lists,
    grid_nodes,
    cell_area,
    step_weights,
    *params,
):
    masters, moments, squares = params[0::3], params[1::3], params[2::3]
    enc_w, embed_w, edge_w, node_w, dec_w, inner_w, vector_w, head_w = masters
    variables = enc_w.shape[0]
    depth = up_to(variables, 16)
    features = embed_w.shape[0]
    feature_rows = up_to(features, 16)
    vector_rows = up_to(vector_w.shape[0], 16)
    last_block = 2 + 2 * LAYERS

    def gather(pieces):
        return lax.all_gather(jnp.concatenate([p.astype(bf16) for p in pieces], 0), N_REP)

    start = gather(
        [
            pad_rows(enc_w, depth),
            inner_w[0],
            pad_rows(embed_w, feature_rows),
            inner_w[1],
            pad_rows(vector_w, vector_rows),
        ]
    )
    of_layer = [
        gather([edge_w[l], inner_w[2 + l], node_w[l], inner_w[2 + LAYERS + l]])
        for l in range(LAYERS)
    ]
    end = gather([dec_w, inner_w[last_block], pad_rows(head_w, depth)])
    enc_first = (start, N_W, (0, depth))
    enc_inner = (start, N_W, (depth, D))
    embed_first = (start, N_W, (depth + D, feature_rows))
    embed_inner = (start, N_W, (depth + D + feature_rows, D))
    at_vectors = depth + 2 * D + feature_rows
    vectors = (
        start[:, at_vectors:, :].astype(f32).transpose(1, 0, 2).reshape(vector_rows, D)
    )
    layer_weights = [
        (
            (of_layer[l], N_W, (0, 3 * D)),
            (of_layer[l], N_W, (3 * D, D)),
            (of_layer[l], N_W, (4 * D, 2 * D)),
            (of_layer[l], N_W, (6 * D, D)),
        )
        for l in range(LAYERS)
    ]
    dec_weights = (
        (end, N_W, (0, 2 * D)),
        (end, N_W, (2 * D, D)),
        (end, N_W, (3 * D, depth)),
    )

    count = node_counts[0]
    send_from = jnp.where(senders < NODE_CAP, senders % count, senders)
    live = jnp.arange(receivers.shape[0]) < edge_counts[0]
    recv = jnp.where(live, receivers, -1)
    picks = (send_lists[0] % count).reshape(-1)
    assign = grid_nodes % count
    regions, slots = send_lists.shape[1:]
    send, send_row = send_from[:, None], send_from[None, :]
    recv, recv_row = recv[:, None], recv[None, :]
    picks, picks_row = picks[:, None], picks[None, :]
    assign, assign_row = assign[:, None], assign[None, :]

    def exchange(rows):
        table = rows.reshape(regions, slots, D)
        table = lax.all_to_all(table, N_REGION, split_axis=0, concat_axis=0, tiled=True)
        return table.reshape(regions * slots, D)

    def column(value, fill):
        return jnp.pad(value, (0, depth - variables), constant_values=fill)[:, None]

    means, scales, delta = column(var_means, 0), column(var_scales, 1), column(delta_scales, 1)
    state = pad_rows(initial_state[0].T, depth)
    target = jnp.pad(
        target_states[0].transpose(0, 2, 1), ((0, 0), (0, depth - variables), (0, 0))
    )
    area = cell_area[None, :]
    geometry = pad_rows(edge_geometry.T, feature_rows).astype(bf16)
    plan = step_weights

    place = jnp.stack([lax.axis_index(N_REP), lax.axis_index(N_REGION)]).astype(jnp.int32)
    bits = [1 << i for i in range(regions.bit_length() - 1)]
    turns = [bits[:1]] + [bits[i : i + 2] for i in range(1, len(bits), 2)]
    unit = CODED * regions
    dec_rows, layer_rows = up_to(3 * D + depth, unit), up_to(7 * D, unit)
    start_rows = up_to(at_vectors + vector_rows, unit)

    def partner(value, axis, bit):
        count = lax.axis_size(axis)
        return lax.ppermute(value, axis, [(i, i ^ bit) for i in range(count)])

    weight_local = (
        jnp.sum(plan.astype(f32)) * jnp.sum(cell_area) * variables * lax.axis_size(N_REP)
    )
    weight_total = jnp.broadcast_to(weight_local, (8, BLOCK))
    for bit in bits:
        weight_total = weight_total + partner(weight_total, N_REGION, bit)
    weight_total = weight_total[0, 0]
    inverse_total = (1.0 / weight_total).reshape(1, 1)

    edges0, edges0_low, *keep_embed = embed_forward(geometry, embed_first, embed_inner, 1, vectors)
    keep_embed = dict(zip((N_HIDDEN, N_NORMED, N_INVERSE), keep_embed))
    records = []
    loss_local = 0.0
    for step in range(STEPS):
        nodes, node_low, outgoing, latent, low, feats, hidden, normed, inverse = encoder_forward(
            state, means, scales, enc_first, enc_inner, vectors, assign_row, picks
        )
        keep_enc = {N_FEATS: feats, N_HIDDEN: hidden, N_NORMED: normed, N_INVERSE: inverse}
        edges, edges_low = edges0, edges0_low
        layers = []
        for l in range(LAYERS):
            halo = exchange(outgoing)
            first = layer_weights[l][0]
            local = layer_local(l, edges_low, node_low, first, vectors, send, recv)
            from_send = (first[0], N_W, (first[2][0] + D, D))
            before = edges_low
            edges, edges_low, nodes, node_low, outgoing, kept = layer_forward(
                l, local, edges, nodes, node_low, halo, (from_send,) + layer_weights[l][1:],
                vectors, send, recv_row, picks, l == LAYERS - 1,
            )
            kept[N_EDGES_LOW] = before
            layers.append(kept)
        state, loss, keep_dec = decoder_forward(
            step, state, target, latent, low, node_low, dec_weights, vectors,
            assign, delta, area, plan,
        )
        loss_local = loss_local + loss[0, 0]
        records.append((keep_enc, layers, keep_dec))

    class Sum:
        def __init__(self, parts):
            self.parts = list(parts)
            self.stage = -2
            self.halves = None

        def job(self):
            p, count = self.parts, len(turns)
            if self.stage == -2:
                return (CORES, [p[0], partner(p[1], N_REP, 1), p[2], partner(p[3], N_REP, 1)], 0)
            if self.stage == -1:
                return (OVER_X, [p[0], partner(p[1], N_REP, 2)], 2 ** len(turns[0]))
            if self.stage < count:
                turn, last = turns[self.stage], self.stage == count - 1
                ways = 1 if last else 2 ** len(turns[self.stage + 1])
                got = [
                    partner(p[q], N_REGION, difference(q, turn)) for q in range(1, 2 ** len(turn))
                ]
                return (TURN, [p[0]] + got, ways)
            turn = turns[2 * count - 1 - self.stage]
            got = [partner(p[0], N_REGION, difference(q, turn)) for q in range(1, 2 ** len(turn))]
            return (JOIN, [p[0]] + got, 0)

        def done(self, parts):
            self.parts = parts
            self.stage += 1
            if self.stage == 2 * len(turns) - 1:
                self.halves = [parts[0], partner(parts[0], N_REGION, bits[0])]

    all_squares = []
    on_way = {}
    arrived = []

    def advance(names, after):
        names = [name for name in names if on_way[name].halves is None]
        if not names:
            return after
        jobs = [on_way[name].job() for name in names]
        parts, squares = combine(jobs, bits, place, list(after) + arrived)
        arrived.clear()
        if squares is not None:
            all_squares.append(jnp.sum(squares, 0))
        for name, found in zip(names, parts):
            on_way[name].done(found)
            if on_way[name].halves is not None:
                arrived.append(on_way[name].halves[1])
        return [parts[0][0]]

    d_state = None
    grads = {}
    d_embed = []
    for step in reversed(range(STEPS)):
        keep_enc, layers, keep_dec = records[step]
        final = step == 0
        d_nodes, d_grid, d_next, sums, grad = decoder_backward(
            step, regions, d_state, keep_dec, dec_weights, vectors, assign_row, delta, area, plan,
            inverse_total, *grads.get(N_DEC, (None, None)),
            (place, dec_rows) if final else None,
        )
        grads[N_DEC] = (grad if final else grad[0], sums)
        returned, d_edges = None, None
        after = []
        if final:
            on_way[N_DEC] = Sum(grad)
        for l in reversed(range(LAYERS)):
            old_grad, old_sums = grads.get(l, (None, None))
            found = layer_backward(
                l, d_nodes, returned, d_edges, layers[l], layer_weights[l], vectors,
                send_row, recv, picks_row, old_sums, after,
            )
            d_edges, sums = found[N_D_EDGES], found[N_SUMS]
            returned = exchange(found[N_D_HALO])
            after = advance(list(on_way), [sums]) + [returned] if final else []
            d_nodes, grad = layer_grads(
                found, layers[l], layer_weights[l][0], send_row, recv_row, layer_rows, old_grad,
                (place, layer_rows) if final else None, after,
            )
            grads[l] = (grad if final else grad[0], sums)
            after = []
            if final:
                on_way[l] = Sum(grad)
        d_embed.append(d_edges)
        others, swap = None, None
        if final:
            embed_sums, embed_grads = embed_backward(
                d_embed[0], d_embed[1], keep_embed, geometry, embed_inner, vectors, after
            )
            after = advance([0, 1, 2, N_DEC], [embed_sums])
            all_sums = {"embed": embed_sums}
            for name in [N_DEC] + list(range(LAYERS)):
                all_sums[name] = grads[name][1]
            others, swap = (embed_grads, all_sums), (place, start_rows)
        out = encoder_backward(
            step, d_grid, d_nodes, returned, d_next, keep_enc, (enc_first, enc_inner), vectors,
            assign, picks_row, scales, *grads.get(N_ENC, (None, None)), others, swap, after,
        )
        if not final:
            d_state, sums, grad = out
            grads[N_ENC] = (grad, sums)
    after = advance([N_DEC, 2, 1], [out[0]])
    on_way["start"] = Sum(out)
    while any(item.halves is None for item in on_way.values()):
        after = advance(list(on_way), after)

    def over_all(value):
        for bit in bits:
            value = value + partner(value, N_REGION, bit)
        for bit in (1, 2):
            value = value + partner(value, N_REP, bit)
        return value

    order = list(on_way)
    groups = [on_way[name].halves for name in order]
    squares_row = sum(all_squares)
    totals = over_all(jnp.stack([squares_row, jnp.broadcast_to(loss_local, (BLOCK,))]))
    gradient_norm = jnp.sqrt(jnp.sum(totals[0]))
    loss_total = totals[1, 0]
    factor = jnp.minimum(1.0, clip_limit / gradient_norm)

    last_group = len(groups) - 1
    chunks = []
    for l in reversed(range(LAYERS)):
        group = order.index(l)
        chunks += [(2, (l,), i * D, D, group, i * D) for i in range(3)]
        chunks.append((5, (2 + l,), 0, D, group, 3 * D))
        chunks += [(3, (l,), i * D, D, group, (4 + i) * D) for i in range(2)]
        chunks.append((5, (2 + LAYERS + l,), 0, D, group, 6 * D))
    chunks += [(4, (), i * D, D, 0, i * D) for i in range(2)]
    chunks.append((5, (last_block,), 0, D, 0, 2 * D))
    chunks.append((7, (), 0, variables, 0, 3 * D))
    chunks.append((0, (), 0, variables, last_group, 0))
    chunks.append((5, (0,), 0, D, last_group, depth))
    chunks.append((1, (), 0, features, last_group, depth + D))
    chunks.append((5, (1,), 0, D, last_group, depth + D + feature_rows))
    chunks.append((6, (), 0, vector_w.shape[0], last_group, at_vectors))
    new = update_weights(
        factor.reshape(1, 1), place, bits, groups, masters, moments, squares, chunks
    )
    weight_copies = jnp.concatenate(
        [new[3 * i + 2].reshape(1, -1) for i in range(len(masters))], 1
    ).astype(bf16)
    return (loss_total, weight_total, gradient_norm, *new, weight_copies)


def solution(mesh):
    two = P(None, N_REP)
    three = P(None, None, N_REP)
    weights = (two, two, three, three, two, three, two, two)
    placed = (
        P(N_REP, N_REGION, None),
        P(N_REP, None, N_REGION, None),
        P(),
        P(),
        P(),
        P(N_REGION, None),
        P(N_REGION),
        P(N_REGION),
        P(N_REGION),
        P(N_REGION),
        P(N_REGION, None, None),
        P(N_REGION),
        P(N_REGION),
        P(),
    ) + tuple(spec for spec in weights for _ in range(3))
    return jax.shard_map(
        body,
        mesh=mesh,
        in_specs=placed,
        out_specs=(P(), P(), P())
        + tuple(spec for spec in weights for _ in range(3))
        + (P(N_REP, None),),
        check_vma=False,
    )
```

```python
import jax
import jax.numpy as jnp
from jax import lax
from jax.experimental import pallas as pl
from jax.experimental.pallas import tpu as pltpu
from jax.sharding import PartitionSpec as P

LAYERS = 3
STEPS = 2
STEP_COUNT = 10
NODE_CAP = 512
D = 512
BLOCK = 128
BLOCKS = D // BLOCK
TILE = 512
CODED = 32
CODE_TOP = 32000.0

norm_eps = 1e-05
beta_first = 0.9
beta_second = 0.95
adam_eps = 1e-08
decay_weight = 0.1
learn_rate = 0.05
clip_limit = 0.02

N_ACT = "act"
N_AREA = "area"
N_ASSIGN = "assign"
N_B = "b"
N_BEFORE = "before"
N_D_EDGES = "d_edges"
N_D_FIRST = "d_first"
N_D_GRID = "d_grid"
N_D_HALO = "d_halo"
N_D_HIDDEN = "d_hidden"
N_D_MIXED = "d_mixed"
N_D_NEXT = "d_next"
N_D_NODES = "d_nodes"
N_D_SECOND = "d_second"
N_D_STATE = "d_state"
N_DEC = "dec"
N_DELTA = "delta"
N_EDGE_FIRST = "edge_first"
N_EDGE_INNER = "edge_inner"
N_EDGES = "edges"
N_EDGES_LOW = "edges_low"
N_EMBED_GRADS = "embed_grads"
N_ENC = "enc"
N_FEATS = "feats"
N_FINAL = "final"
N_FIRST = "first"
N_FROM_RECV = "from_recv"
N_FROM_SEND = "from_send"
N_GEOMETRY = "geometry"
N_GRADS = "grads"
N_H = "h"
N_HALO = "halo"
N_HALO_HIGH = "halo_high"
N_HALO_REST = "halo_rest"
N_HEAD = "head"
N_HIDDEN = "hidden"
N_INNER = "inner"
N_INVERSE = "inverse"
N_LATENT = "latent"
N_LOCAL = "local"
N_LOW = "low"
N_MISS = "miss"
N_NODE_ACT = "node_act"
N_NODE_D_HIDDEN = "node_d_hidden"
N_NODE_D_MIXED = "node_d_mixed"
N_NODE_FIRST = "node_first"
N_NODE_HIDDEN = "node_hidden"
N_NODE_INNER = "node_inner"
N_NODE_INVERSE = "node_inverse"
N_NODE_LOW = "node_low"
N_NODE_NORMED = "node_normed"
N_NODES = "nodes"
N_NORMED = "normed"
N_OUTGOING = "outgoing"
N_PICKS = "picks"
N_PICKS_ROW = "picks_row"
N_PLAN = "plan"
N_RECV = "recv"
N_RECV_ROW = "recv_row"
N_REGION = "region"
N_REP = "rep"
N_RETURNED = "returned"
N_S = "s"
N_SCALES = "scales"
N_SEND = "send"
N_SEND_ROW = "send_row"
N_STATE = "state"
N_SUMS = "sums"
N_SUMS_ = "sums_"
N_TARGET = "target"
N_TOTAL = "total"
N_V = "v"
N_VECTORS = "vectors"
N_W = "w"

f32 = jnp.float32
bf16 = jnp.bfloat16


def up_to(rows, unit):
    return (rows + unit - 1) // unit * unit


class Env:
    pass


def cost_of(micros):
    return pl.CostEstimate(flops=int(micros * 1.15e9), bytes_accessed=0, transcendentals=0)


def launch(body, ins, outs, scratch=(), micros=0, swap=None, after=()):
    in_specs, operands, scratch_shapes, names = [], [], [], []
    loads = {}
    total_sems = 0
    positions = {}
    place = swap[0] if swap is not None else None
    for item in ins:
        name, array, kind = item[:3]
        positions[name] = len(operands)
        if kind == N_W:
            if len(array) > 2:
                place = array[0]
            operands += array[1:]
        else:
            operands.append(array)
        if kind == N_S:
            in_specs.append(pl.BlockSpec(memory_space=pltpu.SMEM))
        elif kind in (N_H, N_V):
            index, parts = item[3] if kind == N_H else ((), 1)
            in_specs.append(pl.BlockSpec(memory_space=pl.ANY))
            shape = array.shape[len(index) :]
            loads[name] = (N_H, index, parts, shape, total_sems)
            total_sems += parts
            names.append(name)
            scratch_shapes.append(pltpu.VMEM(shape, array.dtype))
        else:
            first, rows = item[3]
            in_specs += [pl.BlockSpec(memory_space=pl.ANY)] * (len(array) - 1)
            whole = len(array) == 2
            loads[name] = (N_W, first, rows, whole, total_sems)
            total_sems += BLOCKS
            names.append(name)
            scratch_shapes.append(pltpu.VMEM((rows, D), bf16))
    out_specs, out_shape = [], []
    flushes = {}
    out_sems = 0
    for name, shape, dtype, kind, parts in outs:
        out_shape.append(jax.ShapeDtypeStruct(shape, dtype))
        if kind == N_B:
            out_specs.append(pl.BlockSpec(memory_space=pltpu.VMEM))
        else:
            out_specs.append(pl.BlockSpec(memory_space=pl.ANY))
            flushes[name] = (parts, shape, out_sems)
            out_sems += parts
            if name not in names:
                names.append(name)
                scratch_shapes.append(pltpu.VMEM(shape, dtype))
    if swap is not None:
        for _ in range(BLOCKS):
            out_shape.append(jax.ShapeDtypeStruct((swap[1], BLOCK), f32))
            out_specs.append(pl.BlockSpec(memory_space=pl.ANY))
    place_at = len(operands)
    if place is not None:
        operands.append(place)
        in_specs.append(pl.BlockSpec(memory_space=pltpu.SMEM))
    for array in after:
        operands.append(array)
        in_specs.append(pl.BlockSpec(memory_space=pl.ANY))
    for name, shape, dtype in scratch:
        names.append(name)
        scratch_shapes.append(pltpu.VMEM(shape, dtype))
    scratch_shapes.append(pltpu.SemaphoreType.DMA((max(total_sems, 1),)))
    scratch_shapes.append(pltpu.SemaphoreType.DMA((max(out_sems, 1),)))
    if swap is not None:
        scratch_shapes.append(pltpu.SemaphoreType.DMA((BLOCKS,)))

    def kernel(*refs):
        k = Env()
        out_refs = refs[len(operands) : len(operands) + len(out_shape)]
        rest = refs[len(operands) + len(out_shape) :]
        for name, ref in zip(names, rest):
            setattr(k, name, ref)
        sem_in, sem_out = rest[len(names) : len(names) + 2]
        sources, targets = {}, {}
        for item in ins:
            if item[2] == N_S:
                setattr(k, item[0], refs[positions[item[0]]])
            else:
                sources[item[0]] = positions[item[0]]
        for item, ref in zip(outs, out_refs):
            if item[3] == N_B:
                setattr(k, item[0], ref)
            else:
                targets[item[0]] = ref

        def load(name, part):
            kind, first, parts, shape, base = loads[name]
            src, dst = refs[sources[name]], getattr(k, name)
            if kind == N_H:
                for i in first:
                    src = src.at[i]
                if parts > 1:
                    step = shape[0] // parts
                    rows = pl.ds(pl.multiple_of(part * step, step), step)
                    src, dst = src.at[rows], dst.at[rows]
            else:
                if shape:
                    src = src.at[part, pl.ds(first, parts)]
                    column = part * BLOCK
                else:
                    src = refs[sources[name] + part].at[pl.ds(first, parts)]
                    column = lax.bitwise_xor(refs[place_at][0], part) * BLOCK
                    column = pl.multiple_of(column, BLOCK)
                dst = dst.at[:, pl.ds(column, BLOCK)]
            return pltpu.make_async_copy(src, dst, sem_in.at[base + part])

        def send(name, part):
            parts, shape, base = flushes[name]
            src, dst = getattr(k, name), targets[name]
            if parts > 1:
                step = shape[0] // parts
                rows = pl.ds(pl.multiple_of(part * step, step), step)
                src, dst = src.at[rows], dst.at[rows]
            return pltpu.make_async_copy(src, dst, sem_out.at[base + part])

        def wait(name, part=None):
            if name not in loads:
                return
            if part is not None:
                load(name, part).wait()
                return
            count = BLOCKS if loads[name][0] == N_W else loads[name][2]
            for i in range(count):
                load(name, i).wait()

        def flush(name, part=None):
            if part is not None:
                send(name, part).start()
                return
            for i in range(flushes[name][0]):
                send(name, i).start()

        def swap_copy(other):
            source = k.grads.at[lax.bitwise_xor(refs[place_at][0], other)]
            return pltpu.make_async_copy(source, out_refs[len(outs) + other], rest[-1].at[other])

        def flush_swap():
            for other in range(BLOCKS):
                swap_copy(other).start()

        k.wait, k.flush, k.flush_swap = wait, flush, flush_swap
        for item in sorted(ins, key=lambda item: item[2] != N_V):
            if item[0] in loads:
                count = BLOCKS if item[2] == N_W else loads[item[0]][2]
                for i in range(count):
                    load(item[0], i).start()
        for item in ins:
            if item[2] == N_V:
                wait(item[0])
        body(k)
        for item in outs:
            if item[3] == N_V:
                flush(item[0])
        for name in flushes:
            for i in range(flushes[name][0]):
                send(name, i).wait()
        if swap is not None:
            for other in range(BLOCKS):
                swap_copy(other).wait()

    return pl.pallas_call(
        kernel,
        out_shape=out_shape,
        in_specs=in_specs,
        out_specs=out_specs,
        scratch_shapes=scratch_shapes,
        compiler_params=pltpu.CompilerParams(
            vmem_limit_bytes=56 * 2**20
        ),
        cost_estimate=cost_of(micros),
    )(*operands)


def dense(left, right):
    return jnp.dot(left, right, preferred_element_type=f32)


def dense_left(left, right):
    return lax.dot_general(left, right, (((0,), (0,)), ((), ())), preferred_element_type=f32)


def dense_right(left, right):
    return lax.dot_general(left, right, (((1,), (1,)), ((), ())), preferred_element_type=f32)


def halves(value):
    high = value.astype(bf16)
    return high, (value - high.astype(f32)).astype(bf16)


def rows_hot(column, width):
    spots = lax.broadcasted_iota(jnp.int32, (column.shape[0], width), 1)
    return jnp.where(column == spots, 1.0, 0.0).astype(bf16)


def cols_hot(row, height, first=0):
    spots = lax.broadcasted_iota(jnp.int32, (height, row.shape[1]), 0) + first
    return jnp.where(row == spots, 1.0, 0.0).astype(bf16)


def sigmoid(value):
    return 0.5 * jnp.tanh(0.5 * value) + 0.5


def normalise(mixed):
    centred = mixed - jnp.mean(mixed, -1, keepdims=True)
    inverse = lax.rsqrt(jnp.mean(centred * centred, -1, keepdims=True) + norm_eps)
    return centred * inverse, inverse


def vec(k, block, row):
    at = 3 * block + row
    return k.vectors[at : at + 1, :]


def row_tile(t, size):
    return pl.ds(pl.multiple_of(t * size, size), size)


def loop(count, step, most=1):
    unroll = max(n for n in range(1, most + 1) if count % n == 0)
    lax.fori_loop(0, count, lambda t, carry: (step(t), carry)[1], 0, unroll=unroll)


def forward_rows(k, block, hidden, inner):
    act = (hidden * sigmoid(hidden)).astype(bf16)
    normed, inverse = normalise(dense(act, inner))
    return normed * vec(k, block, 1) + vec(k, block, 2), normed, inverse


def backward_rows(k, block, upstream, hidden, normed, inverse, inner, sums, at):
    sums[at + 1 : at + 2, :] += jnp.sum(upstream * normed, 0, keepdims=True)
    sums[at + 2 : at + 3, :] += jnp.sum(upstream, 0, keepdims=True)
    scaled = upstream * vec(k, block, 1)
    d_mixed = inverse * (
        scaled
        - jnp.mean(scaled, -1, keepdims=True)
        - normed * jnp.mean(scaled * normed, -1, keepdims=True)
    )
    d_mixed = d_mixed.astype(bf16)
    sigma = sigmoid(hidden)
    act = (hidden * sigma).astype(bf16)
    d_act = dense_right(d_mixed, inner)
    d_hidden = (d_act * (sigma * (1.0 + hidden * (1.0 - sigma)))).astype(bf16)
    sums[at : at + 1, :] += jnp.sum(d_hidden.astype(f32), 0, keepdims=True)
    return act, d_mixed, d_hidden


def add_grad(k, first, value):
    rows = value.shape[0]
    for c in range(BLOCKS):
        k.grads[c, first : first + rows, :] += value[:, c * BLOCK : (c + 1) * BLOCK]


def set_grad(k, first, value):
    rows = value.shape[0]
    for c in range(BLOCKS):
        k.grads[c, first : first + rows, :] = value[:, c * BLOCK : (c + 1) * BLOCK]


def put_grad(k, fresh, first, value):
    (set_grad if fresh else add_grad)(k, first, value)


def weight_grad(k, fresh, first, left, right, pieces=2):
    width = left.shape[1]
    step = width // pieces
    for i in range(pieces):
        part = dense_left(left[:, i * step : (i + 1) * step], right[...])
        put_grad(k, fresh, first + i * step, part)


def start_sums(k, fresh):
    if fresh:
        k.sums[...] = jnp.zeros(k.sums.shape, f32)
    else:
        k.wait(N_SUMS)


def embed_forward(geometry, first, inner, at_inner, vectors):
    edges = geometry.shape[1]

    def body(k):
        k.wait(N_FIRST)
        k.wait(N_INNER)

        def tile(t):
            rows = row_tile(t, TILE)
            hidden = dense_left(k.geometry[:, rows], k.first[...]) + vec(k, 1, 0)
            k.hidden[rows] = hidden
            out, normed, inverse = forward_rows(k, 1, hidden, k.inner[...])
            k.normed[rows] = normed
            k.inverse[rows] = inverse
            k.edges[rows] = out
            k.edges_low[rows] = out.astype(bf16)
            for name in (N_HIDDEN, N_NORMED, N_INVERSE, N_EDGES, N_EDGES_LOW):
                k.flush(name, t)

        loop(edges // TILE, tile)

    parts = edges // TILE
    return launch(
        body,
        [
            (N_GEOMETRY, geometry, N_V),
            (N_VECTORS, vectors, N_V),
            (N_FIRST,) + first,
            (N_INNER,) + inner,
        ],
        [
            (N_EDGES, (edges, D), f32, N_H, parts),
            (N_EDGES_LOW, (edges, D), bf16, N_H, parts),
            (N_HIDDEN, (edges, D), f32, N_H, parts),
            (N_NORMED, (edges, D), f32, N_H, parts),
            (N_INVERSE, (edges, 1), f32, N_H, parts),
        ],
        micros=5,
    )


def encoder_forward(state, means, scales, first, inner, vectors, assign, picks):
    depth, grid = state.shape
    out_rows = picks.shape[0]

    def body(k):
        k.wait(N_STATE)
        k.feats[...] = ((k.state[...] - k.means[...]) / k.scales[...]).astype(bf16)
        k.flush(N_FEATS)
        k.wait(N_FIRST)
        k.wait(N_INNER)

        def tile(t):
            rows = row_tile(t, TILE)
            hidden = dense_left(k.feats[:, rows], k.first[...]) + vec(k, 0, 0)
            k.hidden[rows] = hidden
            out, normed, inverse = forward_rows(k, 0, hidden, k.inner[...])
            k.normed[rows] = normed
            k.inverse[rows] = inverse
            k.latent[rows] = out
            k.low[rows] = out.astype(bf16)
            for name in (N_HIDDEN, N_NORMED, N_INVERSE, N_LATENT, N_LOW):
                k.flush(name, t)

        loop(grid // TILE, tile)
        nodes = dense(cols_hot(k.assign[...], NODE_CAP), k.low[...])
        k.nodes[...] = nodes
        k.node_low[...] = nodes.astype(bf16)
        k.outgoing[...] = dense(rows_hot(k.picks[...], NODE_CAP), k.node_low[...]).astype(bf16)

    parts = grid // TILE
    return launch(
        body,
        [
            (N_STATE, state, N_H, ((), 1)),
            ("means", means, N_V),
            (N_SCALES, scales, N_V),
            (N_ASSIGN, assign, N_V),
            (N_PICKS, picks, N_V),
            (N_VECTORS, vectors, N_V),
            (N_FIRST,) + first,
            (N_INNER,) + inner,
        ],
        [
            (N_NODES, (NODE_CAP, D), f32, N_V, 1),
            (N_NODE_LOW, (NODE_CAP, D), bf16, N_V, 1),
            (N_OUTGOING, (out_rows, D), bf16, N_V, 1),
            (N_LATENT, (grid, D), f32, N_H, parts),
            (N_LOW, (grid, D), bf16, N_H, parts),
            (N_FEATS, (depth, grid), bf16, N_H, 1),
            (N_HIDDEN, (grid, D), f32, N_H, parts),
            (N_NORMED, (grid, D), f32, N_H, parts),
            (N_INVERSE, (grid, 1), f32, N_H, parts),
        ],
        micros=5,
    )


def layer_local(layer, edges_low, node_low, edge_first, vectors, send, recv):
    count = edges_low.shape[0]
    at = 2 + layer

    def body(k):
        k.wait(N_EDGE_FIRST)

        def tile(t):
            rows = row_tile(t, TILE)
            sent = dense(rows_hot(k.send[rows], NODE_CAP), k.node_low[...]).astype(bf16)
            got = dense(rows_hot(k.recv[rows], NODE_CAP), k.node_low[...]).astype(bf16)
            k.wait(N_EDGES_LOW, t)
            joined = jnp.concatenate([k.edges_low[rows], sent, got], 1)
            k.local[rows] = dense(joined, k.edge_first[...]) + vec(k, at, 0)
            k.flush(N_LOCAL, t)

        loop(count // TILE, tile)

    parts = count // TILE
    return launch(
        body,
        [
            (N_NODE_LOW, node_low, N_V),
            (N_SEND, send, N_V),
            (N_RECV, recv, N_V),
            (N_VECTORS, vectors, N_V),
            (N_EDGE_FIRST,) + edge_first,
            (N_EDGES_LOW, edges_low, N_H, ((), parts)),
        ],
        [(N_LOCAL, (count, D), f32, N_H, parts)],
        micros=8,
    )[0]


def layer_forward(
    layer, local, edges, nodes, node_low, halo, weights, vectors, send, recv_row, picks, last
):
    count = edges.shape[0]
    halo_rows = halo.shape[0]
    from_send, edge_inner, node_first, node_inner = weights
    at_edge, at_node = 2 + layer, 2 + LAYERS + layer

    def body(k):
        k.wait(N_FROM_SEND)
        high, rest = halves(dense(k.halo[...], k.from_send[...]))
        k.table[:, 0:D] = high
        k.table[:, D : 2 * D] = rest
        k.wait(N_EDGE_INNER)

        def tile(t):
            rows = row_tile(t, TILE)
            both = dense(rows_hot(k.send[rows] - NODE_CAP, halo_rows), k.table[...])
            k.wait(N_HIDDEN, t)
            hidden = k.hidden[rows] + (both[:, 0:D] + both[:, D : 2 * D])
            k.hidden[rows] = hidden
            out, normed, inverse = forward_rows(k, at_edge, hidden, k.edge_inner[...])
            k.normed[rows] = normed
            k.inverse[rows] = inverse
            k.wait(N_EDGES, t)
            edge = k.edges[rows] + out
            k.edges[rows] = edge
            high, rest = halves(edge)
            k.edges_low[rows] = high
            k.rest[rows] = rest
            for name in (N_HIDDEN, N_NORMED, N_INVERSE):
                k.flush(name, t)
            if not last:
                k.flush(N_EDGES, t)
                k.flush(N_EDGES_LOW, t)

        loop(count // TILE, tile)
        k.wait(N_NODE_FIRST)
        k.wait(N_NODE_INNER)
        k.wait(N_NODES)

        def node_tile(t):
            rows = row_tile(t, TILE)
            hot = cols_hot(k.recv_row[...], TILE, t * TILE)
            total = (dense(hot, k.edges_low[...]) + dense(hot, k.rest[...])).astype(bf16)
            k.total[rows] = total
            node_in = jnp.concatenate([k.node_low[rows], total], 1)
            hidden = dense(node_in, k.node_first[...]) + vec(k, at_node, 0)
            k.node_hidden[rows] = hidden
            out, normed, inverse = forward_rows(k, at_node, hidden, k.node_inner[...])
            k.node_normed[rows] = normed
            k.node_inverse[rows] = inverse
            node = k.nodes[rows] + out
            k.nodes[rows] = node
            k.new_low[rows] = node.astype(bf16)
            for name in (N_TOTAL, N_NODE_HIDDEN, N_NODE_NORMED, N_NODE_INVERSE):
                k.flush(name, t)
            if not last:
                k.flush(N_NODES, t)

        loop(NODE_CAP // TILE, node_tile)
        if not last:
            k.outgoing[...] = dense(rows_hot(k.picks[...], NODE_CAP), k.new_low[...]).astype(bf16)

    parts = count // TILE
    node_parts = NODE_CAP // TILE
    ins = [
        (N_NODE_LOW, node_low, N_V),
        (N_HALO, halo, N_V),
        (N_SEND, send, N_V),
        (N_RECV_ROW, recv_row, N_V),
        (N_VECTORS, vectors, N_V),
        (N_FROM_SEND,) + from_send,
        (N_EDGE_INNER,) + edge_inner,
        (N_HIDDEN, local, N_H, ((), parts)),
        (N_EDGES, edges, N_H, ((), parts)),
        (N_NODE_FIRST,) + node_first,
        (N_NODE_INNER,) + node_inner,
        (N_NODES, nodes, N_H, ((), 1)),
    ]
    outs = [
        ("new_low", (NODE_CAP, D), bf16, N_V, 1),
        (N_HIDDEN, (count, D), f32, N_H, parts),
        (N_NORMED, (count, D), f32, N_H, parts),
        (N_INVERSE, (count, 1), f32, N_H, parts),
        (N_TOTAL, (NODE_CAP, D), bf16, N_H, node_parts),
        (N_NODE_HIDDEN, (NODE_CAP, D), f32, N_H, node_parts),
        (N_NODE_NORMED, (NODE_CAP, D), f32, N_H, node_parts),
        (N_NODE_INVERSE, (NODE_CAP, 1), f32, N_H, node_parts),
    ]
    scratch = [("table", (halo_rows, 2 * D), bf16), ("rest", (count, D), bf16)]
    if last:
        scratch.append((N_EDGES_LOW, (count, D), bf16))
    else:
        ins.append((N_PICKS, picks, N_V))
        outs += [
            (N_EDGES, (count, D), f32, N_H, parts),
            (N_NODES, (NODE_CAP, D), f32, N_H, node_parts),
            (N_OUTGOING, (halo_rows, D), bf16, N_V, 1),
            (N_EDGES_LOW, (count, D), bf16, N_H, parts),
        ]
    out = launch(body, ins, outs, scratch, micros=13)
    kept = {
        N_NODE_LOW: node_low,
        N_HALO: halo,
        N_HIDDEN: out[1],
        N_NORMED: out[2],
        N_INVERSE: out[3],
        N_TOTAL: out[4],
        N_NODE_HIDDEN: out[5],
        N_NODE_NORMED: out[6],
        N_NODE_INVERSE: out[7],
    }
    if last:
        return None, None, None, out[0], None, kept
    return out[8], out[11], out[9], out[0], out[10], kept


def decoder_forward(
    step, state, target, latent, low, node_low, weights, vectors, assign, delta, area, plan
):
    depth, grid = state.shape
    first, inner, head = weights
    at = 2 + 2 * LAYERS

    def body(k):
        k.wait(N_FIRST)
        k.wait(N_INNER)

        def tile(t):
            rows = row_tile(t, TILE)
            k.wait(N_LOW, t)
            got = dense(rows_hot(k.assign[rows], NODE_CAP), k.node_low[...]).astype(bf16)
            joined = jnp.concatenate([k.low[rows], got], 1)
            hidden = dense(joined, k.first[...]) + vec(k, at, 0)
            k.hidden[rows] = hidden
            out, normed, inverse = forward_rows(k, at, hidden, k.inner[...])
            k.normed[rows] = normed
            k.inverse[rows] = inverse
            k.wait(N_LATENT, t)
            k.final[rows] = (k.latent[rows] + out).astype(bf16)
            for name in (N_HIDDEN, N_NORMED, N_INVERSE, N_FINAL):
                k.flush(name, t)

        loop(grid // TILE, tile)
        k.wait(N_HEAD)
        k.wait(N_STATE)
        k.wait(N_TARGET)
        update = dense_right(k.head[...], k.final[...])
        new_state = k.state[...] + k.delta[...] * update
        k.new_state[...] = new_state
        miss = (new_state - k.target[...]) / k.delta[...]
        k.miss[...] = miss
        weight = k.plan[step].astype(f32)
        k.loss[...] = weight * jnp.sum(k.area[...] * miss * miss, keepdims=True)

    parts = grid // TILE
    out = launch(
        body,
        [
            (N_NODE_LOW, node_low, N_V),
            (N_ASSIGN, assign, N_V),
            (N_VECTORS, vectors, N_V),
            (N_DELTA, delta, N_V),
            (N_AREA, area, N_V),
            (N_PLAN, plan, N_S),
            (N_FIRST,) + first,
            (N_LOW, low, N_H, ((), parts)),
            (N_INNER,) + inner,
            (N_LATENT, latent, N_H, ((), parts)),
            (N_HEAD,) + head,
            (N_STATE, state, N_H, ((), 1)),
            (N_TARGET, target, N_H, ((step,), 1)),
        ],
        [
            ("new_state", (depth, grid), f32, N_V, 1),
            (N_MISS, (depth, grid), f32, N_V, 1),
            ("loss", (1, 1), f32, N_B, 1),
            (N_HIDDEN, (grid, D), f32, N_H, parts),
            (N_NORMED, (grid, D), f32, N_H, parts),
            (N_INVERSE, (grid, 1), f32, N_H, parts),
            (N_FINAL, (grid, D), bf16, N_H, parts),
        ],
        micros=7,
    )
    kept = {
        N_MISS: out[1],
        N_HIDDEN: out[3],
        N_NORMED: out[4],
        N_INVERSE: out[5],
        N_FINAL: out[6],
        N_LOW: low,
        N_NODE_LOW: node_low,
    }
    return out[0], out[2], kept


def grads_io(outs, scratch, grads, rows, swap):
    shape = (BLOCKS, rows, BLOCK)
    if swap is None:
        outs.append((N_GRADS, shape, f32, N_H, BLOCKS))
    elif grads is None:
        scratch.append((N_GRADS, shape, f32))


def flush_grads(k, swap):
    if swap is None:
        k.flush(N_GRADS)
    else:
        k.flush_swap()


def decoder_backward(
    step, regions, d_state, kept, weights, vectors, assign_row, delta, area, plan, inverse_total, grads, sums,
    swap,
):
    miss = kept[N_MISS]
    depth, grid = miss.shape
    first, inner, head = weights
    at = 2 + 2 * LAYERS
    fresh = grads is None
    more = d_state is not None
    keep_state = step > 0
    rows_all = up_to(3 * D + depth, CODED * regions)

    def body(k):
        k.wait(N_MISS)
        coefficient = 2.0 * k.inverse_total[0, 0] * k.plan[step].astype(f32)
        d_next = coefficient * k.area[...] * k.miss[...] / k.delta[...]
        if more:
            k.wait(N_D_STATE)
            d_next = k.d_state[...] + d_next
        if keep_state:
            k.d_next[...] = d_next
            k.flush(N_D_NEXT)
        k.d_update[...] = (d_next * k.delta[...]).astype(bf16)
        start_sums(k, fresh)
        k.wait(N_HEAD)
        k.wait(N_INNER)
        k.wait(N_FIRST)

        def tile(t):
            rows = row_tile(t, TILE)
            for name in (N_HIDDEN, N_NORMED, N_INVERSE):
                k.wait(name, t)
            d_final = dense_left(k.d_update[:, rows], k.head[...])
            act, d_mixed, d_hidden = backward_rows(
                k, at, d_final, k.hidden[rows], k.normed[rows], k.inverse[rows],
                k.inner[...], k.sums, 0,
            )
            k.act[rows] = act
            k.d_mixed[rows] = d_mixed
            k.d_hidden[rows] = d_hidden
            k.d_grid[rows] = d_final + dense_right(d_hidden, k.first[0:D])
            k.flush(N_D_GRID, t)

        loop(grid // TILE, tile)
        k.flush(N_SUMS)
        gathered = dense(cols_hot(k.assign_row[...], NODE_CAP), k.d_hidden[...])
        high, rest = halves(gathered)
        k.d_nodes[...] = dense_right(high, k.first[D : 2 * D]) + dense_right(rest, k.first[D : 2 * D])
        if not fresh:
            k.wait(N_GRADS)
        k.wait(N_LOW)
        k.wait(N_FINAL)
        weight_grad(k, fresh, 0, k.low, k.d_hidden)
        put_grad(k, fresh, D, dense_left(k.node_low[...], high) + dense_left(k.node_low[...], rest))
        weight_grad(k, fresh, 2 * D, k.act, k.d_mixed)
        put_grad(k, fresh, 3 * D, dense(k.d_update[...], k.final[...]))
        if fresh and rows_all > 3 * D + depth:
            k.grads[:, 3 * D + depth :, :] = jnp.zeros(
                (BLOCKS, rows_all - 3 * D - depth, BLOCK), f32
            )
        flush_grads(k, swap)

    parts = grid // TILE
    ins = [
        (N_MISS, miss, N_H, ((), 1)),
        (N_AREA, area, N_V),
        (N_DELTA, delta, N_V),
        ("assign_row", assign_row, N_V),
        (N_VECTORS, vectors, N_V),
        (N_NODE_LOW, kept[N_NODE_LOW], N_V),
        (N_PLAN, plan, N_S),
        ("inverse_total", inverse_total, N_S),
    ]
    if more:
        ins.append((N_D_STATE, d_state, N_H, ((), 1)))
    ins += [
        (N_HEAD,) + head,
        (N_HIDDEN, kept[N_HIDDEN], N_H, ((), parts)),
        (N_NORMED, kept[N_NORMED], N_H, ((), parts)),
        (N_INVERSE, kept[N_INVERSE], N_H, ((), parts)),
        (N_INNER,) + inner,
        (N_FIRST,) + first,
        (N_LOW, kept[N_LOW], N_H, ((), 1)),
        (N_FINAL, kept[N_FINAL], N_H, ((), 1)),
    ]
    outs = [
        (N_D_NODES, (NODE_CAP, D), f32, N_V, 1),
        (N_D_GRID, (grid, D), f32, N_H, parts),
    ]
    if keep_state:
        outs.append((N_D_NEXT, (depth, grid), f32, N_H, 1))
    scratch = [
        ("d_update", (depth, grid), bf16),
        (N_ACT, (grid, D), bf16),
        (N_D_MIXED, (grid, D), bf16),
        (N_D_HIDDEN, (grid, D), bf16),
    ]
    if not fresh:
        ins += [(N_SUMS, sums, N_H, ((), 1)), (N_GRADS, grads, N_H, ((), BLOCKS))]
    outs.append((N_SUMS, (8, D), f32, N_H, 1))
    grads_io(outs, scratch, grads, rows_all, swap)
    out = launch(
        body, ins, outs, scratch, micros=13, swap=swap
    )
    if keep_state:
        return out[0], out[1], out[2], out[3], out[4:]
    return out[0], out[1], None, out[2], out[3:]


def layer_backward(
    layer, d_nodes, returned, d_edges, kept, weights, vectors, send_row, recv, picks_row,
    sums, after,
):
    count = kept[N_HIDDEN].shape[0]
    halo_rows = kept[N_HALO].shape[0]
    edge_first, edge_inner, node_first, node_inner = weights
    at_edge, at_node = 2 + layer, 2 + LAYERS + layer
    top = d_edges is None

    def body(k):
        start_sums(k, sums is None)
        k.wait(N_D_NODES)
        if not top:
            high, rest = halves(k.returned[...])
            hot = cols_hot(k.picks_row[...], NODE_CAP)
            k.d_nodes[...] += dense(hot, high) + dense(hot, rest)
        for name in (N_NODE_HIDDEN, N_NODE_NORMED, N_NODE_INVERSE, N_NODE_INNER, N_NODE_FIRST):
            k.wait(name)

        def node_tile(t):
            rows = row_tile(t, TILE)
            act, d_mixed, d_hidden = backward_rows(
                k, at_node, k.d_nodes[rows], k.node_hidden[rows], k.node_normed[rows],
                k.node_inverse[rows], k.node_inner[...], k.sums, 3,
            )
            k.node_act[rows] = act
            k.node_d_mixed[rows] = d_mixed
            k.node_d_hidden[rows] = d_hidden
            d_in = dense_right(d_hidden, k.node_first[...])
            k.d_nodes[rows] += d_in[:, 0:D]
            high, rest = halves(d_in[:, D : 2 * D])
            k.d_total[rows, 0:D] = high
            k.d_total[rows, D : 2 * D] = rest

        loop(NODE_CAP // TILE, node_tile)
        for name in (N_D_NODES, N_NODE_ACT, N_NODE_D_MIXED, N_NODE_D_HIDDEN):
            k.flush(name)
        k.wait(N_EDGE_INNER)
        k.wait(N_EDGE_FIRST)

        def tile(t):
            rows = row_tile(t, TILE)
            both = dense(rows_hot(k.recv[rows], NODE_CAP), k.d_total[...])
            upstream = both[:, 0:D] + both[:, D : 2 * D]
            if not top:
                k.wait(N_D_EDGES, t)
                upstream = k.d_edges[rows] + upstream
            for name in (N_HIDDEN, N_NORMED, N_INVERSE):
                k.wait(name, t)
            act, d_mixed, d_hidden = backward_rows(
                k, at_edge, upstream, k.hidden[rows], k.normed[rows], k.inverse[rows],
                k.edge_inner[...], k.sums, 0,
            )
            k.act[rows] = act
            k.d_mixed[rows] = d_mixed
            k.d_hidden[rows] = d_hidden
            k.d_edges[rows] = upstream + dense_right(d_hidden, k.edge_first[0:D])
            for name in (N_ACT, N_D_MIXED, N_D_HIDDEN, N_D_EDGES):
                k.flush(name, t)

        loop(count // TILE, tile)
        k.flush(N_SUMS)
        to_halo = dense(cols_hot(k.send_row[...], halo_rows, NODE_CAP), k.d_hidden[...])
        high, rest = halves(to_halo)
        from_send = k.edge_first[D : 2 * D]
        k.d_halo[...] = dense_right(high, from_send) + dense_right(rest, from_send)
        k.halo_high[...] = high
        k.halo_rest[...] = rest

    parts = count // TILE
    ins = [
        (N_RECV, recv, N_V),
        (N_SEND_ROW, send_row, N_V),
        (N_VECTORS, vectors, N_V),
    ]
    if not top:
        ins += [(N_RETURNED, returned, N_V), (N_PICKS_ROW, picks_row, N_V)]
    ins += [
        (N_D_NODES, d_nodes, N_H, ((), 1)),
        (N_NODE_HIDDEN, kept[N_NODE_HIDDEN], N_H, ((), 1)),
        (N_NODE_NORMED, kept[N_NODE_NORMED], N_H, ((), 1)),
        (N_NODE_INVERSE, kept[N_NODE_INVERSE], N_H, ((), 1)),
        (N_NODE_INNER,) + node_inner,
        (N_NODE_FIRST,) + node_first,
        (N_EDGE_INNER,) + edge_inner,
        (N_EDGE_FIRST,) + edge_first,
    ]
    if sums is not None:
        ins.append((N_SUMS, sums, N_H, ((), 1)))
    if not top:
        ins.append((N_D_EDGES, d_edges, N_H, ((), parts)))
    ins += [
        (N_HIDDEN, kept[N_HIDDEN], N_H, ((), parts)),
        (N_NORMED, kept[N_NORMED], N_H, ((), parts)),
        (N_INVERSE, kept[N_INVERSE], N_H, ((), parts)),
    ]
    outs = [
        (N_D_HALO, (halo_rows, D), f32, N_V, 1),
        (N_HALO_HIGH, (halo_rows, D), bf16, N_V, 1),
        (N_HALO_REST, (halo_rows, D), bf16, N_V, 1),
        (N_D_NODES, (NODE_CAP, D), f32, N_H, 1),
        (N_NODE_ACT, (NODE_CAP, D), bf16, N_H, 1),
        (N_NODE_D_MIXED, (NODE_CAP, D), bf16, N_H, 1),
        (N_NODE_D_HIDDEN, (NODE_CAP, D), bf16, N_H, 1),
        (N_ACT, (count, D), bf16, N_H, parts),
        (N_D_MIXED, (count, D), bf16, N_H, parts),
        (N_D_HIDDEN, (count, D), bf16, N_H, parts),
        (N_D_EDGES, (count, D), f32, N_H, parts),
        (N_SUMS, (8, D), f32, N_H, 1),
    ]
    scratch = [("d_total", (NODE_CAP, 2 * D), bf16)]
    out = launch(body, ins, outs, scratch, micros=14, after=after)
    names = [item[0] for item in outs]
    return dict(zip(names, out))


def layer_grads(found, kept, edge_first, send_row, recv_row, rows_all, grads, swap, after):
    count = kept[N_HIDDEN].shape[0]
    halo_rows = kept[N_HALO].shape[0]
    fresh = grads is None

    def body(k):
        k.wait(N_D_HIDDEN)
        k.wait(N_FROM_SEND)
        k.wait(N_FROM_RECV)
        to_recv = dense(cols_hot(k.recv_row[...], NODE_CAP), k.d_hidden[...])
        to_send = dense(cols_hot(k.send_row[...], NODE_CAP), k.d_hidden[...])
        recv_high, recv_rest = halves(to_recv)
        send_high, send_rest = halves(to_send)
        from_send, from_recv = k.from_send[...], k.from_recv[...]
        k.wait(N_D_NODES)
        k.d_nodes[...] += (
            dense_right(send_high, from_send)
            + dense_right(send_rest, from_send)
            + dense_right(recv_high, from_recv)
            + dense_right(recv_rest, from_recv)
        )
        k.flush(N_D_NODES)
        if not fresh:
            k.wait(N_GRADS)
        low = k.node_low[...]
        put_grad(
            k, fresh, D,
            dense_left(low, send_high)
            + dense_left(low, send_rest)
            + dense_left(k.halo[...], k.halo_high[...])
            + dense_left(k.halo[...], k.halo_rest[...]),
        )
        put_grad(k, fresh, 2 * D, dense_left(low, recv_high) + dense_left(low, recv_rest))
        k.wait(N_EDGES_LOW)
        weight_grad(k, fresh, 0, k.edges_low, k.d_hidden)
        k.wait(N_ACT)
        k.wait(N_D_MIXED)
        weight_grad(k, fresh, 3 * D, k.act, k.d_mixed)
        k.wait(N_TOTAL)
        k.wait(N_NODE_D_HIDDEN)
        weight_grad(k, fresh, 4 * D, k.node_low, k.node_d_hidden)
        weight_grad(k, fresh, 5 * D, k.total, k.node_d_hidden)
        k.wait(N_NODE_ACT)
        k.wait(N_NODE_D_MIXED)
        weight_grad(k, fresh, 6 * D, k.node_act, k.node_d_mixed)
        if fresh and rows_all > 7 * D:
            k.grads[:, 7 * D :, :] = jnp.zeros((BLOCKS, rows_all - 7 * D, BLOCK), f32)
        flush_grads(k, swap)

    source, _, (first, _) = edge_first
    ins = [
        (N_NODE_LOW, kept[N_NODE_LOW], N_V),
        (N_HALO, kept[N_HALO], N_V),
        (N_HALO_HIGH, found[N_HALO_HIGH], N_V),
        (N_HALO_REST, found[N_HALO_REST], N_V),
        (N_RECV_ROW, recv_row, N_V),
        (N_SEND_ROW, send_row, N_V),
        (N_D_HIDDEN, found[N_D_HIDDEN], N_H, ((), 1)),
        (N_FROM_SEND, source, N_W, (first + D, D)),
        (N_FROM_RECV, source, N_W, (first + 2 * D, D)),
        (N_D_NODES, found[N_D_NODES], N_H, ((), 1)),
    ]
    if not fresh:
        ins.append((N_GRADS, grads, N_H, ((), BLOCKS)))
    ins += [
        (N_EDGES_LOW, kept[N_EDGES_LOW], N_H, ((), 1)),
        (N_ACT, found[N_ACT], N_H, ((), 1)),
        (N_D_MIXED, found[N_D_MIXED], N_H, ((), 1)),
        (N_TOTAL, kept[N_TOTAL], N_H, ((), 1)),
        (N_NODE_D_HIDDEN, found[N_NODE_D_HIDDEN], N_H, ((), 1)),
        (N_NODE_ACT, found[N_NODE_ACT], N_H, ((), 1)),
        (N_NODE_D_MIXED, found[N_NODE_D_MIXED], N_H, ((), 1)),
    ]
    outs = [(N_D_NODES, (NODE_CAP, D), f32, N_H, 1)]
    scratch = []
    grads_io(outs, scratch, grads, rows_all, swap)
    out = launch(body, ins, outs, scratch, micros=14, swap=swap, after=after)
    return out[0], out[1:]


def encoder_backward(
    step, d_grid, d_nodes, returned, d_next, kept, weights, vectors, assign, picks_row, scales,
    grads, sums, others, swap, after,
):
    feats = kept[N_FEATS]
    depth, grid = feats.shape
    first, inner = weights
    fresh = grads is None
    keep_state = step > 0
    rows_all = depth + D
    if others is not None:
        embed_grads, all_sums = others
        embed_rows = embed_grads.shape[1]
        at_vectors = depth + D + embed_rows
        rows_all = swap[1]

    def body(k):
        start_sums(k, fresh)
        k.wait(N_D_NODES)
        high, rest = halves(k.returned[...])
        hot = cols_hot(k.picks_row[...], NODE_CAP)
        nodes = k.d_nodes[...] + dense(hot, high) + dense(hot, rest)
        high, rest = halves(nodes)
        k.both[:, 0:D] = high
        k.both[:, D : 2 * D] = rest
        k.wait(N_INNER)

        def tile(t):
            rows = row_tile(t, TILE)
            for name in (N_HIDDEN, N_NORMED, N_INVERSE, N_D_GRID):
                k.wait(name, t)
            both = dense(rows_hot(k.assign[rows], NODE_CAP), k.both[...])
            upstream = k.d_grid[rows] + both[:, 0:D] + both[:, D : 2 * D]
            act, d_mixed, d_hidden = backward_rows(
                k, 0, upstream, k.hidden[rows], k.normed[rows], k.inverse[rows],
                k.inner[...], k.sums, 0,
            )
            k.act[rows] = act
            k.d_mixed[rows] = d_mixed
            k.d_hidden[rows] = d_hidden

        loop(grid // TILE, tile)
        if keep_state:
            k.wait(N_FIRST)
            k.wait(N_D_NEXT)
            k.d_state[...] = (
                k.d_next[...] + dense_right(k.first[...], k.d_hidden[...]) / k.scales[...]
            )
            k.flush(N_D_STATE)
        k.wait(N_FEATS)
        if others is None:
            k.flush(N_SUMS)
            put_grad(k, True, 0, dense(k.feats[...], k.d_hidden[...]))
            weight_grad(k, True, depth, k.act, k.d_mixed)
            k.flush(N_GRADS)
            return
        k.wait(N_BEFORE)
        k.grads[:, 0 : depth + D, :] = k.before[...]
        put_grad(k, False, 0, dense(k.feats[...], k.d_hidden[...]))
        weight_grad(k, False, depth, k.act, k.d_mixed)
        k.wait(N_EMBED_GRADS)
        k.grads[:, depth + D : at_vectors, :] = k.embed_grads[...]
        k.grads[:, at_vectors:, :] = jnp.zeros((BLOCKS, rows_all - at_vectors, BLOCK), f32)
        sources = [(k.sums, 0), (k.sums_embed, 0)]
        sources += [(getattr(k, N_SUMS_ + str(l)), 0) for l in range(LAYERS)]
        sources += [(getattr(k, N_SUMS_ + str(l)), 3) for l in range(LAYERS)]
        sources += [(k.sums_dec, 0)]
        for i, (source, at) in enumerate(sources):
            set_grad(k, at_vectors + 3 * i, source[at : at + 3, :])
        k.flush_swap()

    parts = grid // TILE
    ins = [
        (N_RETURNED, returned, N_V),
        (N_PICKS_ROW, picks_row, N_V),
        (N_ASSIGN, assign, N_V),
        (N_SCALES, scales, N_V),
        (N_VECTORS, vectors, N_V),
        (N_D_NODES, d_nodes, N_H, ((), 1)),
        (N_INNER,) + inner,
        (N_D_GRID, d_grid, N_H, ((), parts)),
        (N_HIDDEN, kept[N_HIDDEN], N_H, ((), parts)),
        (N_NORMED, kept[N_NORMED], N_H, ((), parts)),
        (N_INVERSE, kept[N_INVERSE], N_H, ((), parts)),
        (N_FEATS, feats, N_H, ((), 1)),
    ]
    outs = []
    if keep_state:
        ins += [(N_FIRST,) + first, (N_D_NEXT, d_next, N_H, ((), 1))]
        outs.append((N_D_STATE, (depth, grid), f32, N_H, 1))
    scratch = [
        ("both", (NODE_CAP, 2 * D), bf16),
        (N_ACT, (grid, D), bf16),
        (N_D_MIXED, (grid, D), bf16),
        (N_D_HIDDEN, (grid, D), bf16),
    ]
    if not fresh:
        ins.append((N_SUMS, sums, N_H, ((), 1)))
    if others is None:
        outs.append((N_SUMS, (8, D), f32, N_H, 1))
        outs.append((N_GRADS, (BLOCKS, rows_all, BLOCK), f32, N_H, BLOCKS))
    else:
        ins.append((N_BEFORE, grads, N_H, ((), BLOCKS)))
        ins.append((N_EMBED_GRADS, embed_grads, N_H, ((), BLOCKS)))
        ins += [(N_SUMS_ + str(name), value, N_V) for name, value in all_sums.items()]
        scratch.append((N_GRADS, (BLOCKS, rows_all, BLOCK), f32))
    out = launch(body, ins, outs, scratch, micros=10, swap=swap, after=after)
    if others is not None:
        return out
    return out if keep_state else (None, out[0], out[1])


def embed_backward(d_first, d_second, kept, geometry, inner, vectors, after):
    count = kept[N_HIDDEN].shape[0]
    features = geometry.shape[0]

    def body(k):
        start_sums(k, True)
        k.wait(N_INNER)

        def tile(t):
            rows = row_tile(t, TILE)
            for name in (N_D_FIRST, N_D_SECOND, N_HIDDEN, N_NORMED, N_INVERSE):
                k.wait(name, t)
            act, d_mixed, d_hidden = backward_rows(
                k, 1, k.d_first[rows] + k.d_second[rows], k.hidden[rows], k.normed[rows],
                k.inverse[rows], k.inner[...], k.sums, 0,
            )
            k.act[rows] = act
            k.d_mixed[rows] = d_mixed
            k.d_hidden[rows] = d_hidden

        loop(count // TILE, tile)
        k.flush(N_SUMS)
        set_grad(k, 0, dense(k.geometry[...], k.d_hidden[...]))
        weight_grad(k, True, features, k.act, k.d_mixed)
        k.flush(N_GRADS)

    parts = count // TILE
    ins = [
        (N_GEOMETRY, geometry, N_V),
        (N_VECTORS, vectors, N_V),
        (N_INNER,) + inner,
        (N_D_FIRST, d_first, N_H, ((), parts)),
        (N_D_SECOND, d_second, N_H, ((), parts)),
        (N_HIDDEN, kept[N_HIDDEN], N_H, ((), parts)),
        (N_NORMED, kept[N_NORMED], N_H, ((), parts)),
        (N_INVERSE, kept[N_INVERSE], N_H, ((), parts)),
    ]
    return launch(
        body,
        ins,
        [
            (N_SUMS, (8, D), f32, N_H, 1),
            (N_GRADS, (BLOCKS, features + D, BLOCK), f32, N_H, BLOCKS),
        ],
        [
            (N_ACT, (count, D), bf16),
            (N_D_MIXED, (count, D), bf16),
            (N_D_HIDDEN, (count, D), bf16),
        ],
        micros=11,
        after=after,
    )


def coded_rows(rows):
    return rows + up_to(rows // CODED, 16)


def encode(source, first, rows, target, scale):
    scale[...] = jnp.zeros(scale.shape, f32)

    def step(t):
        value = source[pl.ds(pl.multiple_of(first + t * CODED, CODED), CODED)]
        top = jnp.maximum(jnp.max(jnp.abs(value), 0, keepdims=True), 1e-30)
        exponent = jnp.ceil(jnp.log2(top))
        scale[pl.ds(t, 1), :] = exponent
        value = jnp.round(value * (CODE_TOP * jnp.exp2(-exponent)))
        target[row_tile(t, CODED)] = value.astype(jnp.int32).astype(jnp.int16)

    loop(rows // CODED, step, 8)
    more = coded_rows(rows) - rows
    target[rows : rows + more] = scale[0:more].astype(jnp.int32).astype(jnp.int16)


def scales_of(coded, rows, scale):
    more = coded_rows(rows) - rows
    exponent = coded[rows : rows + more].astype(jnp.int32).astype(f32)
    scale[0:more] = jnp.exp2(exponent) * (1.0 / CODE_TOP)


def decoded(coded, scale, t):
    return coded[row_tile(t, CODED)].astype(jnp.int32).astype(f32) * scale[pl.ds(t, 1), :]


def difference(p, order):
    return sum(bit for i, bit in enumerate(reversed(order)) if p >> i & 1)


CORES, OVER_X, TURN, JOIN, ALL = range(5)


def combine(jobs, order, place, after):
    regions = 2 ** len(order)
    operands, out_shape, scratch_shapes, plans = [], [], [], []
    squares = False

    def buffer(shape, dtype):
        scratch_shapes.append(pltpu.VMEM(shape, dtype))
        return len(scratch_shapes) - 1

    def output(shape, dtype):
        out_shape.append(jax.ShapeDtypeStruct(shape, dtype))
        return len(out_shape) - 1

    for kind, arrays, ways in jobs:
        loads, stores = [], []
        for array in arrays:
            loads.append((len(operands), buffer(array.shape, array.dtype)))
            operands.append(array)
        blocks, size = 1, 0
        if kind == CORES:
            size = arrays[0].shape[0]
            stores.append((output((size, BLOCK), f32), loads[0][1], None))
        elif kind == JOIN:
            shape = arrays[0].shape
            at = output((len(arrays) * shape[0],) + shape[1:], jnp.int16)
            stores = [(at, item[1], i * shape[0]) for i, item in enumerate(loads)]
        elif kind == ALL:
            code = arrays[0].shape[1]
            size = max(r for r in range(CODED, code, CODED) if coded_rows(r) == code)
            at = output((regions, code, BLOCK), jnp.int16)
            kept = buffer((1, code, BLOCK), jnp.int16)
            stores = [(at, kept, i) for i in range(regions)]
            squares = True
        else:
            rows = arrays[0].shape[0]
            if kind == OVER_X:
                size = rows // regions
            else:
                code = arrays[1].shape[1]
                size = max(r for r in range(CODED, code, CODED) if coded_rows(r) == code)
            blocks = rows // size // max(ways, 1)
            if ways > 1:
                at = output((blocks * size, BLOCK), f32)
                stores.append((at, buffer((blocks * size, BLOCK), f32), None))
            elif ways == 1:
                squares = True
        if kind not in (JOIN, ALL):
            for _ in range(max(ways - 1, 1)):
                shape = (blocks, coded_rows(size), BLOCK)
                stores.append((output(shape, jnp.int16), buffer(shape, jnp.int16), None))
        work = None
        if kind != JOIN:
            rows = size if kind == ALL else arrays[0].shape[0]
            work = (buffer((rows, BLOCK), f32), buffer((up_to(rows // CODED, 16), BLOCK), f32))
        plans.append((kind, ways, blocks, size, loads, stores, work))
    count = len(out_shape)
    if squares:
        out_shape.append(jax.ShapeDtypeStruct((CODED, BLOCK), f32))
    most = max(len(plan[5]) for plan in plans)

    def kernel(*refs):
        region = refs[0][1]
        ins = refs[1 : 1 + len(operands)]
        outs = refs[1 + len(operands) + len(after) :][: len(out_shape)]
        rest = refs[1 + len(operands) + len(after) + len(out_shape) :]
        sem_in, sem_out = rest[-2:]

        def load(at, kept):
            return pltpu.make_async_copy(ins[at], rest[kept], sem_in.at[at])

        def store(job, i):
            at, kept, first = plans[job][5][i]
            target = outs[at]
            if first is not None:
                target = target.at[pl.ds(first, rest[kept].shape[0])]
            return pltpu.make_async_copy(rest[kept], target, sem_out.at[job, i])

        def add_squares(total, rows):
            def step(t):
                value = total[row_tile(t, CODED)]
                outs[-1][...] += value * value

            loop(rows // CODED, step, 8)

        for plan in plans:
            for item in plan[4]:
                load(*item).start()
        if squares:
            outs[-1][...] = jnp.zeros((CODED, BLOCK), f32)
        for job, (kind, ways, blocks, size, loads, stores, work) in enumerate(plans):
            for item in loads:
                load(*item).wait()
            values = [rest[item[1]] for item in loads]
            results = [rest[item[1]] for item in stores]
            if kind == CORES:
                total, scale = rest[work[0]], rest[work[1]]

                def step(t):
                    at = row_tile(t, 256)
                    values[0][at] += values[1][at]
                    total[at] = values[2][at] + values[3][at]

                loop(size // 256, step)
                encode(total, 0, size, results[1].at[0], scale)
            elif kind == ALL:
                total, scale = rest[work[0]], rest[work[1]]
                total[...] = jnp.zeros((size, BLOCK), f32)
                for i in range(regions):
                    scales_of(values[0].at[i], size, scale)

                    def step(t):
                        total[row_tile(t, CODED)] += decoded(values[0].at[i], scale, t)

                    loop(size // CODED, step, 8)
                encode(total, 0, size, results[0].at[0], scale)
                add_squares(total, size)
            elif kind != JOIN:
                total, scale = rest[work[0]], rest[work[1]]
                mine = values[0]
                if kind == OVER_X:
                    rows = size * regions
                    scales_of(values[1].at[0], rows, scale)

                    def step(t):
                        at = row_tile(t, CODED)
                        total[at] = mine[at] + decoded(values[1].at[0], scale, t)

                    loop(rows // CODED, step, 8)
                else:
                    for i in range(blocks * ways):
                        for j, coded in enumerate(values[1:]):
                            scales_of(coded.at[i], size, scale)

                            def step(t):
                                at = pl.ds(pl.multiple_of(i * size + t * CODED, CODED), CODED)
                                value = total[at] if j else mine[at]
                                total[at] = value + decoded(coded.at[i], scale, t)

                            loop(size // CODED, step, 8)

                def first_row(p):
                    if kind == OVER_X and ways:
                        return lax.bitwise_xor(region, difference(p, order)) * size
                    return p * size

                for p in range(blocks * max(ways, 1)):
                    way, i = p // blocks, p % blocks
                    if ways > 1 and way == 0:

                        def step(t):
                            at = pl.ds(pl.multiple_of(first_row(p) + t * CODED, CODED), CODED)
                            to = pl.ds(pl.multiple_of(i * size + t * CODED, CODED), CODED)
                            results[0][to] = total[at]

                        loop(size // CODED, step, 8)
                    else:
                        encode(total, first_row(p), size, results[way].at[i], scale)
                if ways == 1:
                    add_squares(total, size)
            for i in range(len(stores)):
                store(job, i).start()
        for job in range(len(plans)):
            for i in range(len(plans[job][5])):
                store(job, i).wait()

    any_space = pl.BlockSpec(memory_space=pl.ANY)
    out_specs = [any_space] * count
    if squares:
        out_specs.append(pl.BlockSpec(memory_space=pltpu.VMEM))
    out = pl.pallas_call(
        kernel,
        out_shape=out_shape,
        in_specs=[pl.BlockSpec(memory_space=pltpu.SMEM)]
        + [any_space] * (len(operands) + len(after)),
        out_specs=out_specs,
        scratch_shapes=scratch_shapes
        + [
            pltpu.SemaphoreType.DMA((len(operands),)),
            pltpu.SemaphoreType.DMA((len(jobs), most)),
        ],
        compiler_params=pltpu.CompilerParams(vmem_limit_bytes=56 * 2**20),
        cost_estimate=cost_of(5),
    )(place, *operands, *after)
    parts = []
    for plan in plans:
        found = []
        for item in plan[5]:
            if item[0] not in found:
                found.append(item[0])
        parts.append([out[i] for i in found])
    return parts, (out[-1] if squares else None)


def pack(pieces, after):
    sizes = [array.shape[-2] for array, _, _ in pieces]
    firsts = [sum(rows for _, _, rows in pieces[:i]) for i in range(len(pieces) + 1)]

    def kernel(*refs):
        ins = refs[: len(pieces)]
        out = refs[len(pieces) + len(after)]
        packed, sem_in, sem_out = refs[-3:]
        buffers = refs[len(pieces) + len(after) + 1 : -3]

        def load(i):
            source = ins[i] if pieces[i][1] is None else ins[i].at[pieces[i][1]]
            target = buffers[i]
            if sizes[i] < pieces[i][2]:
                target = target.at[pl.ds(0, sizes[i])]
            return pltpu.make_async_copy(source, target, sem_in.at[i])

        def store(i):
            rows = pl.ds(firsts[i], pieces[i][2])
            return pltpu.make_async_copy(packed.at[rows], out.at[rows], sem_out.at[i])

        for i, (_, _, rows) in enumerate(pieces):
            if sizes[i] < rows:
                buffers[i][...] = jnp.zeros((rows, BLOCK), f32)
            load(i).start()
        for i, (_, _, rows) in enumerate(pieces):
            load(i).wait()
            step = max(n for n in range(16, 257, 16) if rows % n == 0)
            for row in range(0, rows, step):
                at = firsts[i] + row
                packed[at : at + step] = buffers[i][row : row + step].astype(bf16)
            store(i).start()
        for i in range(len(pieces)):
            store(i).wait()

    any_space = pl.BlockSpec(memory_space=pl.ANY)
    return pl.pallas_call(
        kernel,
        out_shape=jax.ShapeDtypeStruct((firsts[-1], BLOCK), bf16),
        in_specs=[any_space] * (len(pieces) + len(after)),
        out_specs=any_space,
        scratch_shapes=[pltpu.VMEM((rows, BLOCK), f32) for _, _, rows in pieces]
        + [
            pltpu.VMEM((firsts[-1], BLOCK), bf16),
            pltpu.SemaphoreType.DMA((len(pieces),)),
            pltpu.SemaphoreType.DMA((len(pieces),)),
        ],
        compiler_params=pltpu.CompilerParams(vmem_limit_bytes=56 * 2**20),
        cost_estimate=cost_of(2),
    )(*[array for array, _, _ in pieces], *after)


def update_weights(factor, place, order, groups, masters, moments, squares, chunks):
    count = len(masters)
    rows_of = [c[3] for c in chunks]
    places = 2 ** len(order)
    starts = [0]
    for group in groups:
        starts.append(starts[-1] + len(group))
    flat_first = [0]
    for master in masters:
        flat_first.append(flat_first[-1] + master.size // BLOCK)
    block_rows = []
    for group in groups:
        code = group[0].shape[1]
        block_rows.append(max(r for r in range(CODED, code, CODED) if coded_rows(r) == code))

    def kernel(*refs):
        scale = refs[0][0, 0]
        region = refs[1][1]
        group_refs = refs[2 : 2 + starts[-1]]
        at = 2 + starts[-1]
        param_refs = refs[at : at + 3 * count]
        out_refs = refs[at + 3 * count : at + 6 * count]
        flat_out = refs[at + 6 * count]
        rest = refs[at + 6 * count + 1 :]
        sem_in, sem_out, sem_grad = rest[-3:]
        factors, flat = rest[-5:-3]
        coded_refs = rest[3 * len(chunks) :][: starts[-1]]
        grad_refs = rest[3 * len(chunks) + starts[-1] :][: len(groups)]

        def grad_copies(g):
            return [
                pltpu.make_async_copy(group_refs[i], coded_refs[i], sem_grad.at[i])
                for i in range(starts[g], starts[g + 1])
            ]

        def decode(g):
            rows = block_rows[g]

            for p in range(places):
                if starts[g + 1] - starts[g] == 2:
                    coded = coded_refs[starts[g] + 2 * p // places].at[p % (places // 2)]
                    first = lax.bitwise_xor(region, difference(p, order)) * rows
                else:
                    coded, first = coded_refs[starts[g]].at[p], p * rows
                scales_of(coded, rows, factors)

                def step(t):
                    at = pl.ds(pl.multiple_of(first + t * CODED, CODED), CODED)
                    grad_refs[g][at] = decoded(coded, factors, t)

                loop(rows // CODED, step, 8)

        def piece(ref, chunk):
            for i in chunk[1]:
                ref = ref.at[i]
            if chunk[3] < ref.shape[0]:
                ref = ref.at[pl.ds(chunk[2], chunk[3])]
            return ref

        def copies(i):
            chunk = chunks[i]
            w = chunk[0]
            found = []
            for j in range(3):
                found.append(
                    pltpu.make_async_copy(
                        piece(param_refs[3 * w + j], chunk), rest[3 * i + j], sem_in.at[3 * i + j]
                    )
                )
            return found

        def stores(i):
            chunk = chunks[i]
            return [
                pltpu.make_async_copy(
                    rest[3 * i + (j + 1) % 3],
                    piece(out_refs[3 * chunk[0] + j], chunk),
                    sem_out.at[3 * i + j],
                )
                for j in range(3)
            ]

        started = set()
        for i in range(len(chunks)):
            if chunks[i][4] not in started:
                started.add(chunks[i][4])
                for copy in grad_copies(chunks[i][4]):
                    copy.start()
            for copy in copies(i):
                copy.start()
        for i in range(len(chunks)):
            if chunks[i][4] in started:
                started.remove(chunks[i][4])
                for copy in grad_copies(chunks[i][4]):
                    copy.wait()
                decode(chunks[i][4])
            for copy in copies(i):
                copy.wait()
            master_ref, moment_ref, square_ref = rest[3 * i : 3 * i + 3]
            grad_ref, first_row = grad_refs[chunks[i][4]], chunks[i][5]

            flat_row = flat_first[chunks[i][0]] + chunks[i][2]
            if chunks[i][1]:
                flat_row += chunks[i][1][0] * masters[chunks[i][0]].shape[1]
            step = 128 if rows_of[i] % 128 == 0 else rows_of[i]
            for row in range(0, rows_of[i], step):
                rows = slice(row, row + step)
                first, second, master = adam(
                    master_ref[rows],
                    moment_ref[rows],
                    square_ref[rows],
                    grad_ref[first_row + row : first_row + row + step] * scale,
                )
                moment_ref[rows] = first
                square_ref[rows] = second
                master_ref[rows] = master
                flat[flat_row + row : flat_row + row + step] = master

            for copy in stores(i):
                copy.start()
        flat_copy = pltpu.make_async_copy(
            flat.at[pl.ds(0, flat_first[-1])], flat_out.at[:, 0], sem_out.at[3 * len(chunks)]
        )
        flat_copy.start()
        for i in range(len(chunks)):
            for copy in stores(i):
                copy.wait()
        flat_copy.wait()

    any_space = pl.BlockSpec(memory_space=pl.ANY)
    flat_shape = (up_to(flat_first[-1], 8), BLOCK)
    scratch_shapes = []
    for rows in rows_of:
        scratch_shapes += [pltpu.VMEM((rows, BLOCK), f32)] * 3
    coded_parts = [part for group in groups for part in group]
    scratch_shapes += [pltpu.VMEM(part.shape, part.dtype) for part in coded_parts]
    scratch_shapes += [pltpu.VMEM((places * rows, BLOCK), f32) for rows in block_rows]
    scratch_shapes.append(pltpu.VMEM((up_to(max(block_rows) // CODED, 16), BLOCK), f32))
    scratch_shapes.append(pltpu.VMEM(flat_shape, f32))
    scratch_shapes.append(pltpu.SemaphoreType.DMA((3 * len(chunks),)))
    scratch_shapes.append(pltpu.SemaphoreType.DMA((3 * len(chunks) + 1,)))
    scratch_shapes.append(pltpu.SemaphoreType.DMA((starts[-1],)))
    params = [value for item in zip(masters, moments, squares) for value in item]
    return pl.pallas_call(
        kernel,
        out_shape=[jax.ShapeDtypeStruct(p.shape, f32) for p in params]
        + [jax.ShapeDtypeStruct((flat_first[-1], 1, BLOCK), f32)],
        in_specs=[pl.BlockSpec(memory_space=pltpu.SMEM)] * 2
        + [any_space] * (len(coded_parts) + len(params)),
        out_specs=[any_space] * (len(params) + 1),
        scratch_shapes=scratch_shapes,
        compiler_params=pltpu.CompilerParams(vmem_limit_bytes=56 * 2**20),
        cost_estimate=cost_of(0),
    )(factor, place, *coded_parts, *params)


def adam(master, moment, square, grad):
    first = beta_first * moment + (1 - beta_first) * grad
    second = beta_second * square + (1 - beta_second) * grad * grad
    ratio = (
        first
        / (1 - beta_first**STEP_COUNT)
        / (jnp.sqrt(second / (1 - beta_second**STEP_COUNT)) + adam_eps)
    )
    return (first, second, master - learn_rate * (ratio + decay_weight * master))


def pad_rows(value, rows):
    return jnp.pad(value, ((0, rows - value.shape[0]), (0, 0)))


def body(
    initial_state,
    target_states,
    var_means,
    var_scales,
    delta_scales,
    edge_geometry,
    node_counts,
    edge_counts,
    receivers,
    senders,
    send_lists,
    grid_nodes,
    cell_area,
    step_weights,
    *params,
):
    masters, moments, squares = params[0::3], params[1::3], params[2::3]
    enc_w, embed_w, edge_w, node_w, dec_w, inner_w, vector_w, head_w = masters
    variables = enc_w.shape[0]
    depth = up_to(variables, 16)
    features = embed_w.shape[0]
    feature_rows = up_to(features, 16)
    vector_rows = up_to(vector_w.shape[0], 16)
    last_block = 2 + 2 * LAYERS

    def partner(value, axis, bit):
        count = lax.axis_size(axis)
        return lax.ppermute(value, axis, [(i, i ^ bit) for i in range(count)])

    place = jnp.stack([lax.axis_index(N_REP), lax.axis_index(N_REGION)]).astype(jnp.int32)

    def gather(pieces, after=()):
        return (place, lax.all_gather(pack(pieces, after), N_REP))

    start = gather(
        [
            (enc_w, None, depth),
            (inner_w, 0, D),
            (embed_w, None, feature_rows),
            (inner_w, 1, D),
            (vector_w, None, vector_rows),
        ]
    )
    of_layer = []
    for l in range(LAYERS):
        pieces = [(edge_w, l, 3 * D), (inner_w, 2 + l, D)]
        pieces += [(node_w, l, 2 * D), (inner_w, 2 + LAYERS + l, D)]
        of_layer.append(gather(pieces))
    end = gather(
        [(dec_w, None, 2 * D), (inner_w, last_block, D), (head_w, None, depth)]
    )
    enc_first = (start, N_W, (0, depth))
    enc_inner = (start, N_W, (depth, D))
    embed_first = (start, N_W, (depth + D, feature_rows))
    embed_inner = (start, N_W, (depth + D + feature_rows, D))
    at_vectors = depth + 2 * D + feature_rows
    vectors = start[1][:, at_vectors:].astype(f32).transpose(1, 0, 2).reshape(vector_rows, D)
    layer_weights = [
        (
            (of_layer[l], N_W, (0, 3 * D)),
            (of_layer[l], N_W, (3 * D, D)),
            (of_layer[l], N_W, (4 * D, 2 * D)),
            (of_layer[l], N_W, (6 * D, D)),
        )
        for l in range(LAYERS)
    ]
    dec_weights = (
        (end, N_W, (0, 2 * D)),
        (end, N_W, (2 * D, D)),
        (end, N_W, (3 * D, depth)),
    )

    count = node_counts[0]
    send_from = jnp.where(senders < NODE_CAP, senders % count, senders)
    live = jnp.arange(receivers.shape[0]) < edge_counts[0]
    recv = jnp.where(live, receivers, -1)
    picks = (send_lists[0] % count).reshape(-1)
    assign = grid_nodes % count
    regions, slots = send_lists.shape[1:]
    send, send_row = send_from[:, None], send_from[None, :]
    recv, recv_row = recv[:, None], recv[None, :]
    picks, picks_row = picks[:, None], picks[None, :]
    assign, assign_row = assign[:, None], assign[None, :]

    def exchange(rows):
        table = rows.reshape(regions, slots, D)
        table = lax.all_to_all(table, N_REGION, split_axis=0, concat_axis=0, tiled=True)
        return table.reshape(regions * slots, D)

    def column(value, fill):
        return jnp.pad(value, (0, depth - variables), constant_values=fill)[:, None]

    means, scales, delta = column(var_means, 0), column(var_scales, 1), column(delta_scales, 1)
    state = pad_rows(initial_state[0].T, depth)
    target = jnp.pad(
        target_states[0].transpose(0, 2, 1), ((0, 0), (0, depth - variables), (0, 0))
    )
    area = cell_area[None, :]
    geometry = pad_rows(edge_geometry.T, feature_rows).astype(bf16)
    plan = step_weights

    bits = [1 << i for i in range(regions.bit_length() - 1)]
    turns = [bits[:1]] + [bits[i : i + 2] for i in range(1, len(bits), 2)]
    unit = CODED * regions
    dec_rows, layer_rows = up_to(3 * D + depth, unit), up_to(7 * D, unit)
    start_rows = up_to(at_vectors + vector_rows, unit)

    weight_local = (
        jnp.sum(plan.astype(f32)) * jnp.sum(cell_area) * variables * lax.axis_size(N_REP)
    )
    weight_total = jnp.broadcast_to(weight_local, (8, BLOCK))
    for bit in bits:
        weight_total = weight_total + partner(weight_total, N_REGION, bit)
    weight_total = weight_total[0, 0]
    inverse_total = (1.0 / weight_total).reshape(1, 1)

    edges0, edges0_low, *keep_embed = embed_forward(geometry, embed_first, embed_inner, 1, vectors)
    keep_embed = dict(zip((N_HIDDEN, N_NORMED, N_INVERSE), keep_embed))
    records = []
    loss_local = 0.0
    for step in range(STEPS):
        nodes, node_low, outgoing, latent, low, feats, hidden, normed, inverse = encoder_forward(
            state, means, scales, enc_first, enc_inner, vectors, assign_row, picks
        )
        keep_enc = {N_FEATS: feats, N_HIDDEN: hidden, N_NORMED: normed, N_INVERSE: inverse}
        edges, edges_low = edges0, edges0_low
        layers = []
        for l in range(LAYERS):
            halo = exchange(outgoing)
            first = layer_weights[l][0]
            local = layer_local(l, edges_low, node_low, first, vectors, send, recv)
            from_send = (first[0], N_W, (first[2][0] + D, D))
            before = edges_low
            edges, edges_low, nodes, node_low, outgoing, kept = layer_forward(
                l, local, edges, nodes, node_low, halo, (from_send,) + layer_weights[l][1:],
                vectors, send, recv_row, picks, l == LAYERS - 1,
            )
            kept[N_EDGES_LOW] = before
            layers.append(kept)
        state, loss, keep_dec = decoder_forward(
            step, state, target, latent, low, node_low, dec_weights, vectors,
            assign, delta, area, plan,
        )
        loss_local = loss_local + loss[0, 0]
        records.append((keep_enc, layers, keep_dec))

    class Sum:
        def __init__(self, parts, at_once=False):
            self.parts = list(parts)
            self.at_once = at_once
            self.stage = -2
            self.halves = None

        def job(self):
            p, count = self.parts, len(turns)
            if self.stage == -2:
                return (CORES, [p[0], partner(p[1], N_REP, 1), p[2], partner(p[3], N_REP, 1)], 0)
            if self.stage == -1:
                ways = 0 if self.at_once else 2 ** len(turns[0])
                return (OVER_X, [p[0], partner(p[1], N_REP, 2)], ways)
            if self.at_once:
                return (ALL, [self.all_turn()], 1)
            if self.stage < count:
                turn, last = turns[self.stage], self.stage == count - 1
                ways = 1 if last else 2 ** len(turns[self.stage + 1])
                got = [
                    partner(p[q], N_REGION, difference(q, turn)) for q in range(1, 2 ** len(turn))
                ]
                return (TURN, [p[0]] + got, ways)
            turn = turns[2 * count - 1 - self.stage]
            got = [partner(p[0], N_REGION, difference(q, turn)) for q in range(1, 2 ** len(turn))]
            return (JOIN, [p[0]] + got, 0)

        def summed(self):
            return self.stage >= (1 if self.at_once else len(turns))

        def all_turn(self):
            return lax.all_to_all(
                self.parts[0], N_REGION, split_axis=0, concat_axis=0, tiled=True
            )

        def done(self, parts):
            self.parts = parts
            self.stage += 1
            if self.at_once:
                if self.stage == 1:
                    self.halves = [self.all_turn()]
                return
            if self.stage == 2 * len(turns) - 1:
                self.halves = [parts[0], partner(parts[0], N_REGION, bits[0])]

    def over_all(value):
        for bit in bits:
            value = value + partner(value, N_REGION, bit)
        for bit in (1, 2):
            value = value + partner(value, N_REP, bit)
        return value

    all_squares = []
    on_way = {}
    arrived = []

    def advance(names, after):
        names = [name for name in names if on_way[name].halves is None]
        if not names:
            return after
        jobs = [on_way[name].job() for name in names]
        parts, squares = combine(jobs, bits, place, list(after) + arrived)
        arrived.clear()
        if squares is not None:
            all_squares.append(jnp.sum(squares, 0))
        for name, found in zip(names, parts):
            on_way[name].done(found)
            if on_way[name].halves is not None:
                arrived.append(on_way[name].halves[-1])
        return [parts[0][0]]

    d_state = None
    grads = {}
    d_embed = []
    for step in reversed(range(STEPS)):
        keep_enc, layers, keep_dec = records[step]
        final = step == 0
        d_nodes, d_grid, d_next, sums, grad = decoder_backward(
            step, regions, d_state, keep_dec, dec_weights, vectors, assign_row, delta, area, plan,
            inverse_total, *grads.get(N_DEC, (None, None)),
            (place, dec_rows) if final else None,
        )
        grads[N_DEC] = (grad if final else grad[0], sums)
        returned, d_edges = None, None
        after = []
        if final:
            on_way[N_DEC] = Sum(grad)
        for l in reversed(range(LAYERS)):
            old_grad, old_sums = grads.get(l, (None, None))
            found = layer_backward(
                l, d_nodes, returned, d_edges, layers[l], layer_weights[l], vectors,
                send_row, recv, picks_row, old_sums, after,
            )
            d_edges, sums = found[N_D_EDGES], found[N_SUMS]
            returned = exchange(found[N_D_HALO])
            after = advance(list(on_way), [sums]) + [returned] if final else []
            d_nodes, grad = layer_grads(
                found, layers[l], layer_weights[l][0], send_row, recv_row, layer_rows, old_grad,
                (place, layer_rows) if final else None, after,
            )
            grads[l] = (grad if final else grad[0], sums)
            after = advance([N_DEC, 2], [d_nodes]) if final and l == 0 else []
            if final:
                on_way[l] = Sum(grad)
        d_embed.append(d_edges)
        others, swap = None, None
        if final:
            embed_sums, embed_grads = embed_backward(
                d_embed[0], d_embed[1], keep_embed, geometry, embed_inner, vectors, after
            )
            after = advance([0, 1, 2, N_DEC], [embed_sums])
            all_sums = {"embed": embed_sums}
            for name in [N_DEC] + list(range(LAYERS)):
                all_sums[name] = grads[name][1]
            others, swap = (embed_grads, all_sums), (place, start_rows)
        out = encoder_backward(
            step, d_grid, d_nodes, returned, d_next, keep_enc, (enc_first, enc_inner), vectors,
            assign, picks_row, scales, *grads.get(N_ENC, (None, None)), others, swap, after,
        )
        if not final:
            d_state, sums, grad = out
            grads[N_ENC] = (grad, sums)
    after = advance([N_DEC, 2, 1], [out[0]])
    on_way["start"] = Sum(out, True)
    totals = None
    while any(item.halves is None for item in on_way.values()):
        after = advance(list(on_way), after)
        if totals is None and all(item.summed() for item in on_way.values()):
            squares_row = sum(all_squares)
            totals = over_all(jnp.stack([squares_row, jnp.broadcast_to(loss_local, (BLOCK,))]))
            arrived.append(totals)
    gradient_norm = jnp.sqrt(jnp.sum(totals[0]))
    loss_total = totals[1, 0]
    factor = jnp.minimum(1.0, clip_limit / gradient_norm)

    order = list(on_way)
    groups = [on_way[name].halves for name in order]
    last_group = len(groups) - 1
    chunks = []
    for l in reversed(range(LAYERS)):
        group = order.index(l)
        chunks += [(2, (l,), i * D, D, group, i * D) for i in range(3)]
        chunks.append((5, (2 + l,), 0, D, group, 3 * D))
        chunks += [(3, (l,), i * D, D, group, (4 + i) * D) for i in range(2)]
        chunks.append((5, (2 + LAYERS + l,), 0, D, group, 6 * D))
    chunks += [(4, (), i * D, D, 0, i * D) for i in range(2)]
    chunks.append((5, (last_block,), 0, D, 0, 2 * D))
    chunks.append((7, (), 0, variables, 0, 3 * D))
    chunks.append((0, (), 0, variables, last_group, 0))
    chunks.append((5, (0,), 0, D, last_group, depth))
    chunks.append((1, (), 0, features, last_group, depth + D))
    chunks.append((5, (1,), 0, D, last_group, depth + D + feature_rows))
    chunks.append((6, (), 0, vector_w.shape[0], last_group, at_vectors))
    *new, flat = update_weights(
        factor.reshape(1, 1), place, bits, groups, masters, moments, squares, chunks
    )
    weight_copies = flat.reshape(1, -1).astype(bf16)
    return (loss_total, weight_total, gradient_norm, *new, weight_copies)


def solution(mesh):
    two = P(None, N_REP)
    three = P(None, None, N_REP)
    weights = (two, two, three, three, two, three, two, two)
    placed = (
        P(N_REP, N_REGION, None),
        P(N_REP, None, N_REGION, None),
        P(),
        P(),
        P(),
        P(N_REGION, None),
        P(N_REGION),
        P(N_REGION),
        P(N_REGION),
        P(N_REGION),
        P(N_REGION, None, None),
        P(N_REGION),
        P(N_REGION),
        P(),
    ) + tuple(spec for spec in weights for _ in range(3))
    return jax.shard_map(
        body,
        mesh=mesh,
        in_specs=placed,
        out_specs=(P(), P(), P())
        + tuple(spec for spec in weights for _ in range(3))
        + (P(N_REP, None),),
        check_vma=False,
    )
```

```python
import jax
import jax.numpy as jnp
from jax import lax
from jax.experimental import pallas as pl
from jax.experimental.pallas import tpu as pltpu
from jax.sharding import PartitionSpec as P

LAYERS = 3
STEPS = 2
STEP_COUNT = 10
NODE_CAP = 512
D = 512
BLOCK = 128
BLOCKS = D // BLOCK
TILE = 512
CODED = 32
CODE_TOP = 32000.0

norm_eps = 1e-05
beta_first = 0.9
beta_second = 0.95
adam_eps = 1e-08
decay_weight = 0.1
learn_rate = 0.05
clip_limit = 0.02

N_ACT = "act"
N_AREA = "area"
N_ASSIGN = "assign"
N_B = "b"
N_BEFORE = "before"
N_D_EDGES = "d_edges"
N_D_FIRST = "d_first"
N_D_GRID = "d_grid"
N_D_HALO = "d_halo"
N_D_HIDDEN = "d_hidden"
N_D_MIXED = "d_mixed"
N_D_NEXT = "d_next"
N_D_NODES = "d_nodes"
N_D_SECOND = "d_second"
N_D_STATE = "d_state"
N_DEC = "dec"
N_DELTA = "delta"
N_EDGE_FIRST = "edge_first"
N_EDGE_INNER = "edge_inner"
N_EDGES = "edges"
N_EDGES_LOW = "edges_low"
N_EMBED_GRADS = "embed_grads"
N_ENC = "enc"
N_FEATS = "feats"
N_FINAL = "final"
N_FIRST = "first"
N_FROM_RECV = "from_recv"
N_FROM_SEND = "from_send"
N_GEOMETRY = "geometry"
N_GRADS = "grads"
N_H = "h"
N_HALO = "halo"
N_HALO_HIGH = "halo_high"
N_HALO_REST = "halo_rest"
N_HEAD = "head"
N_HIDDEN = "hidden"
N_INNER = "inner"
N_INVERSE = "inverse"
N_LATENT = "latent"
N_LOCAL = "local"
N_LOW = "low"
N_MISS = "miss"
N_NODE_ACT = "node_act"
N_NODE_D_HIDDEN = "node_d_hidden"
N_NODE_D_MIXED = "node_d_mixed"
N_NODE_FIRST = "node_first"
N_NODE_HIDDEN = "node_hidden"
N_NODE_INNER = "node_inner"
N_NODE_INVERSE = "node_inverse"
N_NODE_LOW = "node_low"
N_NODE_NORMED = "node_normed"
N_NODES = "nodes"
N_NORMED = "normed"
N_OUTGOING = "outgoing"
N_PICKS = "picks"
N_PICKS_ROW = "picks_row"
N_PLAN = "plan"
N_RECV = "recv"
N_RECV_ROW = "recv_row"
N_REGION = "region"
N_REP = "rep"
N_RETURNED = "returned"
N_S = "s"
N_SCALES = "scales"
N_SEND = "send"
N_SEND_ROW = "send_row"
N_STATE = "state"
N_SUMS = "sums"
N_SUMS_ = "sums_"
N_TARGET = "target"
N_TOTAL = "total"
N_V = "v"
N_VECTORS = "vectors"
N_W = "w"

f32 = jnp.float32
bf16 = jnp.bfloat16


def up_to(rows, unit):
    return (rows + unit - 1) // unit * unit


class Env:
    pass


def cost_of(micros):
    return pl.CostEstimate(flops=int(micros * 1.15e9), bytes_accessed=0, transcendentals=0)


def launch(body, ins, outs, scratch=(), micros=0, swap=None, after=()):
    in_specs, operands, scratch_shapes, names = [], [], [], []
    loads = {}
    total_sems = 0
    positions = {}
    place = swap[0] if swap is not None else None
    for item in ins:
        name, array, kind = item[:3]
        positions[name] = len(operands)
        if kind == N_W:
            if len(array) > 2:
                place = array[0]
            operands += array[1:]
        else:
            operands.append(array)
        if kind == N_S:
            in_specs.append(pl.BlockSpec(memory_space=pltpu.SMEM))
        elif kind in (N_H, N_V):
            index, parts = item[3] if kind == N_H else ((), 1)
            in_specs.append(pl.BlockSpec(memory_space=pl.ANY))
            shape = array.shape[len(index) :]
            loads[name] = (N_H, index, parts, shape, total_sems)
            total_sems += parts
            names.append(name)
            scratch_shapes.append(pltpu.VMEM(shape, array.dtype))
        else:
            first, rows = item[3]
            in_specs += [pl.BlockSpec(memory_space=pl.ANY)] * (len(array) - 1)
            whole = len(array) == 2
            loads[name] = (N_W, first, rows, whole, total_sems)
            total_sems += BLOCKS
            names.append(name)
            scratch_shapes.append(pltpu.VMEM((rows, D), bf16))
    out_specs, out_shape = [], []
    flushes = {}
    out_sems = 0
    for name, shape, dtype, kind, parts in outs:
        out_shape.append(jax.ShapeDtypeStruct(shape, dtype))
        if kind == N_B:
            out_specs.append(pl.BlockSpec(memory_space=pltpu.VMEM))
        else:
            out_specs.append(pl.BlockSpec(memory_space=pl.ANY))
            flushes[name] = (parts, shape, out_sems)
            out_sems += parts
            if name not in names:
                names.append(name)
                scratch_shapes.append(pltpu.VMEM(shape, dtype))
    if swap is not None:
        for _ in range(BLOCKS):
            out_shape.append(jax.ShapeDtypeStruct((swap[1], BLOCK), f32))
            out_specs.append(pl.BlockSpec(memory_space=pl.ANY))
    place_at = len(operands)
    if place is not None:
        operands.append(place)
        in_specs.append(pl.BlockSpec(memory_space=pltpu.SMEM))
    for array in after:
        operands.append(array)
        in_specs.append(pl.BlockSpec(memory_space=pl.ANY))
    for name, shape, dtype in scratch:
        names.append(name)
        scratch_shapes.append(pltpu.VMEM(shape, dtype))
    scratch_shapes.append(pltpu.SemaphoreType.DMA((max(total_sems, 1),)))
    scratch_shapes.append(pltpu.SemaphoreType.DMA((max(out_sems, 1),)))
    if swap is not None:
        scratch_shapes.append(pltpu.SemaphoreType.DMA((BLOCKS, len(swap[2]) - 1)))

    def kernel(*refs):
        k = Env()
        out_refs = refs[len(operands) : len(operands) + len(out_shape)]
        rest = refs[len(operands) + len(out_shape) :]
        for name, ref in zip(names, rest):
            setattr(k, name, ref)
        sem_in, sem_out = rest[len(names) : len(names) + 2]
        sources, targets = {}, {}
        for item in ins:
            if item[2] == N_S:
                setattr(k, item[0], refs[positions[item[0]]])
            else:
                sources[item[0]] = positions[item[0]]
        for item, ref in zip(outs, out_refs):
            if item[3] == N_B:
                setattr(k, item[0], ref)
            else:
                targets[item[0]] = ref

        def load(name, part):
            kind, first, parts, shape, base = loads[name]
            src, dst = refs[sources[name]], getattr(k, name)
            if kind == N_H:
                for i in first:
                    src = src.at[i]
                if parts > 1:
                    step = shape[0] // parts
                    rows = pl.ds(pl.multiple_of(part * step, step), step)
                    src, dst = src.at[rows], dst.at[rows]
            else:
                if shape:
                    src = src.at[part, pl.ds(first, parts)]
                    column = part * BLOCK
                else:
                    src = refs[sources[name] + part].at[pl.ds(first, parts)]
                    column = lax.bitwise_xor(refs[place_at][0], part) * BLOCK
                    column = pl.multiple_of(column, BLOCK)
                dst = dst.at[:, pl.ds(column, BLOCK)]
            return pltpu.make_async_copy(src, dst, sem_in.at[base + part])

        def send(name, part):
            parts, shape, base = flushes[name]
            src, dst = getattr(k, name), targets[name]
            if parts > 1:
                step = shape[0] // parts
                rows = pl.ds(pl.multiple_of(part * step, step), step)
                src, dst = src.at[rows], dst.at[rows]
            return pltpu.make_async_copy(src, dst, sem_out.at[base + part])

        def wait(name, part=None):
            if name not in loads:
                return
            if part is not None:
                load(name, part).wait()
                return
            count = BLOCKS if loads[name][0] == N_W else loads[name][2]
            for i in range(count):
                load(name, i).wait()

        def flush(name, part=None):
            if part is not None:
                send(name, part).start()
                return
            for i in range(flushes[name][0]):
                send(name, i).start()

        def swap_copy(other, part):
            rows = pl.ds(swap[2][part], swap[2][part + 1] - swap[2][part])
            source = k.grads.at[lax.bitwise_xor(refs[place_at][0], other), rows]
            target = out_refs[len(outs) + other].at[rows]
            return pltpu.make_async_copy(source, target, rest[-1].at[other, part])

        def flush_swap(part=0):
            for other in range(BLOCKS):
                swap_copy(other, part).start()

        k.wait, k.flush, k.flush_swap = wait, flush, flush_swap
        for item in sorted(ins, key=lambda item: item[2] != N_V):
            if item[0] in loads:
                count = BLOCKS if item[2] == N_W else loads[item[0]][2]
                for i in range(count):
                    load(item[0], i).start()
        for item in ins:
            if item[2] == N_V:
                wait(item[0])
        body(k)
        for item in outs:
            if item[3] == N_V:
                flush(item[0])
        for name in flushes:
            for i in range(flushes[name][0]):
                send(name, i).wait()
        if swap is not None:
            for other in range(BLOCKS):
                for part in range(len(swap[2]) - 1):
                    swap_copy(other, part).wait()

    return pl.pallas_call(
        kernel,
        out_shape=out_shape,
        in_specs=in_specs,
        out_specs=out_specs,
        scratch_shapes=scratch_shapes,
        compiler_params=pltpu.CompilerParams(
            vmem_limit_bytes=56 * 2**20
        ),
        cost_estimate=cost_of(micros),
    )(*operands)


def dense(left, right):
    return jnp.dot(left, right, preferred_element_type=f32)


def dense_left(left, right):
    return lax.dot_general(left, right, (((0,), (0,)), ((), ())), preferred_element_type=f32)


def dense_right(left, right):
    return lax.dot_general(left, right, (((1,), (1,)), ((), ())), preferred_element_type=f32)


def halves(value):
    high = value.astype(bf16)
    return high, (value - high.astype(f32)).astype(bf16)


def rows_hot(column, width):
    spots = lax.broadcasted_iota(jnp.int32, (column.shape[0], width), 1)
    return jnp.where(column == spots, 1.0, 0.0).astype(bf16)


def cols_hot(row, height, first=0):
    spots = lax.broadcasted_iota(jnp.int32, (height, row.shape[1]), 0) + first
    return jnp.where(row == spots, 1.0, 0.0).astype(bf16)


def sigmoid(value):
    return 0.5 * jnp.tanh(0.5 * value) + 0.5


def normalise(mixed):
    centred = mixed - jnp.mean(mixed, -1, keepdims=True)
    inverse = lax.rsqrt(jnp.mean(centred * centred, -1, keepdims=True) + norm_eps)
    return centred * inverse, inverse


def vec(k, block, row):
    at = 3 * block + row
    return k.vectors[at : at + 1, :]


def row_tile(t, size):
    return pl.ds(pl.multiple_of(t * size, size), size)


def loop(count, step, most=1):
    unroll = max(n for n in range(1, most + 1) if count % n == 0)
    lax.fori_loop(0, count, lambda t, carry: (step(t), carry)[1], 0, unroll=unroll)


def forward_rows(k, block, hidden, inner):
    act = (hidden * sigmoid(hidden)).astype(bf16)
    normed, inverse = normalise(dense(act, inner))
    return normed * vec(k, block, 1) + vec(k, block, 2), normed, inverse


def backward_rows(k, block, upstream, hidden, normed, inverse, inner, sums, at):
    sums[at + 1 : at + 2, :] += jnp.sum(upstream * normed, 0, keepdims=True)
    sums[at + 2 : at + 3, :] += jnp.sum(upstream, 0, keepdims=True)
    scaled = upstream * vec(k, block, 1)
    d_mixed = inverse * (
        scaled
        - jnp.mean(scaled, -1, keepdims=True)
        - normed * jnp.mean(scaled * normed, -1, keepdims=True)
    )
    d_mixed = d_mixed.astype(bf16)
    sigma = sigmoid(hidden)
    act = (hidden * sigma).astype(bf16)
    d_act = dense_right(d_mixed, inner)
    d_hidden = (d_act * (sigma * (1.0 + hidden * (1.0 - sigma)))).astype(bf16)
    sums[at : at + 1, :] += jnp.sum(d_hidden.astype(f32), 0, keepdims=True)
    return act, d_mixed, d_hidden


def add_grad(k, first, value):
    rows = value.shape[0]
    for c in range(BLOCKS):
        k.grads[c, first : first + rows, :] += value[:, c * BLOCK : (c + 1) * BLOCK]


def set_grad(k, first, value):
    rows = value.shape[0]
    for c in range(BLOCKS):
        k.grads[c, first : first + rows, :] = value[:, c * BLOCK : (c + 1) * BLOCK]


def put_grad(k, fresh, first, value):
    (set_grad if fresh else add_grad)(k, first, value)


def weight_grad(k, fresh, first, left, right, pieces=2):
    width = left.shape[1]
    step = width // pieces
    for i in range(pieces):
        part = dense_left(left[:, i * step : (i + 1) * step], right[...])
        put_grad(k, fresh, first + i * step, part)


def start_sums(k, fresh):
    if fresh:
        k.sums[...] = jnp.zeros(k.sums.shape, f32)
    else:
        k.wait(N_SUMS)


def embed_forward(geometry, first, inner, at_inner, vectors):
    edges = geometry.shape[1]

    def body(k):
        k.wait(N_FIRST)
        k.wait(N_INNER)

        def tile(t):
            rows = row_tile(t, TILE)
            hidden = dense_left(k.geometry[:, rows], k.first[...]) + vec(k, 1, 0)
            k.hidden[rows] = hidden
            out, normed, inverse = forward_rows(k, 1, hidden, k.inner[...])
            k.normed[rows] = normed
            k.inverse[rows] = inverse
            k.edges[rows] = out
            k.edges_low[rows] = out.astype(bf16)
            for name in (N_HIDDEN, N_NORMED, N_INVERSE, N_EDGES, N_EDGES_LOW):
                k.flush(name, t)

        loop(edges // TILE, tile)

    parts = edges // TILE
    return launch(
        body,
        [
            (N_GEOMETRY, geometry, N_V),
            (N_VECTORS, vectors, N_V),
            (N_FIRST,) + first,
            (N_INNER,) + inner,
        ],
        [
            (N_EDGES, (edges, D), f32, N_H, parts),
            (N_EDGES_LOW, (edges, D), bf16, N_H, parts),
            (N_HIDDEN, (edges, D), f32, N_H, parts),
            (N_NORMED, (edges, D), f32, N_H, parts),
            (N_INVERSE, (edges, 1), f32, N_H, parts),
        ],
        micros=5,
    )


def encoder_forward(state, means, scales, first, inner, vectors, assign, picks):
    depth, grid = state.shape
    out_rows = picks.shape[0]

    def body(k):
        k.wait(N_STATE)
        k.feats[...] = ((k.state[...] - k.means[...]) / k.scales[...]).astype(bf16)
        k.flush(N_FEATS)
        k.wait(N_FIRST)
        k.wait(N_INNER)

        def tile(t):
            rows = row_tile(t, TILE)
            hidden = dense_left(k.feats[:, rows], k.first[...]) + vec(k, 0, 0)
            k.hidden[rows] = hidden
            out, normed, inverse = forward_rows(k, 0, hidden, k.inner[...])
            k.normed[rows] = normed
            k.inverse[rows] = inverse
            k.latent[rows] = out
            k.low[rows] = out.astype(bf16)
            for name in (N_HIDDEN, N_NORMED, N_INVERSE, N_LATENT, N_LOW):
                k.flush(name, t)

        loop(grid // TILE, tile)
        nodes = dense(cols_hot(k.assign[...], NODE_CAP), k.low[...])
        k.nodes[...] = nodes
        k.node_low[...] = nodes.astype(bf16)
        k.outgoing[...] = dense(rows_hot(k.picks[...], NODE_CAP), k.node_low[...]).astype(bf16)

    parts = grid // TILE
    return launch(
        body,
        [
            (N_STATE, state, N_H, ((), 1)),
            ("means", means, N_V),
            (N_SCALES, scales, N_V),
            (N_ASSIGN, assign, N_V),
            (N_PICKS, picks, N_V),
            (N_VECTORS, vectors, N_V),
            (N_FIRST,) + first,
            (N_INNER,) + inner,
        ],
        [
            (N_NODES, (NODE_CAP, D), f32, N_V, 1),
            (N_NODE_LOW, (NODE_CAP, D), bf16, N_V, 1),
            (N_OUTGOING, (out_rows, D), bf16, N_V, 1),
            (N_LATENT, (grid, D), f32, N_H, parts),
            (N_LOW, (grid, D), bf16, N_H, parts),
            (N_FEATS, (depth, grid), bf16, N_H, 1),
            (N_HIDDEN, (grid, D), f32, N_H, parts),
            (N_NORMED, (grid, D), f32, N_H, parts),
            (N_INVERSE, (grid, 1), f32, N_H, parts),
        ],
        micros=5,
    )


def layer_local(layer, edges_low, node_low, edge_first, vectors, send, recv):
    count = edges_low.shape[0]
    at = 2 + layer

    def body(k):
        k.wait(N_EDGE_FIRST)

        def tile(t):
            rows = row_tile(t, TILE)
            sent = dense(rows_hot(k.send[rows], NODE_CAP), k.node_low[...]).astype(bf16)
            got = dense(rows_hot(k.recv[rows], NODE_CAP), k.node_low[...]).astype(bf16)
            k.wait(N_EDGES_LOW, t)
            joined = jnp.concatenate([k.edges_low[rows], sent, got], 1)
            k.local[rows] = dense(joined, k.edge_first[...]) + vec(k, at, 0)
            k.flush(N_LOCAL, t)

        loop(count // TILE, tile)

    parts = count // TILE
    return launch(
        body,
        [
            (N_NODE_LOW, node_low, N_V),
            (N_SEND, send, N_V),
            (N_RECV, recv, N_V),
            (N_VECTORS, vectors, N_V),
            (N_EDGE_FIRST,) + edge_first,
            (N_EDGES_LOW, edges_low, N_H, ((), parts)),
        ],
        [(N_LOCAL, (count, D), f32, N_H, parts)],
        micros=8,
    )[0]


def layer_forward(
    layer, local, edges, nodes, node_low, halo, weights, vectors, send, recv_row, picks, last
):
    count = edges.shape[0]
    halo_rows = halo.shape[0]
    from_send, edge_inner, node_first, node_inner = weights
    at_edge, at_node = 2 + layer, 2 + LAYERS + layer

    def body(k):
        k.wait(N_FROM_SEND)
        high, rest = halves(dense(k.halo[...], k.from_send[...]))
        k.table[:, 0:D] = high
        k.table[:, D : 2 * D] = rest
        k.wait(N_EDGE_INNER)

        def tile(t):
            rows = row_tile(t, TILE)
            both = dense(rows_hot(k.send[rows] - NODE_CAP, halo_rows), k.table[...])
            k.wait(N_HIDDEN, t)
            hidden = k.hidden[rows] + (both[:, 0:D] + both[:, D : 2 * D])
            k.hidden[rows] = hidden
            out, normed, inverse = forward_rows(k, at_edge, hidden, k.edge_inner[...])
            k.normed[rows] = normed
            k.inverse[rows] = inverse
            k.wait(N_EDGES, t)
            edge = k.edges[rows] + out
            k.edges[rows] = edge
            high, rest = halves(edge)
            k.edges_low[rows] = high
            k.rest[rows] = rest
            for name in (N_HIDDEN, N_NORMED, N_INVERSE):
                k.flush(name, t)
            if not last:
                k.flush(N_EDGES, t)
                k.flush(N_EDGES_LOW, t)

        loop(count // TILE, tile)
        k.wait(N_NODE_FIRST)
        k.wait(N_NODE_INNER)
        k.wait(N_NODES)

        def node_tile(t):
            rows = row_tile(t, TILE)
            hot = cols_hot(k.recv_row[...], TILE, t * TILE)
            total = (dense(hot, k.edges_low[...]) + dense(hot, k.rest[...])).astype(bf16)
            k.total[rows] = total
            node_in = jnp.concatenate([k.node_low[rows], total], 1)
            hidden = dense(node_in, k.node_first[...]) + vec(k, at_node, 0)
            k.node_hidden[rows] = hidden
            out, normed, inverse = forward_rows(k, at_node, hidden, k.node_inner[...])
            k.node_normed[rows] = normed
            k.node_inverse[rows] = inverse
            node = k.nodes[rows] + out
            k.nodes[rows] = node
            k.new_low[rows] = node.astype(bf16)
            for name in (N_TOTAL, N_NODE_HIDDEN, N_NODE_NORMED, N_NODE_INVERSE):
                k.flush(name, t)
            if not last:
                k.flush(N_NODES, t)

        loop(NODE_CAP // TILE, node_tile)
        if not last:
            k.outgoing[...] = dense(rows_hot(k.picks[...], NODE_CAP), k.new_low[...]).astype(bf16)

    parts = count // TILE
    node_parts = NODE_CAP // TILE
    ins = [
        (N_NODE_LOW, node_low, N_V),
        (N_HALO, halo, N_V),
        (N_SEND, send, N_V),
        (N_RECV_ROW, recv_row, N_V),
        (N_VECTORS, vectors, N_V),
        (N_FROM_SEND,) + from_send,
        (N_EDGE_INNER,) + edge_inner,
        (N_HIDDEN, local, N_H, ((), parts)),
        (N_EDGES, edges, N_H, ((), parts)),
        (N_NODE_FIRST,) + node_first,
        (N_NODE_INNER,) + node_inner,
        (N_NODES, nodes, N_H, ((), 1)),
    ]
    outs = [
        ("new_low", (NODE_CAP, D), bf16, N_V, 1),
        (N_HIDDEN, (count, D), f32, N_H, parts),
        (N_NORMED, (count, D), f32, N_H, parts),
        (N_INVERSE, (count, 1), f32, N_H, parts),
        (N_TOTAL, (NODE_CAP, D), bf16, N_H, node_parts),
        (N_NODE_HIDDEN, (NODE_CAP, D), f32, N_H, node_parts),
        (N_NODE_NORMED, (NODE_CAP, D), f32, N_H, node_parts),
        (N_NODE_INVERSE, (NODE_CAP, 1), f32, N_H, node_parts),
    ]
    scratch = [("table", (halo_rows, 2 * D), bf16), ("rest", (count, D), bf16)]
    if last:
        scratch.append((N_EDGES_LOW, (count, D), bf16))
    else:
        ins.append((N_PICKS, picks, N_V))
        outs += [
            (N_EDGES, (count, D), f32, N_H, parts),
            (N_NODES, (NODE_CAP, D), f32, N_H, node_parts),
            (N_OUTGOING, (halo_rows, D), bf16, N_V, 1),
            (N_EDGES_LOW, (count, D), bf16, N_H, parts),
        ]
    out = launch(body, ins, outs, scratch, micros=13)
    kept = {
        N_NODE_LOW: node_low,
        N_HALO: halo,
        N_HIDDEN: out[1],
        N_NORMED: out[2],
        N_INVERSE: out[3],
        N_TOTAL: out[4],
        N_NODE_HIDDEN: out[5],
        N_NODE_NORMED: out[6],
        N_NODE_INVERSE: out[7],
    }
    if last:
        return None, None, None, out[0], None, kept
    return out[8], out[11], out[9], out[0], out[10], kept


def decoder_forward(
    step, state, target, latent, low, node_low, weights, vectors, assign, delta, area, plan
):
    depth, grid = state.shape
    first, inner, head = weights
    at = 2 + 2 * LAYERS

    def body(k):
        k.wait(N_FIRST)
        k.wait(N_INNER)

        def tile(t):
            rows = row_tile(t, TILE)
            k.wait(N_LOW, t)
            got = dense(rows_hot(k.assign[rows], NODE_CAP), k.node_low[...]).astype(bf16)
            joined = jnp.concatenate([k.low[rows], got], 1)
            hidden = dense(joined, k.first[...]) + vec(k, at, 0)
            k.hidden[rows] = hidden
            out, normed, inverse = forward_rows(k, at, hidden, k.inner[...])
            k.normed[rows] = normed
            k.inverse[rows] = inverse
            k.wait(N_LATENT, t)
            k.final[rows] = (k.latent[rows] + out).astype(bf16)
            for name in (N_HIDDEN, N_NORMED, N_INVERSE, N_FINAL):
                k.flush(name, t)

        loop(grid // TILE, tile)
        k.wait(N_HEAD)
        k.wait(N_STATE)
        k.wait(N_TARGET)
        update = dense_right(k.head[...], k.final[...])
        new_state = k.state[...] + k.delta[...] * update
        k.new_state[...] = new_state
        miss = (new_state - k.target[...]) / k.delta[...]
        k.miss[...] = miss
        weight = k.plan[step].astype(f32)
        k.loss[...] = weight * jnp.sum(k.area[...] * miss * miss, keepdims=True)

    parts = grid // TILE
    out = launch(
        body,
        [
            (N_NODE_LOW, node_low, N_V),
            (N_ASSIGN, assign, N_V),
            (N_VECTORS, vectors, N_V),
            (N_DELTA, delta, N_V),
            (N_AREA, area, N_V),
            (N_PLAN, plan, N_S),
            (N_FIRST,) + first,
            (N_LOW, low, N_H, ((), parts)),
            (N_INNER,) + inner,
            (N_LATENT, latent, N_H, ((), parts)),
            (N_HEAD,) + head,
            (N_STATE, state, N_H, ((), 1)),
            (N_TARGET, target, N_H, ((step,), 1)),
        ],
        [
            ("new_state", (depth, grid), f32, N_V, 1),
            (N_MISS, (depth, grid), f32, N_V, 1),
            ("loss", (1, 1), f32, N_B, 1),
            (N_HIDDEN, (grid, D), f32, N_H, parts),
            (N_NORMED, (grid, D), f32, N_H, parts),
            (N_INVERSE, (grid, 1), f32, N_H, parts),
            (N_FINAL, (grid, D), bf16, N_H, parts),
        ],
        micros=7,
    )
    kept = {
        N_MISS: out[1],
        N_HIDDEN: out[3],
        N_NORMED: out[4],
        N_INVERSE: out[5],
        N_FINAL: out[6],
        N_LOW: low,
        N_NODE_LOW: node_low,
    }
    return out[0], out[2], kept


def grads_io(outs, scratch, grads, rows, swap):
    shape = (BLOCKS, rows, BLOCK)
    if swap is None:
        outs.append((N_GRADS, shape, f32, N_H, BLOCKS))
    elif grads is None:
        scratch.append((N_GRADS, shape, f32))


def flush_grads(k, swap):
    if swap is None:
        k.flush(N_GRADS)
    else:
        k.flush_swap()


def decoder_backward(
    step, regions, d_state, kept, weights, vectors, assign_row, delta, area, plan, inverse_total, grads, sums,
    swap,
):
    miss = kept[N_MISS]
    depth, grid = miss.shape
    first, inner, head = weights
    at = 2 + 2 * LAYERS
    fresh = grads is None
    more = d_state is not None
    keep_state = step > 0
    rows_all = up_to(3 * D + depth, CODED * regions)

    def body(k):
        k.wait(N_MISS)
        coefficient = 2.0 * k.inverse_total[0, 0] * k.plan[step].astype(f32)
        d_next = coefficient * k.area[...] * k.miss[...] / k.delta[...]
        if more:
            k.wait(N_D_STATE)
            d_next = k.d_state[...] + d_next
        if keep_state:
            k.d_next[...] = d_next
            k.flush(N_D_NEXT)
        k.d_update[...] = (d_next * k.delta[...]).astype(bf16)
        start_sums(k, fresh)
        k.wait(N_HEAD)
        k.wait(N_INNER)
        k.wait(N_FIRST)

        def tile(t):
            rows = row_tile(t, TILE)
            for name in (N_HIDDEN, N_NORMED, N_INVERSE):
                k.wait(name, t)
            d_final = dense_left(k.d_update[:, rows], k.head[...])
            act, d_mixed, d_hidden = backward_rows(
                k, at, d_final, k.hidden[rows], k.normed[rows], k.inverse[rows],
                k.inner[...], k.sums, 0,
            )
            k.act[rows] = act
            k.d_mixed[rows] = d_mixed
            k.d_hidden[rows] = d_hidden
            k.d_grid[rows] = d_final + dense_right(d_hidden, k.first[0:D])
            k.flush(N_D_GRID, t)

        loop(grid // TILE, tile)
        k.flush(N_SUMS)
        gathered = dense(cols_hot(k.assign_row[...], NODE_CAP), k.d_hidden[...])
        high, rest = halves(gathered)
        k.d_nodes[...] = dense_right(high, k.first[D : 2 * D]) + dense_right(rest, k.first[D : 2 * D])
        if not fresh:
            k.wait(N_GRADS)
        k.wait(N_LOW)
        k.wait(N_FINAL)
        weight_grad(k, fresh, 0, k.low, k.d_hidden)
        put_grad(k, fresh, D, dense_left(k.node_low[...], high) + dense_left(k.node_low[...], rest))
        weight_grad(k, fresh, 2 * D, k.act, k.d_mixed)
        put_grad(k, fresh, 3 * D, dense(k.d_update[...], k.final[...]))
        if fresh and rows_all > 3 * D + depth:
            k.grads[:, 3 * D + depth :, :] = jnp.zeros(
                (BLOCKS, rows_all - 3 * D - depth, BLOCK), f32
            )
        flush_grads(k, swap)

    parts = grid // TILE
    ins = [
        (N_MISS, miss, N_H, ((), 1)),
        (N_AREA, area, N_V),
        (N_DELTA, delta, N_V),
        ("assign_row", assign_row, N_V),
        (N_VECTORS, vectors, N_V),
        (N_NODE_LOW, kept[N_NODE_LOW], N_V),
        (N_PLAN, plan, N_S),
        ("inverse_total", inverse_total, N_S),
    ]
    if more:
        ins.append((N_D_STATE, d_state, N_H, ((), 1)))
    ins += [
        (N_HEAD,) + head,
        (N_HIDDEN, kept[N_HIDDEN], N_H, ((), parts)),
        (N_NORMED, kept[N_NORMED], N_H, ((), parts)),
        (N_INVERSE, kept[N_INVERSE], N_H, ((), parts)),
        (N_INNER,) + inner,
        (N_FIRST,) + first,
        (N_LOW, kept[N_LOW], N_H, ((), 1)),
        (N_FINAL, kept[N_FINAL], N_H, ((), 1)),
    ]
    outs = [
        (N_D_NODES, (NODE_CAP, D), f32, N_V, 1),
        (N_D_GRID, (grid, D), f32, N_H, parts),
    ]
    if keep_state:
        outs.append((N_D_NEXT, (depth, grid), f32, N_H, 1))
    scratch = [
        ("d_update", (depth, grid), bf16),
        (N_ACT, (grid, D), bf16),
        (N_D_MIXED, (grid, D), bf16),
        (N_D_HIDDEN, (grid, D), bf16),
    ]
    if not fresh:
        ins += [(N_SUMS, sums, N_H, ((), 1)), (N_GRADS, grads, N_H, ((), BLOCKS))]
    outs.append((N_SUMS, (8, D), f32, N_H, 1))
    grads_io(outs, scratch, grads, rows_all, swap)
    out = launch(
        body, ins, outs, scratch, micros=13, swap=swap
    )
    if keep_state:
        return out[0], out[1], out[2], out[3], out[4:]
    return out[0], out[1], None, out[2], out[3:]


def layer_backward(
    layer, d_nodes, returned, d_edges, kept, weights, vectors, send_row, recv, picks_row,
    sums, after,
):
    count = kept[N_HIDDEN].shape[0]
    halo_rows = kept[N_HALO].shape[0]
    edge_first, edge_inner, node_first, node_inner = weights
    at_edge, at_node = 2 + layer, 2 + LAYERS + layer
    top = d_edges is None

    def body(k):
        start_sums(k, sums is None)
        k.wait(N_D_NODES)
        if not top:
            high, rest = halves(k.returned[...])
            hot = cols_hot(k.picks_row[...], NODE_CAP)
            k.d_nodes[...] += dense(hot, high) + dense(hot, rest)
        for name in (N_NODE_HIDDEN, N_NODE_NORMED, N_NODE_INVERSE, N_NODE_INNER, N_NODE_FIRST):
            k.wait(name)

        def node_tile(t):
            rows = row_tile(t, TILE)
            act, d_mixed, d_hidden = backward_rows(
                k, at_node, k.d_nodes[rows], k.node_hidden[rows], k.node_normed[rows],
                k.node_inverse[rows], k.node_inner[...], k.sums, 3,
            )
            k.node_act[rows] = act
            k.node_d_mixed[rows] = d_mixed
            k.node_d_hidden[rows] = d_hidden
            d_in = dense_right(d_hidden, k.node_first[...])
            k.d_nodes[rows] += d_in[:, 0:D]
            high, rest = halves(d_in[:, D : 2 * D])
            k.d_total[rows, 0:D] = high
            k.d_total[rows, D : 2 * D] = rest

        loop(NODE_CAP // TILE, node_tile)
        for name in (N_D_NODES, N_NODE_ACT, N_NODE_D_MIXED, N_NODE_D_HIDDEN):
            k.flush(name)
        k.wait(N_EDGE_INNER)
        k.wait(N_EDGE_FIRST)

        def tile(t):
            rows = row_tile(t, TILE)
            both = dense(rows_hot(k.recv[rows], NODE_CAP), k.d_total[...])
            upstream = both[:, 0:D] + both[:, D : 2 * D]
            if not top:
                k.wait(N_D_EDGES, t)
                upstream = k.d_edges[rows] + upstream
            for name in (N_HIDDEN, N_NORMED, N_INVERSE):
                k.wait(name, t)
            act, d_mixed, d_hidden = backward_rows(
                k, at_edge, upstream, k.hidden[rows], k.normed[rows], k.inverse[rows],
                k.edge_inner[...], k.sums, 0,
            )
            k.act[rows] = act
            k.d_mixed[rows] = d_mixed
            k.d_hidden[rows] = d_hidden
            k.d_edges[rows] = upstream + dense_right(d_hidden, k.edge_first[0:D])
            for name in (N_ACT, N_D_MIXED, N_D_HIDDEN, N_D_EDGES):
                k.flush(name, t)

        loop(count // TILE, tile)
        k.flush(N_SUMS)
        to_halo = dense(cols_hot(k.send_row[...], halo_rows, NODE_CAP), k.d_hidden[...])
        high, rest = halves(to_halo)
        from_send = k.edge_first[D : 2 * D]
        k.d_halo[...] = dense_right(high, from_send) + dense_right(rest, from_send)
        k.halo_high[...] = high
        k.halo_rest[...] = rest

    parts = count // TILE
    ins = [
        (N_RECV, recv, N_V),
        (N_SEND_ROW, send_row, N_V),
        (N_VECTORS, vectors, N_V),
    ]
    if not top:
        ins += [(N_RETURNED, returned, N_V), (N_PICKS_ROW, picks_row, N_V)]
    ins += [
        (N_D_NODES, d_nodes, N_H, ((), 1)),
        (N_NODE_HIDDEN, kept[N_NODE_HIDDEN], N_H, ((), 1)),
        (N_NODE_NORMED, kept[N_NODE_NORMED], N_H, ((), 1)),
        (N_NODE_INVERSE, kept[N_NODE_INVERSE], N_H, ((), 1)),
        (N_NODE_INNER,) + node_inner,
        (N_NODE_FIRST,) + node_first,
        (N_EDGE_INNER,) + edge_inner,
        (N_EDGE_FIRST,) + edge_first,
    ]
    if sums is not None:
        ins.append((N_SUMS, sums, N_H, ((), 1)))
    if not top:
        ins.append((N_D_EDGES, d_edges, N_H, ((), parts)))
    ins += [
        (N_HIDDEN, kept[N_HIDDEN], N_H, ((), parts)),
        (N_NORMED, kept[N_NORMED], N_H, ((), parts)),
        (N_INVERSE, kept[N_INVERSE], N_H, ((), parts)),
    ]
    outs = [
        (N_D_HALO, (halo_rows, D), f32, N_V, 1),
        (N_HALO_HIGH, (halo_rows, D), bf16, N_V, 1),
        (N_HALO_REST, (halo_rows, D), bf16, N_V, 1),
        (N_D_NODES, (NODE_CAP, D), f32, N_H, 1),
        (N_NODE_ACT, (NODE_CAP, D), bf16, N_H, 1),
        (N_NODE_D_MIXED, (NODE_CAP, D), bf16, N_H, 1),
        (N_NODE_D_HIDDEN, (NODE_CAP, D), bf16, N_H, 1),
        (N_ACT, (count, D), bf16, N_H, parts),
        (N_D_MIXED, (count, D), bf16, N_H, parts),
        (N_D_HIDDEN, (count, D), bf16, N_H, parts),
        (N_D_EDGES, (count, D), f32, N_H, parts),
        (N_SUMS, (8, D), f32, N_H, 1),
    ]
    scratch = [("d_total", (NODE_CAP, 2 * D), bf16)]
    out = launch(body, ins, outs, scratch, micros=14, after=after)
    names = [item[0] for item in outs]
    return dict(zip(names, out))


def layer_grads(found, kept, edge_first, send_row, recv_row, rows_all, grads, swap, after):
    count = kept[N_HIDDEN].shape[0]
    halo_rows = kept[N_HALO].shape[0]
    fresh = grads is None

    def body(k):
        k.wait(N_D_HIDDEN)
        k.wait(N_FROM_SEND)
        k.wait(N_FROM_RECV)
        to_recv = dense(cols_hot(k.recv_row[...], NODE_CAP), k.d_hidden[...])
        to_send = dense(cols_hot(k.send_row[...], NODE_CAP), k.d_hidden[...])
        recv_high, recv_rest = halves(to_recv)
        send_high, send_rest = halves(to_send)
        from_send, from_recv = k.from_send[...], k.from_recv[...]
        k.wait(N_D_NODES)
        k.d_nodes[...] += (
            dense_right(send_high, from_send)
            + dense_right(send_rest, from_send)
            + dense_right(recv_high, from_recv)
            + dense_right(recv_rest, from_recv)
        )
        k.flush(N_D_NODES)
        if not fresh:
            k.wait(N_GRADS)
        low = k.node_low[...]
        put_grad(
            k, fresh, D,
            dense_left(low, send_high)
            + dense_left(low, send_rest)
            + dense_left(k.halo[...], k.halo_high[...])
            + dense_left(k.halo[...], k.halo_rest[...]),
        )
        put_grad(k, fresh, 2 * D, dense_left(low, recv_high) + dense_left(low, recv_rest))
        k.wait(N_EDGES_LOW)
        weight_grad(k, fresh, 0, k.edges_low, k.d_hidden)
        k.wait(N_ACT)
        k.wait(N_D_MIXED)
        weight_grad(k, fresh, 3 * D, k.act, k.d_mixed)
        if swap is not None:
            k.flush_swap(0)
        k.wait(N_TOTAL)
        k.wait(N_NODE_D_HIDDEN)
        weight_grad(k, fresh, 4 * D, k.node_low, k.node_d_hidden)
        weight_grad(k, fresh, 5 * D, k.total, k.node_d_hidden)
        k.wait(N_NODE_ACT)
        k.wait(N_NODE_D_MIXED)
        weight_grad(k, fresh, 6 * D, k.node_act, k.node_d_mixed)
        if fresh and rows_all > 7 * D:
            k.grads[:, 7 * D :, :] = jnp.zeros((BLOCKS, rows_all - 7 * D, BLOCK), f32)
        if swap is None:
            k.flush(N_GRADS)
        else:
            k.flush_swap(1)

    source, _, (first, _) = edge_first
    ins = [
        (N_NODE_LOW, kept[N_NODE_LOW], N_V),
        (N_HALO, kept[N_HALO], N_V),
        (N_HALO_HIGH, found[N_HALO_HIGH], N_V),
        (N_HALO_REST, found[N_HALO_REST], N_V),
        (N_RECV_ROW, recv_row, N_V),
        (N_SEND_ROW, send_row, N_V),
        (N_D_HIDDEN, found[N_D_HIDDEN], N_H, ((), 1)),
        (N_FROM_SEND, source, N_W, (first + D, D)),
        (N_FROM_RECV, source, N_W, (first + 2 * D, D)),
        (N_D_NODES, found[N_D_NODES], N_H, ((), 1)),
    ]
    if not fresh:
        ins.append((N_GRADS, grads, N_H, ((), BLOCKS)))
    ins += [
        (N_EDGES_LOW, kept[N_EDGES_LOW], N_H, ((), 1)),
        (N_ACT, found[N_ACT], N_H, ((), 1)),
        (N_D_MIXED, found[N_D_MIXED], N_H, ((), 1)),
        (N_TOTAL, kept[N_TOTAL], N_H, ((), 1)),
        (N_NODE_D_HIDDEN, found[N_NODE_D_HIDDEN], N_H, ((), 1)),
        (N_NODE_ACT, found[N_NODE_ACT], N_H, ((), 1)),
        (N_NODE_D_MIXED, found[N_NODE_D_MIXED], N_H, ((), 1)),
    ]
    outs = [(N_D_NODES, (NODE_CAP, D), f32, N_H, 1)]
    scratch = []
    grads_io(outs, scratch, grads, rows_all, swap)
    out = launch(body, ins, outs, scratch, micros=14, swap=swap, after=after)
    return out[0], out[1:]


def encoder_backward(
    step, d_grid, d_nodes, returned, d_next, kept, weights, vectors, assign, picks_row, scales,
    grads, sums, others, swap, after,
):
    feats = kept[N_FEATS]
    depth, grid = feats.shape
    first, inner = weights
    fresh = grads is None
    keep_state = step > 0
    rows_all = depth + D
    if others is not None:
        embed_grads, all_sums = others
        embed_rows = embed_grads.shape[1]
        at_vectors = depth + D + embed_rows
        rows_all = swap[1]

    def body(k):
        start_sums(k, fresh)
        k.wait(N_D_NODES)
        high, rest = halves(k.returned[...])
        hot = cols_hot(k.picks_row[...], NODE_CAP)
        nodes = k.d_nodes[...] + dense(hot, high) + dense(hot, rest)
        high, rest = halves(nodes)
        k.both[:, 0:D] = high
        k.both[:, D : 2 * D] = rest
        k.wait(N_INNER)

        def tile(t):
            rows = row_tile(t, TILE)
            for name in (N_HIDDEN, N_NORMED, N_INVERSE, N_D_GRID):
                k.wait(name, t)
            both = dense(rows_hot(k.assign[rows], NODE_CAP), k.both[...])
            upstream = k.d_grid[rows] + both[:, 0:D] + both[:, D : 2 * D]
            act, d_mixed, d_hidden = backward_rows(
                k, 0, upstream, k.hidden[rows], k.normed[rows], k.inverse[rows],
                k.inner[...], k.sums, 0,
            )
            k.act[rows] = act
            k.d_mixed[rows] = d_mixed
            k.d_hidden[rows] = d_hidden

        loop(grid // TILE, tile)
        if keep_state:
            k.wait(N_FIRST)
            k.wait(N_D_NEXT)
            k.d_state[...] = (
                k.d_next[...] + dense_right(k.first[...], k.d_hidden[...]) / k.scales[...]
            )
            k.flush(N_D_STATE)
        k.wait(N_FEATS)
        if others is None:
            k.flush(N_SUMS)
            put_grad(k, True, 0, dense(k.feats[...], k.d_hidden[...]))
            weight_grad(k, True, depth, k.act, k.d_mixed)
            k.flush(N_GRADS)
            return
        k.wait(N_BEFORE)
        k.grads[:, 0 : depth + D, :] = k.before[...]
        put_grad(k, False, 0, dense(k.feats[...], k.d_hidden[...]))
        weight_grad(k, False, depth, k.act, k.d_mixed)
        k.wait(N_EMBED_GRADS)
        k.grads[:, depth + D : at_vectors, :] = k.embed_grads[...]
        k.grads[:, at_vectors:, :] = jnp.zeros((BLOCKS, rows_all - at_vectors, BLOCK), f32)
        sources = [(k.sums, 0), (k.sums_embed, 0)]
        sources += [(getattr(k, N_SUMS_ + str(l)), 0) for l in range(LAYERS)]
        sources += [(getattr(k, N_SUMS_ + str(l)), 3) for l in range(LAYERS)]
        sources += [(k.sums_dec, 0)]
        for i, (source, at) in enumerate(sources):
            set_grad(k, at_vectors + 3 * i, source[at : at + 3, :])
        k.flush_swap()

    parts = grid // TILE
    ins = [
        (N_RETURNED, returned, N_V),
        (N_PICKS_ROW, picks_row, N_V),
        (N_ASSIGN, assign, N_V),
        (N_SCALES, scales, N_V),
        (N_VECTORS, vectors, N_V),
        (N_D_NODES, d_nodes, N_H, ((), 1)),
        (N_INNER,) + inner,
        (N_D_GRID, d_grid, N_H, ((), parts)),
        (N_HIDDEN, kept[N_HIDDEN], N_H, ((), parts)),
        (N_NORMED, kept[N_NORMED], N_H, ((), parts)),
        (N_INVERSE, kept[N_INVERSE], N_H, ((), parts)),
        (N_FEATS, feats, N_H, ((), 1)),
    ]
    outs = []
    if keep_state:
        ins += [(N_FIRST,) + first, (N_D_NEXT, d_next, N_H, ((), 1))]
        outs.append((N_D_STATE, (depth, grid), f32, N_H, 1))
    scratch = [
        ("both", (NODE_CAP, 2 * D), bf16),
        (N_ACT, (grid, D), bf16),
        (N_D_MIXED, (grid, D), bf16),
        (N_D_HIDDEN, (grid, D), bf16),
    ]
    if not fresh:
        ins.append((N_SUMS, sums, N_H, ((), 1)))
    if others is None:
        outs.append((N_SUMS, (8, D), f32, N_H, 1))
        outs.append((N_GRADS, (BLOCKS, rows_all, BLOCK), f32, N_H, BLOCKS))
    else:
        ins.append((N_BEFORE, grads, N_H, ((), BLOCKS)))
        ins.append((N_EMBED_GRADS, embed_grads, N_H, ((), BLOCKS)))
        ins += [(N_SUMS_ + str(name), value, N_V) for name, value in all_sums.items()]
        scratch.append((N_GRADS, (BLOCKS, rows_all, BLOCK), f32))
    out = launch(body, ins, outs, scratch, micros=10, swap=swap, after=after)
    if others is not None:
        return out
    return out if keep_state else (None, out[0], out[1])


def embed_backward(d_first, d_second, kept, geometry, inner, vectors, after):
    count = kept[N_HIDDEN].shape[0]
    features = geometry.shape[0]

    def body(k):
        start_sums(k, True)
        k.wait(N_INNER)

        def tile(t):
            rows = row_tile(t, TILE)
            for name in (N_D_FIRST, N_D_SECOND, N_HIDDEN, N_NORMED, N_INVERSE):
                k.wait(name, t)
            act, d_mixed, d_hidden = backward_rows(
                k, 1, k.d_first[rows] + k.d_second[rows], k.hidden[rows], k.normed[rows],
                k.inverse[rows], k.inner[...], k.sums, 0,
            )
            k.act[rows] = act
            k.d_mixed[rows] = d_mixed
            k.d_hidden[rows] = d_hidden

        loop(count // TILE, tile)
        k.flush(N_SUMS)
        set_grad(k, 0, dense(k.geometry[...], k.d_hidden[...]))
        weight_grad(k, True, features, k.act, k.d_mixed)
        k.flush(N_GRADS)

    parts = count // TILE
    ins = [
        (N_GEOMETRY, geometry, N_V),
        (N_VECTORS, vectors, N_V),
        (N_INNER,) + inner,
        (N_D_FIRST, d_first, N_H, ((), parts)),
        (N_D_SECOND, d_second, N_H, ((), parts)),
        (N_HIDDEN, kept[N_HIDDEN], N_H, ((), parts)),
        (N_NORMED, kept[N_NORMED], N_H, ((), parts)),
        (N_INVERSE, kept[N_INVERSE], N_H, ((), parts)),
    ]
    return launch(
        body,
        ins,
        [
            (N_SUMS, (8, D), f32, N_H, 1),
            (N_GRADS, (BLOCKS, features + D, BLOCK), f32, N_H, BLOCKS),
        ],
        [
            (N_ACT, (count, D), bf16),
            (N_D_MIXED, (count, D), bf16),
            (N_D_HIDDEN, (count, D), bf16),
        ],
        micros=11,
        after=after,
    )


def coded_rows(rows):
    return rows + up_to(rows // CODED, 16)


def encode(source, first, rows, target, scale):
    scale[...] = jnp.zeros(scale.shape, f32)

    def step(t):
        value = source[pl.ds(pl.multiple_of(first + t * CODED, CODED), CODED)]
        top = jnp.maximum(jnp.max(jnp.abs(value), 0, keepdims=True), 1e-30)
        exponent = jnp.ceil(jnp.log2(top))
        scale[pl.ds(t, 1), :] = exponent
        value = jnp.round(value * (CODE_TOP * jnp.exp2(-exponent)))
        target[row_tile(t, CODED)] = value.astype(jnp.int32).astype(jnp.int16)

    loop(rows // CODED, step, 8)
    more = coded_rows(rows) - rows
    target[rows : rows + more] = scale[0:more].astype(jnp.int32).astype(jnp.int16)


def scales_of(coded, rows, scale):
    more = coded_rows(rows) - rows
    exponent = coded[rows : rows + more].astype(jnp.int32).astype(f32)
    scale[0:more] = jnp.exp2(exponent) * (1.0 / CODE_TOP)


def decoded(coded, scale, t):
    return coded[row_tile(t, CODED)].astype(jnp.int32).astype(f32) * scale[pl.ds(t, 1), :]


def difference(p, order):
    return sum(bit for i, bit in enumerate(reversed(order)) if p >> i & 1)


CORES, OVER_X, TURN, JOIN, ALL = range(5)


def combine(jobs, order, place, after):
    regions = 2 ** len(order)
    operands, out_shape, scratch_shapes, plans = [], [], [], []
    squares = False

    def buffer(shape, dtype):
        scratch_shapes.append(pltpu.VMEM(shape, dtype))
        return len(scratch_shapes) - 1

    def output(shape, dtype):
        out_shape.append(jax.ShapeDtypeStruct(shape, dtype))
        return len(out_shape) - 1

    for kind, arrays, ways in jobs:
        loads, stores = [], []
        for array in arrays:
            loads.append((len(operands), buffer(array.shape, array.dtype)))
            operands.append(array)
        blocks, size = 1, 0
        if kind == CORES:
            size = arrays[0].shape[0]
            stores.append((output((size, BLOCK), f32), loads[0][1], None))
        elif kind == JOIN:
            shape = arrays[0].shape
            at = output((len(arrays) * shape[0],) + shape[1:], jnp.int16)
            stores = [(at, item[1], i * shape[0]) for i, item in enumerate(loads)]
        elif kind == ALL:
            code = arrays[0].shape[1]
            size = max(r for r in range(CODED, code, CODED) if coded_rows(r) == code)
            at = output((regions, code, BLOCK), jnp.int16)
            kept = buffer((1, code, BLOCK), jnp.int16)
            stores = [(at, kept, i) for i in range(regions)]
            squares = True
        else:
            rows = arrays[0].shape[0]
            if kind == OVER_X:
                size = rows // regions
            else:
                code = arrays[1].shape[1]
                size = max(r for r in range(CODED, code, CODED) if coded_rows(r) == code)
            blocks = rows // size // max(ways, 1)
            if ways > 1:
                at = output((blocks * size, BLOCK), f32)
                stores.append((at, buffer((blocks * size, BLOCK), f32), None))
            elif ways == 1:
                squares = True
        if kind not in (JOIN, ALL):
            for _ in range(max(ways - 1, 1)):
                shape = (blocks, coded_rows(size), BLOCK)
                stores.append((output(shape, jnp.int16), buffer(shape, jnp.int16), None))
        work = None
        if kind != JOIN:
            rows = size if kind == ALL else arrays[0].shape[0]
            work = (buffer((rows, BLOCK), f32), buffer((up_to(rows // CODED, 16), BLOCK), f32))
        plans.append((kind, ways, blocks, size, loads, stores, work))
    count = len(out_shape)
    if squares:
        out_shape.append(jax.ShapeDtypeStruct((CODED, BLOCK), f32))
    most = max(len(plan[5]) for plan in plans)

    def kernel(*refs):
        region = refs[0][1]
        ins = refs[1 : 1 + len(operands)]
        outs = refs[1 + len(operands) + len(after) :][: len(out_shape)]
        rest = refs[1 + len(operands) + len(after) + len(out_shape) :]
        sem_in, sem_out = rest[-2:]

        def load(at, kept):
            return pltpu.make_async_copy(ins[at], rest[kept], sem_in.at[at])

        def store(job, i):
            at, kept, first = plans[job][5][i]
            target = outs[at]
            if first is not None:
                target = target.at[pl.ds(first, rest[kept].shape[0])]
            return pltpu.make_async_copy(rest[kept], target, sem_out.at[job, i])

        def add_squares(total, rows):
            def step(t):
                value = total[row_tile(t, CODED)]
                outs[-1][...] += value * value

            loop(rows // CODED, step, 8)

        for plan in plans:
            for item in plan[4]:
                load(*item).start()
        if squares:
            outs[-1][...] = jnp.zeros((CODED, BLOCK), f32)
        for job, (kind, ways, blocks, size, loads, stores, work) in enumerate(plans):
            for item in loads:
                load(*item).wait()
            values = [rest[item[1]] for item in loads]
            results = [rest[item[1]] for item in stores]
            if kind == CORES:
                total, scale = rest[work[0]], rest[work[1]]

                def step(t):
                    at = row_tile(t, 256)
                    values[0][at] += values[1][at]
                    total[at] = values[2][at] + values[3][at]

                loop(size // 256, step)
                encode(total, 0, size, results[1].at[0], scale)
            elif kind == ALL:
                total, scale = rest[work[0]], rest[work[1]]
                total[...] = jnp.zeros((size, BLOCK), f32)
                for i in range(regions):
                    scales_of(values[0].at[i], size, scale)

                    def step(t):
                        total[row_tile(t, CODED)] += decoded(values[0].at[i], scale, t)

                    loop(size // CODED, step, 8)
                encode(total, 0, size, results[0].at[0], scale)
                add_squares(total, size)
            elif kind != JOIN:
                total, scale = rest[work[0]], rest[work[1]]
                mine = values[0]
                if kind == OVER_X:
                    rows = size * regions
                    scales_of(values[1].at[0], rows, scale)

                    def step(t):
                        at = row_tile(t, CODED)
                        total[at] = mine[at] + decoded(values[1].at[0], scale, t)

                    loop(rows // CODED, step, 8)
                else:
                    for i in range(blocks * ways):
                        for j, coded in enumerate(values[1:]):
                            scales_of(coded.at[i], size, scale)

                            def step(t):
                                at = pl.ds(pl.multiple_of(i * size + t * CODED, CODED), CODED)
                                value = total[at] if j else mine[at]
                                total[at] = value + decoded(coded.at[i], scale, t)

                            loop(size // CODED, step, 8)

                def first_row(p):
                    if kind == OVER_X and ways:
                        return lax.bitwise_xor(region, difference(p, order)) * size
                    return p * size

                for p in range(blocks * max(ways, 1)):
                    way, i = p // blocks, p % blocks
                    if ways > 1 and way == 0:

                        def step(t):
                            at = pl.ds(pl.multiple_of(first_row(p) + t * CODED, CODED), CODED)
                            to = pl.ds(pl.multiple_of(i * size + t * CODED, CODED), CODED)
                            results[0][to] = total[at]

                        loop(size // CODED, step, 8)
                    else:
                        encode(total, first_row(p), size, results[way].at[i], scale)
                if ways == 1:
                    add_squares(total, size)
            for i in range(len(stores)):
                store(job, i).start()
        for job in range(len(plans)):
            for i in range(len(plans[job][5])):
                store(job, i).wait()

    any_space = pl.BlockSpec(memory_space=pl.ANY)
    out_specs = [any_space] * count
    if squares:
        out_specs.append(pl.BlockSpec(memory_space=pltpu.VMEM))
    out = pl.pallas_call(
        kernel,
        out_shape=out_shape,
        in_specs=[pl.BlockSpec(memory_space=pltpu.SMEM)]
        + [any_space] * (len(operands) + len(after)),
        out_specs=out_specs,
        scratch_shapes=scratch_shapes
        + [
            pltpu.SemaphoreType.DMA((len(operands),)),
            pltpu.SemaphoreType.DMA((len(jobs), most)),
        ],
        compiler_params=pltpu.CompilerParams(vmem_limit_bytes=56 * 2**20),
        cost_estimate=cost_of(5),
    )(place, *operands, *after)
    parts = []
    for plan in plans:
        found = []
        for item in plan[5]:
            if item[0] not in found:
                found.append(item[0])
        parts.append([out[i] for i in found])
    return parts, (out[-1] if squares else None)


def pack(pieces, after):
    sizes = [array.shape[-2] for array, _, _ in pieces]
    firsts = [sum(rows for _, _, rows in pieces[:i]) for i in range(len(pieces) + 1)]

    def kernel(*refs):
        ins = refs[: len(pieces)]
        out = refs[len(pieces) + len(after)]
        packed, sem_in, sem_out = refs[-3:]
        buffers = refs[len(pieces) + len(after) + 1 : -3]

        def load(i):
            source = ins[i] if pieces[i][1] is None else ins[i].at[pieces[i][1]]
            target = buffers[i]
            if sizes[i] < pieces[i][2]:
                target = target.at[pl.ds(0, sizes[i])]
            return pltpu.make_async_copy(source, target, sem_in.at[i])

        def store(i):
            rows = pl.ds(firsts[i], pieces[i][2])
            return pltpu.make_async_copy(packed.at[rows], out.at[rows], sem_out.at[i])

        for i, (_, _, rows) in enumerate(pieces):
            if sizes[i] < rows:
                buffers[i][...] = jnp.zeros((rows, BLOCK), f32)
            load(i).start()
        for i, (_, _, rows) in enumerate(pieces):
            load(i).wait()
            step = max(n for n in range(16, 257, 16) if rows % n == 0)
            for row in range(0, rows, step):
                at = firsts[i] + row
                packed[at : at + step] = buffers[i][row : row + step].astype(bf16)
            store(i).start()
        for i in range(len(pieces)):
            store(i).wait()

    any_space = pl.BlockSpec(memory_space=pl.ANY)
    return pl.pallas_call(
        kernel,
        out_shape=jax.ShapeDtypeStruct((firsts[-1], BLOCK), bf16),
        in_specs=[any_space] * (len(pieces) + len(after)),
        out_specs=any_space,
        scratch_shapes=[pltpu.VMEM((rows, BLOCK), f32) for _, _, rows in pieces]
        + [
            pltpu.VMEM((firsts[-1], BLOCK), bf16),
            pltpu.SemaphoreType.DMA((len(pieces),)),
            pltpu.SemaphoreType.DMA((len(pieces),)),
        ],
        compiler_params=pltpu.CompilerParams(vmem_limit_bytes=56 * 2**20),
        cost_estimate=cost_of(2),
    )(*[array for array, _, _ in pieces], *after)


def update_weights(factor, place, order, groups, masters, moments, squares, chunks):
    count = len(masters)
    rows_of = [c[3] for c in chunks]
    places = 2 ** len(order)
    starts = [0]
    for group in groups:
        starts.append(starts[-1] + len(group))
    flat_first = [0]
    for master in masters:
        flat_first.append(flat_first[-1] + master.size // BLOCK)
    block_rows = []
    for group in groups:
        code = group[0].shape[1]
        block_rows.append(max(r for r in range(CODED, code, CODED) if coded_rows(r) == code))

    def kernel(*refs):
        scale = refs[0][0, 0]
        region = refs[1][1]
        group_refs = refs[2 : 2 + starts[-1]]
        at = 2 + starts[-1]
        param_refs = refs[at : at + 3 * count]
        out_refs = refs[at + 3 * count : at + 6 * count]
        flat_out = refs[at + 6 * count]
        rest = refs[at + 6 * count + 1 :]
        sem_in, sem_out, sem_grad = rest[-3:]
        factors, flat = rest[-5:-3]
        coded_refs = rest[3 * len(chunks) :][: starts[-1]]
        grad_refs = rest[3 * len(chunks) + starts[-1] :][: len(groups)]

        def grad_copies(g):
            return [
                pltpu.make_async_copy(group_refs[i], coded_refs[i], sem_grad.at[i])
                for i in range(starts[g], starts[g + 1])
            ]

        def decode(g):
            rows = block_rows[g]

            for p in range(places):
                if starts[g + 1] - starts[g] == 2:
                    coded = coded_refs[starts[g] + 2 * p // places].at[p % (places // 2)]
                    first = lax.bitwise_xor(region, difference(p, order)) * rows
                else:
                    coded, first = coded_refs[starts[g]].at[p], p * rows
                scales_of(coded, rows, factors)

                def step(t):
                    at = pl.ds(pl.multiple_of(first + t * CODED, CODED), CODED)
                    grad_refs[g][at] = decoded(coded, factors, t)

                loop(rows // CODED, step, 8)

        def piece(ref, chunk):
            for i in chunk[1]:
                ref = ref.at[i]
            if chunk[3] < ref.shape[0]:
                ref = ref.at[pl.ds(chunk[2], chunk[3])]
            return ref

        def copies(i):
            chunk = chunks[i]
            w = chunk[0]
            found = []
            for j in range(3):
                found.append(
                    pltpu.make_async_copy(
                        piece(param_refs[3 * w + j], chunk), rest[3 * i + j], sem_in.at[3 * i + j]
                    )
                )
            return found

        def stores(i):
            chunk = chunks[i]
            return [
                pltpu.make_async_copy(
                    rest[3 * i + (j + 1) % 3],
                    piece(out_refs[3 * chunk[0] + j], chunk),
                    sem_out.at[3 * i + j],
                )
                for j in range(3)
            ]

        started = set()
        for i in range(len(chunks)):
            if chunks[i][4] not in started:
                started.add(chunks[i][4])
                for copy in grad_copies(chunks[i][4]):
                    copy.start()
            for copy in copies(i):
                copy.start()
        for i in range(len(chunks)):
            if chunks[i][4] in started:
                started.remove(chunks[i][4])
                for copy in grad_copies(chunks[i][4]):
                    copy.wait()
                decode(chunks[i][4])
            for copy in copies(i):
                copy.wait()
            master_ref, moment_ref, square_ref = rest[3 * i : 3 * i + 3]
            grad_ref, first_row = grad_refs[chunks[i][4]], chunks[i][5]

            flat_row = flat_first[chunks[i][0]] + chunks[i][2]
            if chunks[i][1]:
                flat_row += chunks[i][1][0] * masters[chunks[i][0]].shape[1]
            step = 128 if rows_of[i] % 128 == 0 else rows_of[i]
            for row in range(0, rows_of[i], step):
                rows = slice(row, row + step)
                first, second, master = adam(
                    master_ref[rows],
                    moment_ref[rows],
                    square_ref[rows],
                    grad_ref[first_row + row : first_row + row + step] * scale,
                )
                moment_ref[rows] = first
                square_ref[rows] = second
                master_ref[rows] = master
                flat[flat_row + row : flat_row + row + step] = master

            for copy in stores(i):
                copy.start()
        flat_copy = pltpu.make_async_copy(
            flat.at[pl.ds(0, flat_first[-1])], flat_out.at[:, 0], sem_out.at[3 * len(chunks)]
        )
        flat_copy.start()
        for i in range(len(chunks)):
            for copy in stores(i):
                copy.wait()
        flat_copy.wait()

    any_space = pl.BlockSpec(memory_space=pl.ANY)
    flat_shape = (up_to(flat_first[-1], 8), BLOCK)
    scratch_shapes = []
    for rows in rows_of:
        scratch_shapes += [pltpu.VMEM((rows, BLOCK), f32)] * 3
    coded_parts = [part for group in groups for part in group]
    scratch_shapes += [pltpu.VMEM(part.shape, part.dtype) for part in coded_parts]
    scratch_shapes += [pltpu.VMEM((places * rows, BLOCK), f32) for rows in block_rows]
    scratch_shapes.append(pltpu.VMEM((up_to(max(block_rows) // CODED, 16), BLOCK), f32))
    scratch_shapes.append(pltpu.VMEM(flat_shape, f32))
    scratch_shapes.append(pltpu.SemaphoreType.DMA((3 * len(chunks),)))
    scratch_shapes.append(pltpu.SemaphoreType.DMA((3 * len(chunks) + 1,)))
    scratch_shapes.append(pltpu.SemaphoreType.DMA((starts[-1],)))
    params = [value for item in zip(masters, moments, squares) for value in item]
    return pl.pallas_call(
        kernel,
        out_shape=[jax.ShapeDtypeStruct(p.shape, f32) for p in params]
        + [jax.ShapeDtypeStruct((flat_first[-1], 1, BLOCK), f32)],
        in_specs=[pl.BlockSpec(memory_space=pltpu.SMEM)] * 2
        + [any_space] * (len(coded_parts) + len(params)),
        out_specs=[any_space] * (len(params) + 1),
        scratch_shapes=scratch_shapes,
        compiler_params=pltpu.CompilerParams(vmem_limit_bytes=56 * 2**20),
        cost_estimate=cost_of(0),
    )(factor, place, *coded_parts, *params)


def adam(master, moment, square, grad):
    first = beta_first * moment + (1 - beta_first) * grad
    second = beta_second * square + (1 - beta_second) * grad * grad
    spread = second * (1.0 / (1 - beta_second**STEP_COUNT))
    root = spread * lax.rsqrt(jnp.maximum(spread, 1e-37))
    ratio = first * (1.0 / (1 - beta_first**STEP_COUNT)) / (root + adam_eps)
    return (first, second, master - learn_rate * (ratio + decay_weight * master))


def pad_rows(value, rows):
    return jnp.pad(value, ((0, rows - value.shape[0]), (0, 0)))


def body(
    initial_state,
    target_states,
    var_means,
    var_scales,
    delta_scales,
    edge_geometry,
    node_counts,
    edge_counts,
    receivers,
    senders,
    send_lists,
    grid_nodes,
    cell_area,
    step_weights,
    *params,
):
    masters, moments, squares = params[0::3], params[1::3], params[2::3]
    enc_w, embed_w, edge_w, node_w, dec_w, inner_w, vector_w, head_w = masters
    variables = enc_w.shape[0]
    depth = up_to(variables, 16)
    features = embed_w.shape[0]
    feature_rows = up_to(features, 16)
    vector_rows = up_to(vector_w.shape[0], 16)
    last_block = 2 + 2 * LAYERS

    def partner(value, axis, bit):
        count = lax.axis_size(axis)
        return lax.ppermute(value, axis, [(i, i ^ bit) for i in range(count)])

    place = jnp.stack([lax.axis_index(N_REP), lax.axis_index(N_REGION)]).astype(jnp.int32)

    def gather(pieces, after=()):
        return (place, lax.all_gather(pack(pieces, after), N_REP))

    start = gather(
        [
            (enc_w, None, depth),
            (inner_w, 0, D),
            (embed_w, None, feature_rows),
            (inner_w, 1, D),
            (vector_w, None, vector_rows),
        ]
    )
    of_layer = []
    for l in range(LAYERS):
        pieces = [(edge_w, l, 3 * D), (inner_w, 2 + l, D)]
        pieces += [(node_w, l, 2 * D), (inner_w, 2 + LAYERS + l, D)]
        of_layer.append(gather(pieces))
    end = gather(
        [(dec_w, None, 2 * D), (inner_w, last_block, D), (head_w, None, depth)]
    )
    enc_first = (start, N_W, (0, depth))
    enc_inner = (start, N_W, (depth, D))
    embed_first = (start, N_W, (depth + D, feature_rows))
    embed_inner = (start, N_W, (depth + D + feature_rows, D))
    at_vectors = depth + 2 * D + feature_rows
    vectors = start[1][:, at_vectors:].astype(f32).transpose(1, 0, 2).reshape(vector_rows, D)
    layer_weights = [
        (
            (of_layer[l], N_W, (0, 3 * D)),
            (of_layer[l], N_W, (3 * D, D)),
            (of_layer[l], N_W, (4 * D, 2 * D)),
            (of_layer[l], N_W, (6 * D, D)),
        )
        for l in range(LAYERS)
    ]
    dec_weights = (
        (end, N_W, (0, 2 * D)),
        (end, N_W, (2 * D, D)),
        (end, N_W, (3 * D, depth)),
    )

    count = node_counts[0]
    send_from = jnp.where(senders < NODE_CAP, senders % count, senders)
    live = jnp.arange(receivers.shape[0]) < edge_counts[0]
    recv = jnp.where(live, receivers, -1)
    picks = (send_lists[0] % count).reshape(-1)
    assign = grid_nodes % count
    regions, slots = send_lists.shape[1:]
    send, send_row = send_from[:, None], send_from[None, :]
    recv, recv_row = recv[:, None], recv[None, :]
    picks, picks_row = picks[:, None], picks[None, :]
    assign, assign_row = assign[:, None], assign[None, :]

    def exchange(rows):
        table = rows.reshape(regions, slots, D)
        table = lax.all_to_all(table, N_REGION, split_axis=0, concat_axis=0, tiled=True)
        return table.reshape(regions * slots, D)

    def column(value, fill):
        return jnp.pad(value, (0, depth - variables), constant_values=fill)[:, None]

    means, scales, delta = column(var_means, 0), column(var_scales, 1), column(delta_scales, 1)
    state = pad_rows(initial_state[0].T, depth)
    target = jnp.pad(
        target_states[0].transpose(0, 2, 1), ((0, 0), (0, depth - variables), (0, 0))
    )
    area = cell_area[None, :]
    geometry = pad_rows(edge_geometry.T, feature_rows).astype(bf16)
    plan = step_weights

    bits = [1 << i for i in range(regions.bit_length() - 1)]
    turns = [bits[:1]] + [bits[i : i + 2] for i in range(1, len(bits), 2)]
    unit = CODED * regions
    dec_rows, layer_rows = up_to(3 * D + depth, unit), up_to(7 * D, unit)
    start_rows = up_to(at_vectors + vector_rows, unit)

    weight_local = (
        jnp.sum(plan.astype(f32)) * jnp.sum(cell_area) * variables * lax.axis_size(N_REP)
    )
    weight_total = jnp.broadcast_to(weight_local, (8, BLOCK))
    for bit in bits:
        weight_total = weight_total + partner(weight_total, N_REGION, bit)
    weight_total = weight_total[0, 0]
    inverse_total = (1.0 / weight_total).reshape(1, 1)

    edges0, edges0_low, *keep_embed = embed_forward(geometry, embed_first, embed_inner, 1, vectors)
    keep_embed = dict(zip((N_HIDDEN, N_NORMED, N_INVERSE), keep_embed))
    records = []
    loss_local = 0.0
    for step in range(STEPS):
        nodes, node_low, outgoing, latent, low, feats, hidden, normed, inverse = encoder_forward(
            state, means, scales, enc_first, enc_inner, vectors, assign_row, picks
        )
        keep_enc = {N_FEATS: feats, N_HIDDEN: hidden, N_NORMED: normed, N_INVERSE: inverse}
        edges, edges_low = edges0, edges0_low
        layers = []
        for l in range(LAYERS):
            halo = exchange(outgoing)
            first = layer_weights[l][0]
            local = layer_local(l, edges_low, node_low, first, vectors, send, recv)
            from_send = (first[0], N_W, (first[2][0] + D, D))
            before = edges_low
            edges, edges_low, nodes, node_low, outgoing, kept = layer_forward(
                l, local, edges, nodes, node_low, halo, (from_send,) + layer_weights[l][1:],
                vectors, send, recv_row, picks, l == LAYERS - 1,
            )
            kept[N_EDGES_LOW] = before
            layers.append(kept)
        state, loss, keep_dec = decoder_forward(
            step, state, target, latent, low, node_low, dec_weights, vectors,
            assign, delta, area, plan,
        )
        loss_local = loss_local + loss[0, 0]
        records.append((keep_enc, layers, keep_dec))

    class Sum:
        def __init__(self, parts, at_once=False):
            self.parts = list(parts)
            self.at_once = at_once
            self.stage = -2
            self.halves = None

        def job(self):
            p, count = self.parts, len(turns)
            if self.stage == -2:
                return (CORES, [p[0], partner(p[1], N_REP, 1), p[2], partner(p[3], N_REP, 1)], 0)
            if self.stage == -1:
                ways = 0 if self.at_once else 2 ** len(turns[0])
                return (OVER_X, [p[0], partner(p[1], N_REP, 2)], ways)
            if self.at_once:
                return (ALL, [self.all_turn()], 1)
            if self.stage < count:
                turn, last = turns[self.stage], self.stage == count - 1
                ways = 1 if last else 2 ** len(turns[self.stage + 1])
                got = [
                    partner(p[q], N_REGION, difference(q, turn)) for q in range(1, 2 ** len(turn))
                ]
                return (TURN, [p[0]] + got, ways)
            turn = turns[2 * count - 1 - self.stage]
            got = [partner(p[0], N_REGION, difference(q, turn)) for q in range(1, 2 ** len(turn))]
            return (JOIN, [p[0]] + got, 0)

        def summed(self):
            return self.stage >= (1 if self.at_once else len(turns))

        def all_turn(self):
            return lax.all_to_all(
                self.parts[0], N_REGION, split_axis=0, concat_axis=0, tiled=True
            )

        def done(self, parts):
            self.parts = parts
            self.stage += 1
            if self.at_once:
                if self.stage == 1:
                    self.halves = [self.all_turn()]
                return
            if self.stage == 2 * len(turns) - 1:
                self.halves = [parts[0], partner(parts[0], N_REGION, bits[0])]

    def over_all(value):
        for bit in bits:
            value = value + partner(value, N_REGION, bit)
        for bit in (1, 2):
            value = value + partner(value, N_REP, bit)
        return value

    all_squares = []
    on_way = {}
    arrived = []

    def advance(names, after):
        names = [name for name in names if on_way[name].halves is None]
        if not names:
            return after
        jobs = [on_way[name].job() for name in names]
        parts, squares = combine(jobs, bits, place, list(after) + arrived)
        arrived.clear()
        if squares is not None:
            all_squares.append(jnp.sum(squares, 0))
        for name, found in zip(names, parts):
            on_way[name].done(found)
            if on_way[name].halves is not None:
                arrived.append(on_way[name].halves[-1])
        return [parts[0][0]]

    d_state = None
    grads = {}
    d_embed = []
    for step in reversed(range(STEPS)):
        keep_enc, layers, keep_dec = records[step]
        final = step == 0
        d_nodes, d_grid, d_next, sums, grad = decoder_backward(
            step, regions, d_state, keep_dec, dec_weights, vectors, assign_row, delta, area, plan,
            inverse_total, *grads.get(N_DEC, (None, None)),
            (place, dec_rows, (0, dec_rows)) if final else None,
        )
        grads[N_DEC] = (grad if final else grad[0], sums)
        returned, d_edges = None, None
        after = []
        if final:
            on_way[N_DEC] = Sum(grad)
        for l in reversed(range(LAYERS)):
            old_grad, old_sums = grads.get(l, (None, None))
            found = layer_backward(
                l, d_nodes, returned, d_edges, layers[l], layer_weights[l], vectors,
                send_row, recv, picks_row, old_sums, after,
            )
            d_edges, sums = found[N_D_EDGES], found[N_SUMS]
            returned = exchange(found[N_D_HALO])
            after = advance(list(on_way), [sums]) + [returned] if final else []
            d_nodes, grad = layer_grads(
                found, layers[l], layer_weights[l][0], send_row, recv_row, layer_rows, old_grad,
                (place, layer_rows, (0, 4 * D, layer_rows)) if final else None, after,
            )
            grads[l] = (grad if final else grad[0], sums)
            after = advance([N_DEC, 2, 1], [d_nodes]) if final and l == 0 else []
            if final:
                on_way[l] = Sum(grad)
        d_embed.append(d_edges)
        others, swap = None, None
        if final:
            embed_sums, embed_grads = embed_backward(
                d_embed[0], d_embed[1], keep_embed, geometry, embed_inner, vectors, after
            )
            after = advance([0, 1, 2, N_DEC], [embed_sums])
            all_sums = {"embed": embed_sums}
            for name in [N_DEC] + list(range(LAYERS)):
                all_sums[name] = grads[name][1]
            others, swap = (embed_grads, all_sums), (place, start_rows, (0, start_rows))
        out = encoder_backward(
            step, d_grid, d_nodes, returned, d_next, keep_enc, (enc_first, enc_inner), vectors,
            assign, picks_row, scales, *grads.get(N_ENC, (None, None)), others, swap, after,
        )
        if not final:
            d_state, sums, grad = out
            grads[N_ENC] = (grad, sums)
    after = advance([N_DEC, 2, 1, 0], [out[0]])
    on_way["start"] = Sum(out, True)
    totals = None
    while any(item.halves is None for item in on_way.values()):
        after = advance(list(on_way), after)
        if totals is None and all(item.summed() for item in on_way.values()):
            squares_row = sum(all_squares)
            totals = over_all(jnp.stack([squares_row, jnp.broadcast_to(loss_local, (BLOCK,))]))
            arrived.append(totals)
    gradient_norm = jnp.sqrt(jnp.sum(totals[0]))
    loss_total = totals[1, 0]
    factor = jnp.minimum(1.0, clip_limit / gradient_norm)

    order = list(on_way)
    groups = [on_way[name].halves for name in order]
    last_group = len(groups) - 1
    chunks = []
    for l in reversed(range(LAYERS)):
        group = order.index(l)
        chunks += [(2, (l,), i * D, D, group, i * D) for i in range(3)]
        chunks.append((5, (2 + l,), 0, D, group, 3 * D))
        chunks += [(3, (l,), i * D, D, group, (4 + i) * D) for i in range(2)]
        chunks.append((5, (2 + LAYERS + l,), 0, D, group, 6 * D))
    chunks += [(4, (), i * D, D, 0, i * D) for i in range(2)]
    chunks.append((5, (last_block,), 0, D, 0, 2 * D))
    chunks.append((7, (), 0, variables, 0, 3 * D))
    chunks.append((0, (), 0, variables, last_group, 0))
    chunks.append((5, (0,), 0, D, last_group, depth))
    chunks.append((1, (), 0, features, last_group, depth + D))
    chunks.append((5, (1,), 0, D, last_group, depth + D + feature_rows))
    chunks.append((6, (), 0, vector_w.shape[0], last_group, at_vectors))
    *new, flat = update_weights(
        factor.reshape(1, 1), place, bits, groups, masters, moments, squares, chunks
    )
    weight_copies = flat.reshape(1, -1).astype(bf16)
    return (loss_total, weight_total, gradient_norm, *new, weight_copies)


def solution(mesh):
    two = P(None, N_REP)
    three = P(None, None, N_REP)
    weights = (two, two, three, three, two, three, two, two)
    placed = (
        P(N_REP, N_REGION, None),
        P(N_REP, None, N_REGION, None),
        P(),
        P(),
        P(),
        P(N_REGION, None),
        P(N_REGION),
        P(N_REGION),
        P(N_REGION),
        P(N_REGION),
        P(N_REGION, None, None),
        P(N_REGION),
        P(N_REGION),
        P(),
    ) + tuple(spec for spec in weights for _ in range(3))
    return jax.shard_map(
        body,
        mesh=mesh,
        in_specs=placed,
        out_specs=(P(), P(), P())
        + tuple(spec for spec in weights for _ in range(3))
        + (P(N_REP, None),),
        check_vma=False,
    )
```

```python
import jax
import jax.numpy as jnp
from jax import lax
from jax.experimental import pallas as pl
from jax.experimental.pallas import tpu as pltpu
from jax.sharding import PartitionSpec as P

LAYERS = 3
STEPS = 2
STEP_COUNT = 10
NODE_CAP = 512
D = 512
BLOCK = 128
BLOCKS = D // BLOCK
TILE = 512
CODED = 32
CODE_TOP = 32000.0

norm_eps = 1e-05
beta_first = 0.9
beta_second = 0.95
adam_eps = 1e-08
decay_weight = 0.1
learn_rate = 0.05
clip_limit = 0.02

N_ACT = "act"
N_AREA = "area"
N_ASSIGN = "assign"
N_B = "b"
N_BEFORE = "before"
N_D_EDGES = "d_edges"
N_D_FIRST = "d_first"
N_D_GRID = "d_grid"
N_D_HALO = "d_halo"
N_D_HIDDEN = "d_hidden"
N_D_MIXED = "d_mixed"
N_D_NEXT = "d_next"
N_D_NODES = "d_nodes"
N_D_SECOND = "d_second"
N_D_STATE = "d_state"
N_DEC = "dec"
N_DELTA = "delta"
N_EDGE_FIRST = "edge_first"
N_EDGE_INNER = "edge_inner"
N_EDGES = "edges"
N_EDGES_LOW = "edges_low"
N_EMBED_GRADS = "embed_grads"
N_ENC = "enc"
N_FEATS = "feats"
N_FINAL = "final"
N_FIRST = "first"
N_FROM_RECV = "from_recv"
N_FROM_SEND = "from_send"
N_GEOMETRY = "geometry"
N_GRADS = "grads"
N_H = "h"
N_HALO = "halo"
N_HALO_HIGH = "halo_high"
N_HALO_REST = "halo_rest"
N_HEAD = "head"
N_HIDDEN = "hidden"
N_INNER = "inner"
N_INVERSE = "inverse"
N_LATENT = "latent"
N_LOCAL = "local"
N_LOW = "low"
N_MISS = "miss"
N_NODE_ACT = "node_act"
N_NODE_D_HIDDEN = "node_d_hidden"
N_NODE_D_MIXED = "node_d_mixed"
N_NODE_FIRST = "node_first"
N_NODE_HIDDEN = "node_hidden"
N_NODE_INNER = "node_inner"
N_NODE_INVERSE = "node_inverse"
N_NODE_LOW = "node_low"
N_NODE_NORMED = "node_normed"
N_NODES = "nodes"
N_NORMED = "normed"
N_OUTGOING = "outgoing"
N_PICKS = "picks"
N_PICKS_ROW = "picks_row"
N_PLAN = "plan"
N_RECV = "recv"
N_RECV_ROW = "recv_row"
N_REGION = "region"
N_REP = "rep"
N_RETURNED = "returned"
N_S = "s"
N_SCALES = "scales"
N_SEND = "send"
N_SEND_ROW = "send_row"
N_STATE = "state"
N_SUMS = "sums"
N_SUMS_ = "sums_"
N_TARGET = "target"
N_TOTAL = "total"
N_V = "v"
N_VECTORS = "vectors"
N_W = "w"

f32 = jnp.float32
bf16 = jnp.bfloat16


def up_to(rows, unit):
    return (rows + unit - 1) // unit * unit


class Env:
    pass


def cost_of(micros):
    return pl.CostEstimate(flops=int(micros * 1.15e9), bytes_accessed=0, transcendentals=0)


def launch(body, ins, outs, scratch=(), micros=0, swap=None, after=()):
    in_specs, operands, scratch_shapes, names = [], [], [], []
    loads = {}
    total_sems = 0
    positions = {}
    place = None
    for item in ins:
        name, array, kind = item[:3]
        positions[name] = len(operands)
        if kind == N_W:
            if len(array) > 2:
                place = array[0]
            operands += array[1:]
        else:
            operands.append(array)
        if kind == N_S:
            in_specs.append(pl.BlockSpec(memory_space=pltpu.SMEM))
        elif kind in (N_H, N_V):
            index, parts = item[3] if kind == N_H else ((), 1)
            in_specs.append(pl.BlockSpec(memory_space=pl.ANY))
            shape = array.shape[len(index) :]
            loads[name] = (N_H, index, parts, shape, total_sems)
            total_sems += parts
            names.append(name)
            scratch_shapes.append(pltpu.VMEM(shape, array.dtype))
        else:
            first, rows = item[3]
            in_specs += [pl.BlockSpec(memory_space=pl.ANY)] * (len(array) - 1)
            whole = len(array) == 2
            loads[name] = (N_W, first, rows, whole, total_sems)
            total_sems += BLOCKS
            names.append(name)
            scratch_shapes.append(pltpu.VMEM((rows, D), bf16))
    out_specs, out_shape = [], []
    flushes = {}
    out_sems = 0
    for name, shape, dtype, kind, parts in outs:
        out_shape.append(jax.ShapeDtypeStruct(shape, dtype))
        if kind == N_B:
            out_specs.append(pl.BlockSpec(memory_space=pltpu.VMEM))
        else:
            out_specs.append(pl.BlockSpec(memory_space=pl.ANY))
            flushes[name] = (parts, shape, out_sems)
            out_sems += parts
            if name not in names:
                names.append(name)
                scratch_shapes.append(pltpu.VMEM(shape, dtype))
    if swap is not None:
        for _ in range(BLOCKS):
            out_shape.append(jax.ShapeDtypeStruct((swap[1], BLOCK), f32))
            out_specs.append(pl.BlockSpec(memory_space=pl.ANY))
    place_at = len(operands)
    if place is not None:
        operands.append(place)
        in_specs.append(pl.BlockSpec(memory_space=pltpu.SMEM))
    for array in after:
        operands.append(array)
        in_specs.append(pl.BlockSpec(memory_space=pl.ANY))
    for name, shape, dtype in scratch:
        names.append(name)
        scratch_shapes.append(pltpu.VMEM(shape, dtype))
    scratch_shapes.append(pltpu.SemaphoreType.DMA((max(total_sems, 1),)))
    scratch_shapes.append(pltpu.SemaphoreType.DMA((max(out_sems, 1),)))
    if swap is not None:
        scratch_shapes.append(pltpu.SemaphoreType.DMA((BLOCKS, len(swap[2]) - 1)))

    def kernel(*refs):
        k = Env()
        out_refs = refs[len(operands) : len(operands) + len(out_shape)]
        rest = refs[len(operands) + len(out_shape) :]
        for name, ref in zip(names, rest):
            setattr(k, name, ref)
        sem_in, sem_out = rest[len(names) : len(names) + 2]
        sources, targets = {}, {}
        for item in ins:
            if item[2] == N_S:
                setattr(k, item[0], refs[positions[item[0]]])
            else:
                sources[item[0]] = positions[item[0]]
        for item, ref in zip(outs, out_refs):
            if item[3] == N_B:
                setattr(k, item[0], ref)
            else:
                targets[item[0]] = ref

        def load(name, part):
            kind, first, parts, shape, base = loads[name]
            src, dst = refs[sources[name]], getattr(k, name)
            if kind == N_H:
                for i in first:
                    src = src.at[i]
                if parts > 1:
                    step = shape[0] // parts
                    rows = pl.ds(pl.multiple_of(part * step, step), step)
                    src, dst = src.at[rows], dst.at[rows]
            else:
                if shape:
                    src = src.at[part, pl.ds(first, parts)]
                    column = part * BLOCK
                else:
                    src = refs[sources[name] + part].at[pl.ds(first, parts)]
                    column = lax.bitwise_xor(refs[place_at][0], part) * BLOCK
                    column = pl.multiple_of(column, BLOCK)
                dst = dst.at[:, pl.ds(column, BLOCK)]
            return pltpu.make_async_copy(src, dst, sem_in.at[base + part])

        def send(name, part):
            parts, shape, base = flushes[name]
            src, dst = getattr(k, name), targets[name]
            if parts > 1:
                step = shape[0] // parts
                rows = pl.ds(pl.multiple_of(part * step, step), step)
                src, dst = src.at[rows], dst.at[rows]
            return pltpu.make_async_copy(src, dst, sem_out.at[base + part])

        def wait(name, part=None):
            if name not in loads:
                return
            if part is not None:
                load(name, part).wait()
                return
            count = BLOCKS if loads[name][0] == N_W else loads[name][2]
            for i in range(count):
                load(name, i).wait()

        def flush(name, part=None):
            if part is not None:
                send(name, part).start()
                return
            for i in range(flushes[name][0]):
                send(name, i).start()

        def swap_copy(other, part):
            rows = pl.ds(swap[2][part], swap[2][part + 1] - swap[2][part])
            source = k.grads.at[lax.bitwise_xor(lax.axis_index(N_REP), other), rows]
            target = out_refs[len(outs) + other].at[rows]
            return pltpu.make_async_copy(source, target, rest[-1].at[other, part])

        def flush_swap(part=0):
            for other in range(BLOCKS):
                swap_copy(other, part).start()

        k.wait, k.flush, k.flush_swap = wait, flush, flush_swap
        for item in sorted(ins, key=lambda item: item[2] != N_V):
            if item[0] in loads:
                count = BLOCKS if item[2] == N_W else loads[item[0]][2]
                for i in range(count):
                    load(item[0], i).start()
        for item in ins:
            if item[2] == N_V:
                wait(item[0])
        body(k)
        for item in outs:
            if item[3] == N_V:
                flush(item[0])
        for name in flushes:
            for i in range(flushes[name][0]):
                send(name, i).wait()
        if swap is not None:
            for other in range(BLOCKS):
                for part in range(len(swap[2]) - 1):
                    swap_copy(other, part).wait()

    return pl.pallas_call(
        kernel,
        out_shape=out_shape,
        in_specs=in_specs,
        out_specs=out_specs,
        scratch_shapes=scratch_shapes,
        compiler_params=pltpu.CompilerParams(
            vmem_limit_bytes=56 * 2**20
        ),
        cost_estimate=cost_of(micros),
    )(*operands)


def dense(left, right):
    return jnp.dot(left, right, preferred_element_type=f32)


def dense_left(left, right):
    return lax.dot_general(left, right, (((0,), (0,)), ((), ())), preferred_element_type=f32)


def dense_right(left, right):
    return lax.dot_general(left, right, (((1,), (1,)), ((), ())), preferred_element_type=f32)


def halves(value):
    high = value.astype(bf16)
    return high, (value - high.astype(f32)).astype(bf16)


def rows_hot(column, width):
    spots = lax.broadcasted_iota(jnp.int32, (column.shape[0], width), 1)
    return jnp.where(column == spots, 1.0, 0.0).astype(bf16)


def cols_hot(row, height, first=0):
    spots = lax.broadcasted_iota(jnp.int32, (height, row.shape[1]), 0) + first
    return jnp.where(row == spots, 1.0, 0.0).astype(bf16)


def sigmoid(value):
    return 0.5 * jnp.tanh(0.5 * value) + 0.5


def normalise(mixed):
    centred = mixed - jnp.mean(mixed, -1, keepdims=True)
    inverse = lax.rsqrt(jnp.mean(centred * centred, -1, keepdims=True) + norm_eps)
    return centred * inverse, inverse


def vec(k, block, row):
    at = 3 * block + row
    return k.vectors[at : at + 1, :]


def row_tile(t, size):
    return pl.ds(pl.multiple_of(t * size, size), size)


def loop(count, step, most=1):
    unroll = max(n for n in range(1, most + 1) if count % n == 0)
    lax.fori_loop(0, count, lambda t, carry: (step(t), carry)[1], 0, unroll=unroll)


def forward_rows(k, block, hidden, inner):
    act = (hidden * sigmoid(hidden)).astype(bf16)
    normed, inverse = normalise(dense(act, inner))
    return normed * vec(k, block, 1) + vec(k, block, 2), normed, inverse


def backward_rows(k, block, upstream, hidden, normed, inverse, inner, sums, at):
    sums[at + 1 : at + 2, :] += jnp.sum(upstream * normed, 0, keepdims=True)
    sums[at + 2 : at + 3, :] += jnp.sum(upstream, 0, keepdims=True)
    scaled = upstream * vec(k, block, 1)
    d_mixed = inverse * (
        scaled
        - jnp.mean(scaled, -1, keepdims=True)
        - normed * jnp.mean(scaled * normed, -1, keepdims=True)
    )
    d_mixed = d_mixed.astype(bf16)
    sigma = sigmoid(hidden)
    act = (hidden * sigma).astype(bf16)
    d_act = dense_right(d_mixed, inner)
    d_hidden = (d_act * (sigma * (1.0 + hidden * (1.0 - sigma)))).astype(bf16)
    sums[at : at + 1, :] += jnp.sum(d_hidden.astype(f32), 0, keepdims=True)
    return act, d_mixed, d_hidden


def add_grad(k, first, value):
    rows = value.shape[0]
    for c in range(BLOCKS):
        k.grads[c, first : first + rows, :] += value[:, c * BLOCK : (c + 1) * BLOCK]


def set_grad(k, first, value):
    rows = value.shape[0]
    for c in range(BLOCKS):
        k.grads[c, first : first + rows, :] = value[:, c * BLOCK : (c + 1) * BLOCK]


def put_grad(k, fresh, first, value):
    (set_grad if fresh else add_grad)(k, first, value)


def weight_grad(k, fresh, first, left, right, pieces=2):
    width = left.shape[1]
    step = width // pieces
    for i in range(pieces):
        part = dense_left(left[:, i * step : (i + 1) * step], right[...])
        put_grad(k, fresh, first + i * step, part)


def start_sums(k, fresh):
    if fresh:
        k.sums[...] = jnp.zeros(k.sums.shape, f32)
    else:
        k.wait(N_SUMS)


def embed_forward(geometry, first, inner, at_inner, vectors):
    edges = geometry.shape[1]

    def body(k):
        k.wait(N_FIRST)
        k.wait(N_INNER)

        def tile(t):
            rows = row_tile(t, TILE)
            hidden = dense_left(k.geometry[:, rows], k.first[...]) + vec(k, 1, 0)
            k.hidden[rows] = hidden
            out, normed, inverse = forward_rows(k, 1, hidden, k.inner[...])
            k.normed[rows] = normed
            k.inverse[rows] = inverse
            k.edges[rows] = out
            k.edges_low[rows] = out.astype(bf16)
            for name in (N_HIDDEN, N_NORMED, N_INVERSE, N_EDGES, N_EDGES_LOW):
                k.flush(name, t)

        loop(edges // TILE, tile)

    parts = edges // TILE
    return launch(
        body,
        [
            (N_GEOMETRY, geometry, N_V),
            (N_VECTORS, vectors, N_V),
            (N_FIRST,) + first,
            (N_INNER,) + inner,
        ],
        [
            (N_EDGES, (edges, D), f32, N_H, parts),
            (N_EDGES_LOW, (edges, D), bf16, N_H, parts),
            (N_HIDDEN, (edges, D), f32, N_H, parts),
            (N_NORMED, (edges, D), f32, N_H, parts),
            (N_INVERSE, (edges, 1), f32, N_H, parts),
        ],
        micros=5,
    )


def encoder_forward(state, means, scales, first, inner, vectors, assign, picks):
    depth, grid = state.shape
    out_rows = picks.shape[0]

    def body(k):
        k.wait(N_STATE)
        k.feats[...] = ((k.state[...] - k.means[...]) / k.scales[...]).astype(bf16)
        k.flush(N_FEATS)
        k.wait(N_FIRST)
        k.wait(N_INNER)

        def tile(t):
            rows = row_tile(t, TILE)
            hidden = dense_left(k.feats[:, rows], k.first[...]) + vec(k, 0, 0)
            k.hidden[rows] = hidden
            out, normed, inverse = forward_rows(k, 0, hidden, k.inner[...])
            k.normed[rows] = normed
            k.inverse[rows] = inverse
            k.latent[rows] = out
            k.low[rows] = out.astype(bf16)
            for name in (N_HIDDEN, N_NORMED, N_INVERSE, N_LATENT, N_LOW):
                k.flush(name, t)

        loop(grid // TILE, tile)
        nodes = dense(cols_hot(k.assign[...], NODE_CAP), k.low[...])
        k.nodes[...] = nodes
        k.node_low[...] = nodes.astype(bf16)
        k.outgoing[...] = dense(rows_hot(k.picks[...], NODE_CAP), k.node_low[...]).astype(bf16)

    parts = grid // TILE
    return launch(
        body,
        [
            (N_STATE, state, N_H, ((), 1)),
            ("means", means, N_V),
            (N_SCALES, scales, N_V),
            (N_ASSIGN, assign, N_V),
            (N_PICKS, picks, N_V),
            (N_VECTORS, vectors, N_V),
            (N_FIRST,) + first,
            (N_INNER,) + inner,
        ],
        [
            (N_NODES, (NODE_CAP, D), f32, N_V, 1),
            (N_NODE_LOW, (NODE_CAP, D), bf16, N_V, 1),
            (N_OUTGOING, (out_rows, D), bf16, N_V, 1),
            (N_LATENT, (grid, D), f32, N_H, parts),
            (N_LOW, (grid, D), bf16, N_H, parts),
            (N_FEATS, (depth, grid), bf16, N_H, 1),
            (N_HIDDEN, (grid, D), f32, N_H, parts),
            (N_NORMED, (grid, D), f32, N_H, parts),
            (N_INVERSE, (grid, 1), f32, N_H, parts),
        ],
        micros=5,
    )


def layer_local(layer, edges_low, node_low, edge_first, vectors, send, recv):
    count = edges_low.shape[0]
    at = 2 + layer

    def body(k):
        k.wait(N_EDGE_FIRST)

        def tile(t):
            rows = row_tile(t, TILE)
            sent = dense(rows_hot(k.send[rows], NODE_CAP), k.node_low[...]).astype(bf16)
            got = dense(rows_hot(k.recv[rows], NODE_CAP), k.node_low[...]).astype(bf16)
            k.wait(N_EDGES_LOW, t)
            joined = jnp.concatenate([k.edges_low[rows], sent, got], 1)
            k.local[rows] = dense(joined, k.edge_first[...]) + vec(k, at, 0)
            k.flush(N_LOCAL, t)

        loop(count // TILE, tile)

    parts = count // TILE
    return launch(
        body,
        [
            (N_NODE_LOW, node_low, N_V),
            (N_SEND, send, N_V),
            (N_RECV, recv, N_V),
            (N_VECTORS, vectors, N_V),
            (N_EDGE_FIRST,) + edge_first,
            (N_EDGES_LOW, edges_low, N_H, ((), parts)),
        ],
        [(N_LOCAL, (count, D), f32, N_H, parts)],
        micros=8,
    )[0]


def layer_forward(
    layer, local, edges, nodes, node_low, halo, weights, vectors, send, recv_row, picks, last
):
    count = edges.shape[0]
    halo_rows = halo.shape[0]
    from_send, edge_inner, node_first, node_inner = weights
    at_edge, at_node = 2 + layer, 2 + LAYERS + layer

    def body(k):
        k.wait(N_FROM_SEND)
        high, rest = halves(dense(k.halo[...], k.from_send[...]))
        k.table[:, 0:D] = high
        k.table[:, D : 2 * D] = rest
        k.wait(N_EDGE_INNER)

        def tile(t):
            rows = row_tile(t, TILE)
            both = dense(rows_hot(k.send[rows] - NODE_CAP, halo_rows), k.table[...])
            k.wait(N_HIDDEN, t)
            hidden = k.hidden[rows] + (both[:, 0:D] + both[:, D : 2 * D])
            k.hidden[rows] = hidden
            out, normed, inverse = forward_rows(k, at_edge, hidden, k.edge_inner[...])
            k.normed[rows] = normed
            k.inverse[rows] = inverse
            k.wait(N_EDGES, t)
            edge = k.edges[rows] + out
            k.edges[rows] = edge
            high, rest = halves(edge)
            k.edges_low[rows] = high
            k.rest[rows] = rest
            for name in (N_HIDDEN, N_NORMED, N_INVERSE):
                k.flush(name, t)
            if not last:
                k.flush(N_EDGES, t)
                k.flush(N_EDGES_LOW, t)

        loop(count // TILE, tile)
        k.wait(N_NODE_FIRST)
        k.wait(N_NODE_INNER)
        k.wait(N_NODES)

        def node_tile(t):
            rows = row_tile(t, TILE)
            hot = cols_hot(k.recv_row[...], TILE, t * TILE)
            total = (dense(hot, k.edges_low[...]) + dense(hot, k.rest[...])).astype(bf16)
            k.total[rows] = total
            node_in = jnp.concatenate([k.node_low[rows], total], 1)
            hidden = dense(node_in, k.node_first[...]) + vec(k, at_node, 0)
            k.node_hidden[rows] = hidden
            out, normed, inverse = forward_rows(k, at_node, hidden, k.node_inner[...])
            k.node_normed[rows] = normed
            k.node_inverse[rows] = inverse
            node = k.nodes[rows] + out
            k.nodes[rows] = node
            k.new_low[rows] = node.astype(bf16)
            for name in (N_TOTAL, N_NODE_HIDDEN, N_NODE_NORMED, N_NODE_INVERSE):
                k.flush(name, t)
            if not last:
                k.flush(N_NODES, t)

        loop(NODE_CAP // TILE, node_tile)
        if not last:
            k.outgoing[...] = dense(rows_hot(k.picks[...], NODE_CAP), k.new_low[...]).astype(bf16)

    parts = count // TILE
    node_parts = NODE_CAP // TILE
    ins = [
        (N_NODE_LOW, node_low, N_V),
        (N_HALO, halo, N_V),
        (N_SEND, send, N_V),
        (N_RECV_ROW, recv_row, N_V),
        (N_VECTORS, vectors, N_V),
        (N_FROM_SEND,) + from_send,
        (N_EDGE_INNER,) + edge_inner,
        (N_HIDDEN, local, N_H, ((), parts)),
        (N_EDGES, edges, N_H, ((), parts)),
        (N_NODE_FIRST,) + node_first,
        (N_NODE_INNER,) + node_inner,
        (N_NODES, nodes, N_H, ((), 1)),
    ]
    outs = [
        ("new_low", (NODE_CAP, D), bf16, N_V, 1),
        (N_HIDDEN, (count, D), f32, N_H, parts),
        (N_NORMED, (count, D), f32, N_H, parts),
        (N_INVERSE, (count, 1), f32, N_H, parts),
        (N_TOTAL, (NODE_CAP, D), bf16, N_H, node_parts),
        (N_NODE_HIDDEN, (NODE_CAP, D), f32, N_H, node_parts),
        (N_NODE_NORMED, (NODE_CAP, D), f32, N_H, node_parts),
        (N_NODE_INVERSE, (NODE_CAP, 1), f32, N_H, node_parts),
    ]
    scratch = [("table", (halo_rows, 2 * D), bf16), ("rest", (count, D), bf16)]
    if last:
        scratch.append((N_EDGES_LOW, (count, D), bf16))
    else:
        ins.append((N_PICKS, picks, N_V))
        outs += [
            (N_EDGES, (count, D), f32, N_H, parts),
            (N_NODES, (NODE_CAP, D), f32, N_H, node_parts),
            (N_OUTGOING, (halo_rows, D), bf16, N_V, 1),
            (N_EDGES_LOW, (count, D), bf16, N_H, parts),
        ]
    out = launch(body, ins, outs, scratch, micros=13)
    kept = {
        N_NODE_LOW: node_low,
        N_HALO: halo,
        N_HIDDEN: out[1],
        N_NORMED: out[2],
        N_INVERSE: out[3],
        N_TOTAL: out[4],
        N_NODE_HIDDEN: out[5],
        N_NODE_NORMED: out[6],
        N_NODE_INVERSE: out[7],
    }
    if last:
        return None, None, None, out[0], None, kept
    return out[8], out[11], out[9], out[0], out[10], kept


def decoder_forward(
    step, state, target, latent, low, node_low, weights, vectors, assign, delta, area, plan
):
    depth, grid = state.shape
    first, inner, head = weights
    at = 2 + 2 * LAYERS

    def body(k):
        k.wait(N_FIRST)
        k.wait(N_INNER)

        def tile(t):
            rows = row_tile(t, TILE)
            k.wait(N_LOW, t)
            got = dense(rows_hot(k.assign[rows], NODE_CAP), k.node_low[...]).astype(bf16)
            joined = jnp.concatenate([k.low[rows], got], 1)
            hidden = dense(joined, k.first[...]) + vec(k, at, 0)
            k.hidden[rows] = hidden
            out, normed, inverse = forward_rows(k, at, hidden, k.inner[...])
            k.normed[rows] = normed
            k.inverse[rows] = inverse
            k.wait(N_LATENT, t)
            k.final[rows] = (k.latent[rows] + out).astype(bf16)
            for name in (N_HIDDEN, N_NORMED, N_INVERSE, N_FINAL):
                k.flush(name, t)

        loop(grid // TILE, tile)
        k.wait(N_HEAD)
        k.wait(N_STATE)
        k.wait(N_TARGET)
        update = dense_right(k.head[...], k.final[...])
        new_state = k.state[...] + k.delta[...] * update
        k.new_state[...] = new_state
        miss = (new_state - k.target[...]) / k.delta[...]
        k.miss[...] = miss
        weight = k.plan[step].astype(f32)
        k.loss[...] = weight * jnp.sum(k.area[...] * miss * miss, keepdims=True)

    parts = grid // TILE
    out = launch(
        body,
        [
            (N_NODE_LOW, node_low, N_V),
            (N_ASSIGN, assign, N_V),
            (N_VECTORS, vectors, N_V),
            (N_DELTA, delta, N_V),
            (N_AREA, area, N_V),
            (N_PLAN, plan, N_S),
            (N_FIRST,) + first,
            (N_LOW, low, N_H, ((), parts)),
            (N_INNER,) + inner,
            (N_LATENT, latent, N_H, ((), parts)),
            (N_HEAD,) + head,
            (N_STATE, state, N_H, ((), 1)),
            (N_TARGET, target, N_H, ((step,), 1)),
        ],
        [
            ("new_state", (depth, grid), f32, N_V, 1),
            (N_MISS, (depth, grid), f32, N_V, 1),
            ("loss", (1, 1), f32, N_B, 1),
            (N_HIDDEN, (grid, D), f32, N_H, parts),
            (N_NORMED, (grid, D), f32, N_H, parts),
            (N_INVERSE, (grid, 1), f32, N_H, parts),
            (N_FINAL, (grid, D), bf16, N_H, parts),
        ],
        micros=7,
    )
    kept = {
        N_MISS: out[1],
        N_HIDDEN: out[3],
        N_NORMED: out[4],
        N_INVERSE: out[5],
        N_FINAL: out[6],
        N_LOW: low,
        N_NODE_LOW: node_low,
    }
    return out[0], out[2], kept


def grads_io(outs, scratch, grads, rows, swap):
    shape = (BLOCKS, rows, BLOCK)
    if swap is None:
        outs.append((N_GRADS, shape, f32, N_H, BLOCKS))
    elif grads is None:
        scratch.append((N_GRADS, shape, f32))


def flush_grads(k, swap):
    if swap is None:
        k.flush(N_GRADS)
    else:
        k.flush_swap()


def decoder_backward(
    step, regions, d_state, kept, weights, vectors, assign_row, delta, area, plan, inverse_total, grads, sums,
    swap,
):
    miss = kept[N_MISS]
    depth, grid = miss.shape
    first, inner, head = weights
    at = 2 + 2 * LAYERS
    fresh = grads is None
    more = d_state is not None
    keep_state = step > 0
    rows_all = up_to(3 * D + depth, CODED * regions)

    def body(k):
        k.wait(N_MISS)
        coefficient = 2.0 * k.inverse_total[0, 0] * k.plan[step].astype(f32)
        d_next = coefficient * k.area[...] * k.miss[...] / k.delta[...]
        if more:
            k.wait(N_D_STATE)
            d_next = k.d_state[...] + d_next
        if keep_state:
            k.d_next[...] = d_next
            k.flush(N_D_NEXT)
        k.d_update[...] = (d_next * k.delta[...]).astype(bf16)
        start_sums(k, fresh)
        k.wait(N_HEAD)
        k.wait(N_INNER)
        k.wait(N_FIRST)

        def tile(t):
            rows = row_tile(t, TILE)
            for name in (N_HIDDEN, N_NORMED, N_INVERSE):
                k.wait(name, t)
            d_final = dense_left(k.d_update[:, rows], k.head[...])
            act, d_mixed, d_hidden = backward_rows(
                k, at, d_final, k.hidden[rows], k.normed[rows], k.inverse[rows],
                k.inner[...], k.sums, 0,
            )
            k.act[rows] = act
            k.d_mixed[rows] = d_mixed
            k.d_hidden[rows] = d_hidden
            k.d_grid[rows] = d_final + dense_right(d_hidden, k.first[0:D])
            k.flush(N_D_GRID, t)

        loop(grid // TILE, tile)
        k.flush(N_SUMS)
        gathered = dense(cols_hot(k.assign_row[...], NODE_CAP), k.d_hidden[...])
        high, rest = halves(gathered)
        k.d_nodes[...] = dense_right(high, k.first[D : 2 * D]) + dense_right(rest, k.first[D : 2 * D])
        if not fresh:
            k.wait(N_GRADS)
        k.wait(N_LOW)
        k.wait(N_FINAL)
        weight_grad(k, fresh, 0, k.low, k.d_hidden)
        put_grad(k, fresh, D, dense_left(k.node_low[...], high) + dense_left(k.node_low[...], rest))
        weight_grad(k, fresh, 2 * D, k.act, k.d_mixed)
        put_grad(k, fresh, 3 * D, dense(k.d_update[...], k.final[...]))
        if fresh and rows_all > 3 * D + depth:
            k.grads[:, 3 * D + depth :, :] = jnp.zeros(
                (BLOCKS, rows_all - 3 * D - depth, BLOCK), f32
            )
        flush_grads(k, swap)

    parts = grid // TILE
    ins = [
        (N_MISS, miss, N_H, ((), 1)),
        (N_AREA, area, N_V),
        (N_DELTA, delta, N_V),
        ("assign_row", assign_row, N_V),
        (N_VECTORS, vectors, N_V),
        (N_NODE_LOW, kept[N_NODE_LOW], N_V),
        (N_PLAN, plan, N_S),
        ("inverse_total", inverse_total, N_S),
    ]
    if more:
        ins.append((N_D_STATE, d_state, N_H, ((), 1)))
    ins += [
        (N_HEAD,) + head,
        (N_HIDDEN, kept[N_HIDDEN], N_H, ((), parts)),
        (N_NORMED, kept[N_NORMED], N_H, ((), parts)),
        (N_INVERSE, kept[N_INVERSE], N_H, ((), parts)),
        (N_INNER,) + inner,
        (N_FIRST,) + first,
        (N_LOW, kept[N_LOW], N_H, ((), 1)),
        (N_FINAL, kept[N_FINAL], N_H, ((), 1)),
    ]
    outs = [
        (N_D_NODES, (NODE_CAP, D), f32, N_V, 1),
        (N_D_GRID, (grid, D), f32, N_H, parts),
    ]
    if keep_state:
        outs.append((N_D_NEXT, (depth, grid), f32, N_H, 1))
    scratch = [
        ("d_update", (depth, grid), bf16),
        (N_ACT, (grid, D), bf16),
        (N_D_MIXED, (grid, D), bf16),
        (N_D_HIDDEN, (grid, D), bf16),
    ]
    if not fresh:
        ins += [(N_SUMS, sums, N_H, ((), 1)), (N_GRADS, grads, N_H, ((), BLOCKS))]
    outs.append((N_SUMS, (8, D), f32, N_H, 1))
    grads_io(outs, scratch, grads, rows_all, swap)
    out = launch(
        body, ins, outs, scratch, micros=13, swap=swap
    )
    if keep_state:
        return out[0], out[1], out[2], out[3], out[4:]
    return out[0], out[1], None, out[2], out[3:]


def layer_backward(
    layer, d_nodes, returned, d_edges, kept, weights, vectors, send_row, recv, picks_row,
    sums, after,
):
    count = kept[N_HIDDEN].shape[0]
    halo_rows = kept[N_HALO].shape[0]
    edge_first, edge_inner, node_first, node_inner = weights
    at_edge, at_node = 2 + layer, 2 + LAYERS + layer
    top = d_edges is None

    def body(k):
        start_sums(k, sums is None)
        k.wait(N_D_NODES)
        if not top:
            high, rest = halves(k.returned[...])
            hot = cols_hot(k.picks_row[...], NODE_CAP)
            k.d_nodes[...] += dense(hot, high) + dense(hot, rest)
        for name in (N_NODE_HIDDEN, N_NODE_NORMED, N_NODE_INVERSE, N_NODE_INNER, N_NODE_FIRST):
            k.wait(name)

        def node_tile(t):
            rows = row_tile(t, TILE)
            act, d_mixed, d_hidden = backward_rows(
                k, at_node, k.d_nodes[rows], k.node_hidden[rows], k.node_normed[rows],
                k.node_inverse[rows], k.node_inner[...], k.sums, 3,
            )
            k.node_act[rows] = act
            k.node_d_mixed[rows] = d_mixed
            k.node_d_hidden[rows] = d_hidden
            d_in = dense_right(d_hidden, k.node_first[...])
            k.d_nodes[rows] += d_in[:, 0:D]
            high, rest = halves(d_in[:, D : 2 * D])
            k.d_total[rows, 0:D] = high
            k.d_total[rows, D : 2 * D] = rest

        loop(NODE_CAP // TILE, node_tile)
        for name in (N_D_NODES, N_NODE_ACT, N_NODE_D_MIXED, N_NODE_D_HIDDEN):
            k.flush(name)
        k.wait(N_EDGE_INNER)
        k.wait(N_EDGE_FIRST)

        def tile(t):
            rows = row_tile(t, TILE)
            both = dense(rows_hot(k.recv[rows], NODE_CAP), k.d_total[...])
            upstream = both[:, 0:D] + both[:, D : 2 * D]
            if not top:
                k.wait(N_D_EDGES, t)
                upstream = k.d_edges[rows] + upstream
            for name in (N_HIDDEN, N_NORMED, N_INVERSE):
                k.wait(name, t)
            act, d_mixed, d_hidden = backward_rows(
                k, at_edge, upstream, k.hidden[rows], k.normed[rows], k.inverse[rows],
                k.edge_inner[...], k.sums, 0,
            )
            k.act[rows] = act
            k.d_mixed[rows] = d_mixed
            k.d_hidden[rows] = d_hidden
            k.d_edges[rows] = upstream + dense_right(d_hidden, k.edge_first[0:D])
            for name in (N_ACT, N_D_MIXED, N_D_HIDDEN, N_D_EDGES):
                k.flush(name, t)

        loop(count // TILE, tile)
        k.flush(N_SUMS)
        to_halo = dense(cols_hot(k.send_row[...], halo_rows, NODE_CAP), k.d_hidden[...])
        high, rest = halves(to_halo)
        from_send = k.edge_first[D : 2 * D]
        k.d_halo[...] = dense_right(high, from_send) + dense_right(rest, from_send)
        k.halo_high[...] = high
        k.halo_rest[...] = rest

    parts = count // TILE
    ins = [
        (N_RECV, recv, N_V),
        (N_SEND_ROW, send_row, N_V),
        (N_VECTORS, vectors, N_V),
    ]
    if not top:
        ins += [(N_RETURNED, returned, N_V), (N_PICKS_ROW, picks_row, N_V)]
    ins += [
        (N_D_NODES, d_nodes, N_H, ((), 1)),
        (N_NODE_HIDDEN, kept[N_NODE_HIDDEN], N_H, ((), 1)),
        (N_NODE_NORMED, kept[N_NODE_NORMED], N_H, ((), 1)),
        (N_NODE_INVERSE, kept[N_NODE_INVERSE], N_H, ((), 1)),
        (N_NODE_INNER,) + node_inner,
        (N_NODE_FIRST,) + node_first,
        (N_EDGE_INNER,) + edge_inner,
        (N_EDGE_FIRST,) + edge_first,
    ]
    if sums is not None:
        ins.append((N_SUMS, sums, N_H, ((), 1)))
    if not top:
        ins.append((N_D_EDGES, d_edges, N_H, ((), parts)))
    ins += [
        (N_HIDDEN, kept[N_HIDDEN], N_H, ((), parts)),
        (N_NORMED, kept[N_NORMED], N_H, ((), parts)),
        (N_INVERSE, kept[N_INVERSE], N_H, ((), parts)),
    ]
    outs = [
        (N_D_HALO, (halo_rows, D), f32, N_V, 1),
        (N_HALO_HIGH, (halo_rows, D), bf16, N_V, 1),
        (N_HALO_REST, (halo_rows, D), bf16, N_V, 1),
        (N_D_NODES, (NODE_CAP, D), f32, N_H, 1),
        (N_NODE_ACT, (NODE_CAP, D), bf16, N_H, 1),
        (N_NODE_D_MIXED, (NODE_CAP, D), bf16, N_H, 1),
        (N_NODE_D_HIDDEN, (NODE_CAP, D), bf16, N_H, 1),
        (N_ACT, (count, D), bf16, N_H, parts),
        (N_D_MIXED, (count, D), bf16, N_H, parts),
        (N_D_HIDDEN, (count, D), bf16, N_H, parts),
        (N_D_EDGES, (count, D), f32, N_H, parts),
        (N_SUMS, (8, D), f32, N_H, 1),
    ]
    scratch = [("d_total", (NODE_CAP, 2 * D), bf16)]
    out = launch(body, ins, outs, scratch, micros=14, after=after)
    names = [item[0] for item in outs]
    return dict(zip(names, out))


def layer_grads(found, kept, edge_first, send_row, recv_row, rows_all, grads, swap, after):
    count = kept[N_HIDDEN].shape[0]
    halo_rows = kept[N_HALO].shape[0]
    fresh = grads is None

    def body(k):
        k.wait(N_D_HIDDEN)
        k.wait(N_FROM_SEND)
        k.wait(N_FROM_RECV)
        to_recv = dense(cols_hot(k.recv_row[...], NODE_CAP), k.d_hidden[...])
        to_send = dense(cols_hot(k.send_row[...], NODE_CAP), k.d_hidden[...])
        recv_high, recv_rest = halves(to_recv)
        send_high, send_rest = halves(to_send)
        from_send, from_recv = k.from_send[...], k.from_recv[...]
        k.wait(N_D_NODES)
        k.d_nodes[...] += (
            dense_right(send_high, from_send)
            + dense_right(send_rest, from_send)
            + dense_right(recv_high, from_recv)
            + dense_right(recv_rest, from_recv)
        )
        k.flush(N_D_NODES)
        if not fresh:
            k.wait(N_GRADS)
        low = k.node_low[...]
        put_grad(
            k, fresh, D,
            dense_left(low, send_high)
            + dense_left(low, send_rest)
            + dense_left(k.halo[...], k.halo_high[...])
            + dense_left(k.halo[...], k.halo_rest[...]),
        )
        put_grad(k, fresh, 2 * D, dense_left(low, recv_high) + dense_left(low, recv_rest))
        k.wait(N_EDGES_LOW)
        weight_grad(k, fresh, 0, k.edges_low, k.d_hidden)
        k.wait(N_ACT)
        k.wait(N_D_MIXED)
        weight_grad(k, fresh, 3 * D, k.act, k.d_mixed)
        if swap is not None:
            k.flush_swap(0)
        k.wait(N_TOTAL)
        k.wait(N_NODE_D_HIDDEN)
        weight_grad(k, fresh, 4 * D, k.node_low, k.node_d_hidden)
        weight_grad(k, fresh, 5 * D, k.total, k.node_d_hidden)
        k.wait(N_NODE_ACT)
        k.wait(N_NODE_D_MIXED)
        weight_grad(k, fresh, 6 * D, k.node_act, k.node_d_mixed)
        if fresh and rows_all > 7 * D:
            k.grads[:, 7 * D :, :] = jnp.zeros((BLOCKS, rows_all - 7 * D, BLOCK), f32)
        if swap is None:
            k.flush(N_GRADS)
        else:
            k.flush_swap(1)

    source, _, (first, _) = edge_first
    ins = [
        (N_NODE_LOW, kept[N_NODE_LOW], N_V),
        (N_HALO, kept[N_HALO], N_V),
        (N_HALO_HIGH, found[N_HALO_HIGH], N_V),
        (N_HALO_REST, found[N_HALO_REST], N_V),
        (N_RECV_ROW, recv_row, N_V),
        (N_SEND_ROW, send_row, N_V),
        (N_D_HIDDEN, found[N_D_HIDDEN], N_H, ((), 1)),
        (N_FROM_SEND, source, N_W, (first + D, D)),
        (N_FROM_RECV, source, N_W, (first + 2 * D, D)),
        (N_D_NODES, found[N_D_NODES], N_H, ((), 1)),
    ]
    if not fresh:
        ins.append((N_GRADS, grads, N_H, ((), BLOCKS)))
    ins += [
        (N_EDGES_LOW, kept[N_EDGES_LOW], N_H, ((), 1)),
        (N_ACT, found[N_ACT], N_H, ((), 1)),
        (N_D_MIXED, found[N_D_MIXED], N_H, ((), 1)),
        (N_TOTAL, kept[N_TOTAL], N_H, ((), 1)),
        (N_NODE_D_HIDDEN, found[N_NODE_D_HIDDEN], N_H, ((), 1)),
        (N_NODE_ACT, found[N_NODE_ACT], N_H, ((), 1)),
        (N_NODE_D_MIXED, found[N_NODE_D_MIXED], N_H, ((), 1)),
    ]
    outs = [(N_D_NODES, (NODE_CAP, D), f32, N_H, 1)]
    scratch = []
    grads_io(outs, scratch, grads, rows_all, swap)
    out = launch(body, ins, outs, scratch, micros=14, swap=swap, after=after)
    return out[0], out[1:]


def encoder_backward(
    step, d_grid, d_nodes, returned, d_next, kept, weights, vectors, assign, picks_row, scales,
    grads, sums, others, swap, after,
):
    feats = kept[N_FEATS]
    depth, grid = feats.shape
    first, inner = weights
    fresh = grads is None
    keep_state = step > 0
    rows_all = depth + D
    if others is not None:
        embed_grads, all_sums = others
        embed_rows = embed_grads.shape[1]
        at_vectors = depth + D + embed_rows
        rows_all = swap[1]

    def body(k):
        start_sums(k, fresh)
        k.wait(N_D_NODES)
        high, rest = halves(k.returned[...])
        hot = cols_hot(k.picks_row[...], NODE_CAP)
        nodes = k.d_nodes[...] + dense(hot, high) + dense(hot, rest)
        high, rest = halves(nodes)
        k.both[:, 0:D] = high
        k.both[:, D : 2 * D] = rest
        k.wait(N_INNER)

        def tile(t):
            rows = row_tile(t, TILE)
            for name in (N_HIDDEN, N_NORMED, N_INVERSE, N_D_GRID):
                k.wait(name, t)
            both = dense(rows_hot(k.assign[rows], NODE_CAP), k.both[...])
            upstream = k.d_grid[rows] + both[:, 0:D] + both[:, D : 2 * D]
            act, d_mixed, d_hidden = backward_rows(
                k, 0, upstream, k.hidden[rows], k.normed[rows], k.inverse[rows],
                k.inner[...], k.sums, 0,
            )
            k.act[rows] = act
            k.d_mixed[rows] = d_mixed
            k.d_hidden[rows] = d_hidden

        loop(grid // TILE, tile)
        if keep_state:
            k.wait(N_FIRST)
            k.wait(N_D_NEXT)
            k.d_state[...] = (
                k.d_next[...] + dense_right(k.first[...], k.d_hidden[...]) / k.scales[...]
            )
            k.flush(N_D_STATE)
        k.wait(N_FEATS)
        if others is None:
            k.flush(N_SUMS)
            put_grad(k, True, 0, dense(k.feats[...], k.d_hidden[...]))
            weight_grad(k, True, depth, k.act, k.d_mixed)
            k.flush(N_GRADS)
            return
        k.wait(N_BEFORE)
        k.grads[:, 0 : depth + D, :] = k.before[...]
        put_grad(k, False, 0, dense(k.feats[...], k.d_hidden[...]))
        weight_grad(k, False, depth, k.act, k.d_mixed)
        k.wait(N_EMBED_GRADS)
        k.grads[:, depth + D : at_vectors, :] = k.embed_grads[...]
        k.grads[:, at_vectors:, :] = jnp.zeros((BLOCKS, rows_all - at_vectors, BLOCK), f32)
        sources = [(k.sums, 0), (k.sums_embed, 0)]
        sources += [(getattr(k, N_SUMS_ + str(l)), 0) for l in range(LAYERS)]
        sources += [(getattr(k, N_SUMS_ + str(l)), 3) for l in range(LAYERS)]
        sources += [(k.sums_dec, 0)]
        for i, (source, at) in enumerate(sources):
            set_grad(k, at_vectors + 3 * i, source[at : at + 3, :])
        k.flush_swap()

    parts = grid // TILE
    ins = [
        (N_RETURNED, returned, N_V),
        (N_PICKS_ROW, picks_row, N_V),
        (N_ASSIGN, assign, N_V),
        (N_SCALES, scales, N_V),
        (N_VECTORS, vectors, N_V),
        (N_D_NODES, d_nodes, N_H, ((), 1)),
        (N_INNER,) + inner,
        (N_D_GRID, d_grid, N_H, ((), parts)),
        (N_HIDDEN, kept[N_HIDDEN], N_H, ((), parts)),
        (N_NORMED, kept[N_NORMED], N_H, ((), parts)),
        (N_INVERSE, kept[N_INVERSE], N_H, ((), parts)),
        (N_FEATS, feats, N_H, ((), 1)),
    ]
    outs = []
    if keep_state:
        ins += [(N_FIRST,) + first, (N_D_NEXT, d_next, N_H, ((), 1))]
        outs.append((N_D_STATE, (depth, grid), f32, N_H, 1))
    scratch = [
        ("both", (NODE_CAP, 2 * D), bf16),
        (N_ACT, (grid, D), bf16),
        (N_D_MIXED, (grid, D), bf16),
        (N_D_HIDDEN, (grid, D), bf16),
    ]
    if not fresh:
        ins.append((N_SUMS, sums, N_H, ((), 1)))
    if others is None:
        outs.append((N_SUMS, (8, D), f32, N_H, 1))
        outs.append((N_GRADS, (BLOCKS, rows_all, BLOCK), f32, N_H, BLOCKS))
    else:
        ins.append((N_BEFORE, grads, N_H, ((), BLOCKS)))
        ins.append((N_EMBED_GRADS, embed_grads, N_H, ((), BLOCKS)))
        ins += [(N_SUMS_ + str(name), value, N_V) for name, value in all_sums.items()]
        scratch.append((N_GRADS, (BLOCKS, rows_all, BLOCK), f32))
    out = launch(body, ins, outs, scratch, micros=10, swap=swap, after=after)
    if others is not None:
        return out
    return out if keep_state else (None, out[0], out[1])


def embed_backward(d_first, d_second, kept, geometry, inner, vectors, after):
    count = kept[N_HIDDEN].shape[0]
    features = geometry.shape[0]

    def body(k):
        start_sums(k, True)
        k.wait(N_INNER)

        def tile(t):
            rows = row_tile(t, TILE)
            for name in (N_D_FIRST, N_D_SECOND, N_HIDDEN, N_NORMED, N_INVERSE):
                k.wait(name, t)
            act, d_mixed, d_hidden = backward_rows(
                k, 1, k.d_first[rows] + k.d_second[rows], k.hidden[rows], k.normed[rows],
                k.inverse[rows], k.inner[...], k.sums, 0,
            )
            k.act[rows] = act
            k.d_mixed[rows] = d_mixed
            k.d_hidden[rows] = d_hidden

        loop(count // TILE, tile)
        k.flush(N_SUMS)
        set_grad(k, 0, dense(k.geometry[...], k.d_hidden[...]))
        weight_grad(k, True, features, k.act, k.d_mixed)
        k.flush(N_GRADS)

    parts = count // TILE
    ins = [
        (N_GEOMETRY, geometry, N_V),
        (N_VECTORS, vectors, N_V),
        (N_INNER,) + inner,
        (N_D_FIRST, d_first, N_H, ((), parts)),
        (N_D_SECOND, d_second, N_H, ((), parts)),
        (N_HIDDEN, kept[N_HIDDEN], N_H, ((), parts)),
        (N_NORMED, kept[N_NORMED], N_H, ((), parts)),
        (N_INVERSE, kept[N_INVERSE], N_H, ((), parts)),
    ]
    return launch(
        body,
        ins,
        [
            (N_SUMS, (8, D), f32, N_H, 1),
            (N_GRADS, (BLOCKS, features + D, BLOCK), f32, N_H, BLOCKS),
        ],
        [
            (N_ACT, (count, D), bf16),
            (N_D_MIXED, (count, D), bf16),
            (N_D_HIDDEN, (count, D), bf16),
        ],
        micros=11,
        after=after,
    )


def coded_rows(rows):
    return rows + up_to(rows // CODED, 16)


def encode(source, first, rows, target, scale):
    scale[...] = jnp.zeros(scale.shape, f32)

    def step(t):
        value = source[pl.ds(pl.multiple_of(first + t * CODED, CODED), CODED)]
        top = jnp.maximum(jnp.max(jnp.abs(value), 0, keepdims=True), 1e-30)
        exponent = jnp.ceil(jnp.log2(top))
        scale[pl.ds(t, 1), :] = exponent
        value = jnp.round(value * (CODE_TOP * jnp.exp2(-exponent)))
        target[row_tile(t, CODED)] = value.astype(jnp.int32).astype(jnp.int16)

    loop(rows // CODED, step, 8)
    more = coded_rows(rows) - rows
    target[rows : rows + more] = scale[0:more].astype(jnp.int32).astype(jnp.int16)


def scales_of(coded, rows, scale):
    more = coded_rows(rows) - rows
    exponent = coded[rows : rows + more].astype(jnp.int32).astype(f32)
    scale[0:more] = jnp.exp2(exponent) * (1.0 / CODE_TOP)


def decoded(coded, scale, t):
    return coded[row_tile(t, CODED)].astype(jnp.int32).astype(f32) * scale[pl.ds(t, 1), :]


def difference(p, order):
    return sum(bit for i, bit in enumerate(reversed(order)) if p >> i & 1)


CORES, OVER_X, TURN, JOIN, ALL = range(5)


def combine(jobs, order, after):
    regions = 2 ** len(order)
    operands, out_shape, scratch_shapes, plans = [], [], [], []
    squares = False

    def buffer(shape, dtype):
        scratch_shapes.append(pltpu.VMEM(shape, dtype))
        return len(scratch_shapes) - 1

    def output(shape, dtype):
        out_shape.append(jax.ShapeDtypeStruct(shape, dtype))
        return len(out_shape) - 1

    for kind, arrays, ways in jobs:
        loads, stores = [], []
        for array in arrays:
            loads.append((len(operands), buffer(array.shape, array.dtype)))
            operands.append(array)
        blocks, size = 1, 0
        if kind == CORES:
            size = arrays[0].shape[0]
            stores.append((output((size, BLOCK), f32), loads[0][1], None))
        elif kind == JOIN:
            shape = arrays[0].shape
            at = output((len(arrays) * shape[0],) + shape[1:], jnp.int16)
            stores = [(at, item[1], i * shape[0]) for i, item in enumerate(loads)]
        elif kind == ALL:
            code = arrays[0].shape[1]
            size = max(r for r in range(CODED, code, CODED) if coded_rows(r) == code)
            at = output((regions, code, BLOCK), jnp.int16)
            kept = buffer((1, code, BLOCK), jnp.int16)
            stores = [(at, kept, i) for i in range(regions)]
            squares = True
        else:
            rows = arrays[0].shape[0]
            if kind == OVER_X:
                size = rows // regions
            else:
                code = arrays[1].shape[1]
                size = max(r for r in range(CODED, code, CODED) if coded_rows(r) == code)
            blocks = rows // size // max(ways, 1)
            if ways > 1:
                at = output((blocks * size, BLOCK), f32)
                stores.append((at, buffer((blocks * size, BLOCK), f32), None))
            elif ways == 1:
                squares = True
        if kind not in (JOIN, ALL):
            for _ in range(max(ways - 1, 1)):
                shape = (blocks, coded_rows(size), BLOCK)
                stores.append((output(shape, jnp.int16), buffer(shape, jnp.int16), None))
        work = None
        if kind != JOIN:
            rows = size if kind == ALL else arrays[0].shape[0]
            work = (buffer((rows, BLOCK), f32), buffer((up_to(rows // CODED, 16), BLOCK), f32))
        plans.append((kind, ways, blocks, size, loads, stores, work))
    count = len(out_shape)
    if squares:
        out_shape.append(jax.ShapeDtypeStruct((CODED, BLOCK), f32))
    most = max(len(plan[5]) for plan in plans)

    def kernel(*refs):
        region = lax.axis_index(N_REGION)
        ins = refs[: len(operands)]
        outs = refs[len(operands) + len(after) :][: len(out_shape)]
        rest = refs[len(operands) + len(after) + len(out_shape) :]
        sem_in, sem_out = rest[-2:]

        def load(at, kept):
            return pltpu.make_async_copy(ins[at], rest[kept], sem_in.at[at])

        def store(job, i):
            at, kept, first = plans[job][5][i]
            target = outs[at]
            if first is not None:
                target = target.at[pl.ds(first, rest[kept].shape[0])]
            return pltpu.make_async_copy(rest[kept], target, sem_out.at[job, i])

        def add_squares(total, rows):
            def step(t):
                value = total[row_tile(t, CODED)]
                outs[-1][...] += value * value

            loop(rows // CODED, step, 8)

        for plan in plans:
            for item in plan[4]:
                load(*item).start()
        if squares:
            outs[-1][...] = jnp.zeros((CODED, BLOCK), f32)
        for job, (kind, ways, blocks, size, loads, stores, work) in enumerate(plans):
            for item in loads:
                load(*item).wait()
            values = [rest[item[1]] for item in loads]
            results = [rest[item[1]] for item in stores]
            if kind == CORES:
                total, scale = rest[work[0]], rest[work[1]]

                def step(t):
                    at = row_tile(t, 256)
                    values[0][at] += values[1][at]
                    total[at] = values[2][at] + values[3][at]

                loop(size // 256, step)
                encode(total, 0, size, results[1].at[0], scale)
            elif kind == ALL:
                total, scale = rest[work[0]], rest[work[1]]
                total[...] = jnp.zeros((size, BLOCK), f32)
                for i in range(regions):
                    scales_of(values[0].at[i], size, scale)

                    def step(t):
                        total[row_tile(t, CODED)] += decoded(values[0].at[i], scale, t)

                    loop(size // CODED, step, 8)
                encode(total, 0, size, results[0].at[0], scale)
                add_squares(total, size)
            elif kind != JOIN:
                total, scale = rest[work[0]], rest[work[1]]
                mine = values[0]
                if kind == OVER_X:
                    rows = size * regions
                    scales_of(values[1].at[0], rows, scale)

                    def step(t):
                        at = row_tile(t, CODED)
                        total[at] = mine[at] + decoded(values[1].at[0], scale, t)

                    loop(rows // CODED, step, 8)
                else:
                    for i in range(blocks * ways):
                        for j, coded in enumerate(values[1:]):
                            scales_of(coded.at[i], size, scale)

                            def step(t):
                                at = pl.ds(pl.multiple_of(i * size + t * CODED, CODED), CODED)
                                value = total[at] if j else mine[at]
                                total[at] = value + decoded(coded.at[i], scale, t)

                            loop(size // CODED, step, 8)

                def first_row(p):
                    if kind == OVER_X and ways:
                        return lax.bitwise_xor(region, difference(p, order)) * size
                    return p * size

                for p in range(blocks * max(ways, 1)):
                    way, i = p // blocks, p % blocks
                    if ways > 1 and way == 0:

                        def step(t):
                            at = pl.ds(pl.multiple_of(first_row(p) + t * CODED, CODED), CODED)
                            to = pl.ds(pl.multiple_of(i * size + t * CODED, CODED), CODED)
                            results[0][to] = total[at]

                        loop(size // CODED, step, 8)
                    else:
                        encode(total, first_row(p), size, results[way].at[i], scale)
                if ways == 1:
                    add_squares(total, size)
            for i in range(len(stores)):
                store(job, i).start()
        for job in range(len(plans)):
            for i in range(len(plans[job][5])):
                store(job, i).wait()

    any_space = pl.BlockSpec(memory_space=pl.ANY)
    out_specs = [any_space] * count
    if squares:
        out_specs.append(pl.BlockSpec(memory_space=pltpu.VMEM))
    out = pl.pallas_call(
        kernel,
        out_shape=out_shape,
        in_specs=[any_space] * (len(operands) + len(after)),
        out_specs=out_specs,
        scratch_shapes=scratch_shapes
        + [
            pltpu.SemaphoreType.DMA((len(operands),)),
            pltpu.SemaphoreType.DMA((len(jobs), most)),
        ],
        compiler_params=pltpu.CompilerParams(vmem_limit_bytes=56 * 2**20),
        cost_estimate=cost_of(5),
    )(*operands, *after)
    parts = []
    for plan in plans:
        found = []
        for item in plan[5]:
            if item[0] not in found:
                found.append(item[0])
        parts.append([out[i] for i in found])
    return parts, (out[-1] if squares else None)


def pack(pieces, after):
    sizes = [array.shape[-2] for array, _, _ in pieces]
    firsts = [sum(rows for _, _, rows in pieces[:i]) for i in range(len(pieces) + 1)]

    def kernel(*refs):
        ins = refs[: len(pieces)]
        out = refs[len(pieces) + len(after)]
        packed, sem_in, sem_out = refs[-3:]
        buffers = refs[len(pieces) + len(after) + 1 : -3]

        def load(i):
            source = ins[i] if pieces[i][1] is None else ins[i].at[pieces[i][1]]
            target = buffers[i]
            if sizes[i] < pieces[i][2]:
                target = target.at[pl.ds(0, sizes[i])]
            return pltpu.make_async_copy(source, target, sem_in.at[i])

        def store(i):
            rows = pl.ds(firsts[i], pieces[i][2])
            return pltpu.make_async_copy(packed.at[rows], out.at[rows], sem_out.at[i])

        for i, (_, _, rows) in enumerate(pieces):
            if sizes[i] < rows:
                buffers[i][...] = jnp.zeros((rows, BLOCK), f32)
            load(i).start()
        for i, (_, _, rows) in enumerate(pieces):
            load(i).wait()
            step = max(n for n in range(16, 257, 16) if rows % n == 0)
            for row in range(0, rows, step):
                at = firsts[i] + row
                packed[at : at + step] = buffers[i][row : row + step].astype(bf16)
            store(i).start()
        for i in range(len(pieces)):
            store(i).wait()

    any_space = pl.BlockSpec(memory_space=pl.ANY)
    return pl.pallas_call(
        kernel,
        out_shape=jax.ShapeDtypeStruct((firsts[-1], BLOCK), bf16),
        in_specs=[any_space] * (len(pieces) + len(after)),
        out_specs=any_space,
        scratch_shapes=[pltpu.VMEM((rows, BLOCK), f32) for _, _, rows in pieces]
        + [
            pltpu.VMEM((firsts[-1], BLOCK), bf16),
            pltpu.SemaphoreType.DMA((len(pieces),)),
            pltpu.SemaphoreType.DMA((len(pieces),)),
        ],
        compiler_params=pltpu.CompilerParams(vmem_limit_bytes=56 * 2**20),
        cost_estimate=cost_of(2),
    )(*[array for array, _, _ in pieces], *after)


def update_weights(factor, place, order, groups, masters, moments, squares, chunks):
    count = len(masters)
    rows_of = [c[3] for c in chunks]
    places = 2 ** len(order)
    starts = [0]
    for group in groups:
        starts.append(starts[-1] + len(group))
    flat_first = [0]
    for master in masters:
        flat_first.append(flat_first[-1] + master.size // BLOCK)
    block_rows = []
    for group in groups:
        code = group[0].shape[1]
        block_rows.append(max(r for r in range(CODED, code, CODED) if coded_rows(r) == code))

    def kernel(*refs):
        scale = refs[0][0, 0]
        region = refs[1][1]
        group_refs = refs[2 : 2 + starts[-1]]
        at = 2 + starts[-1]
        param_refs = refs[at : at + 3 * count]
        out_refs = refs[at + 3 * count : at + 6 * count]
        flat_out = refs[at + 6 * count]
        rest = refs[at + 6 * count + 1 :]
        sem_in, sem_out, sem_grad = rest[-3:]
        factors, flat = rest[-5:-3]
        coded_refs = rest[3 * len(chunks) :][: starts[-1]]
        grad_refs = rest[3 * len(chunks) + starts[-1] :][: len(groups)]

        def grad_copies(g):
            return [
                pltpu.make_async_copy(group_refs[i], coded_refs[i], sem_grad.at[i])
                for i in range(starts[g], starts[g + 1])
            ]

        def decode(g):
            rows = block_rows[g]

            for p in range(places):
                if starts[g + 1] - starts[g] == 2:
                    coded = coded_refs[starts[g] + 2 * p // places].at[p % (places // 2)]
                    first = lax.bitwise_xor(region, difference(p, order)) * rows
                else:
                    coded, first = coded_refs[starts[g]].at[p], p * rows
                scales_of(coded, rows, factors)

                def step(t):
                    at = pl.ds(pl.multiple_of(first + t * CODED, CODED), CODED)
                    grad_refs[g][at] = decoded(coded, factors, t)

                loop(rows // CODED, step, 8)

        def piece(ref, chunk):
            for i in chunk[1]:
                ref = ref.at[i]
            if chunk[3] < ref.shape[0]:
                ref = ref.at[pl.ds(chunk[2], chunk[3])]
            return ref

        def copies(i):
            chunk = chunks[i]
            w = chunk[0]
            found = []
            for j in range(3):
                found.append(
                    pltpu.make_async_copy(
                        piece(param_refs[3 * w + j], chunk), rest[3 * i + j], sem_in.at[3 * i + j]
                    )
                )
            return found

        def stores(i):
            chunk = chunks[i]
            return [
                pltpu.make_async_copy(
                    rest[3 * i + (j + 1) % 3],
                    piece(out_refs[3 * chunk[0] + j], chunk),
                    sem_out.at[3 * i + j],
                )
                for j in range(3)
            ]

        started = set()
        for i in range(len(chunks)):
            if chunks[i][4] not in started:
                started.add(chunks[i][4])
                for copy in grad_copies(chunks[i][4]):
                    copy.start()
            for copy in copies(i):
                copy.start()
        for i in range(len(chunks)):
            if chunks[i][4] in started:
                started.remove(chunks[i][4])
                for copy in grad_copies(chunks[i][4]):
                    copy.wait()
                decode(chunks[i][4])
            for copy in copies(i):
                copy.wait()
            master_ref, moment_ref, square_ref = rest[3 * i : 3 * i + 3]
            grad_ref, first_row = grad_refs[chunks[i][4]], chunks[i][5]

            flat_row = flat_first[chunks[i][0]] + chunks[i][2]
            if chunks[i][1]:
                flat_row += chunks[i][1][0] * masters[chunks[i][0]].shape[1]
            step = 128 if rows_of[i] % 128 == 0 else rows_of[i]
            for row in range(0, rows_of[i], step):
                rows = slice(row, row + step)
                first, second, master = adam(
                    master_ref[rows],
                    moment_ref[rows],
                    square_ref[rows],
                    grad_ref[first_row + row : first_row + row + step] * scale,
                )
                moment_ref[rows] = first
                square_ref[rows] = second
                master_ref[rows] = master
                flat[flat_row + row : flat_row + row + step] = master

            for copy in stores(i):
                copy.start()
        flat_copy = pltpu.make_async_copy(
            flat.at[pl.ds(0, flat_first[-1])], flat_out.at[:, 0], sem_out.at[3 * len(chunks)]
        )
        flat_copy.start()
        for i in range(len(chunks)):
            for copy in stores(i):
                copy.wait()
        flat_copy.wait()

    any_space = pl.BlockSpec(memory_space=pl.ANY)
    flat_shape = (up_to(flat_first[-1], 8), BLOCK)
    scratch_shapes = []
    for rows in rows_of:
        scratch_shapes += [pltpu.VMEM((rows, BLOCK), f32)] * 3
    coded_parts = [part for group in groups for part in group]
    scratch_shapes += [pltpu.VMEM(part.shape, part.dtype) for part in coded_parts]
    scratch_shapes += [pltpu.VMEM((places * rows, BLOCK), f32) for rows in block_rows]
    scratch_shapes.append(pltpu.VMEM((up_to(max(block_rows) // CODED, 16), BLOCK), f32))
    scratch_shapes.append(pltpu.VMEM(flat_shape, f32))
    scratch_shapes.append(pltpu.SemaphoreType.DMA((3 * len(chunks),)))
    scratch_shapes.append(pltpu.SemaphoreType.DMA((3 * len(chunks) + 1,)))
    scratch_shapes.append(pltpu.SemaphoreType.DMA((starts[-1],)))
    params = [value for item in zip(masters, moments, squares) for value in item]
    return pl.pallas_call(
        kernel,
        out_shape=[jax.ShapeDtypeStruct(p.shape, f32) for p in params]
        + [jax.ShapeDtypeStruct((flat_first[-1], 1, BLOCK), f32)],
        in_specs=[pl.BlockSpec(memory_space=pltpu.SMEM)] * 2
        + [any_space] * (len(coded_parts) + len(params)),
        out_specs=[any_space] * (len(params) + 1),
        scratch_shapes=scratch_shapes,
        compiler_params=pltpu.CompilerParams(vmem_limit_bytes=56 * 2**20),
        cost_estimate=cost_of(0),
    )(factor, place, *coded_parts, *params)


def adam(master, moment, square, grad):
    first = beta_first * moment + (1 - beta_first) * grad
    second = beta_second * square + (1 - beta_second) * grad * grad
    spread = second * (1.0 / (1 - beta_second**STEP_COUNT))
    root = spread * lax.rsqrt(jnp.maximum(spread, 1e-37))
    ratio = first * (1.0 / (1 - beta_first**STEP_COUNT)) / (root + adam_eps)
    return (first, second, master - learn_rate * (ratio + decay_weight * master))


def pad_rows(value, rows):
    return jnp.pad(value, ((0, rows - value.shape[0]), (0, 0)))


def body(
    initial_state,
    target_states,
    var_means,
    var_scales,
    delta_scales,
    edge_geometry,
    node_counts,
    edge_counts,
    receivers,
    senders,
    send_lists,
    grid_nodes,
    cell_area,
    step_weights,
    *params,
):
    masters, moments, squares = params[0::3], params[1::3], params[2::3]
    enc_w, embed_w, edge_w, node_w, dec_w, inner_w, vector_w, head_w = masters
    variables = enc_w.shape[0]
    depth = up_to(variables, 16)
    features = embed_w.shape[0]
    feature_rows = up_to(features, 16)
    vector_rows = up_to(vector_w.shape[0], 16)
    last_block = 2 + 2 * LAYERS

    def partner(value, axis, bit):
        count = lax.axis_size(axis)
        return lax.ppermute(value, axis, [(i, i ^ bit) for i in range(count)])

    place = jnp.stack([lax.axis_index(N_REP), lax.axis_index(N_REGION)]).astype(jnp.int32)

    def gather(pieces, after=()):
        return (place, lax.all_gather(pack(pieces, after), N_REP))

    start = gather(
        [
            (enc_w, None, depth),
            (inner_w, 0, D),
            (embed_w, None, feature_rows),
            (inner_w, 1, D),
            (vector_w, None, vector_rows),
        ]
    )
    of_layer = []
    for l in range(LAYERS):
        pieces = [(edge_w, l, 3 * D), (inner_w, 2 + l, D)]
        pieces += [(node_w, l, 2 * D), (inner_w, 2 + LAYERS + l, D)]
        of_layer.append(gather(pieces))
    end = gather(
        [(dec_w, None, 2 * D), (inner_w, last_block, D), (head_w, None, depth)]
    )
    enc_first = (start, N_W, (0, depth))
    enc_inner = (start, N_W, (depth, D))
    embed_first = (start, N_W, (depth + D, feature_rows))
    embed_inner = (start, N_W, (depth + D + feature_rows, D))
    at_vectors = depth + 2 * D + feature_rows
    vectors = start[1][:, at_vectors:].astype(f32).transpose(1, 0, 2).reshape(vector_rows, D)
    layer_weights = [
        (
            (of_layer[l], N_W, (0, 3 * D)),
            (of_layer[l], N_W, (3 * D, D)),
            (of_layer[l], N_W, (4 * D, 2 * D)),
            (of_layer[l], N_W, (6 * D, D)),
        )
        for l in range(LAYERS)
    ]
    dec_weights = (
        (end, N_W, (0, 2 * D)),
        (end, N_W, (2 * D, D)),
        (end, N_W, (3 * D, depth)),
    )

    count = node_counts[0]
    send_from = jnp.where(senders < NODE_CAP, senders % count, senders)
    live = jnp.arange(receivers.shape[0]) < edge_counts[0]
    recv = jnp.where(live, receivers, -1)
    picks = (send_lists[0] % count).reshape(-1)
    assign = grid_nodes % count
    regions, slots = send_lists.shape[1:]
    send, send_row = send_from[:, None], send_from[None, :]
    recv, recv_row = recv[:, None], recv[None, :]
    picks, picks_row = picks[:, None], picks[None, :]
    assign, assign_row = assign[:, None], assign[None, :]

    def exchange(rows):
        table = rows.reshape(regions, slots, D)
        table = lax.all_to_all(table, N_REGION, split_axis=0, concat_axis=0, tiled=True)
        return table.reshape(regions * slots, D)

    def column(value, fill):
        return jnp.pad(value, (0, depth - variables), constant_values=fill)[:, None]

    means, scales, delta = column(var_means, 0), column(var_scales, 1), column(delta_scales, 1)
    state = pad_rows(initial_state[0].T, depth)
    target = jnp.pad(
        target_states[0].transpose(0, 2, 1), ((0, 0), (0, depth - variables), (0, 0))
    )
    area = cell_area[None, :]
    geometry = pad_rows(edge_geometry.T, feature_rows).astype(bf16)
    plan = step_weights

    bits = [1 << i for i in range(regions.bit_length() - 1)]
    turns = [bits[:1]] + [bits[i : i + 2] for i in range(1, len(bits), 2)]
    unit = CODED * regions
    dec_rows, layer_rows = up_to(3 * D + depth, unit), up_to(7 * D, unit)
    start_rows = up_to(at_vectors + vector_rows, unit)

    weight_local = (
        jnp.sum(plan.astype(f32)) * jnp.sum(cell_area) * variables * lax.axis_size(N_REP)
    )
    weight_total = jnp.broadcast_to(weight_local, (8, BLOCK))
    for bit in bits:
        weight_total = weight_total + partner(weight_total, N_REGION, bit)
    weight_total = weight_total[0, 0]
    inverse_total = (1.0 / weight_total).reshape(1, 1)

    edges0, edges0_low, *keep_embed = embed_forward(geometry, embed_first, embed_inner, 1, vectors)
    keep_embed = dict(zip((N_HIDDEN, N_NORMED, N_INVERSE), keep_embed))
    records = []
    loss_local = 0.0
    for step in range(STEPS):
        nodes, node_low, outgoing, latent, low, feats, hidden, normed, inverse = encoder_forward(
            state, means, scales, enc_first, enc_inner, vectors, assign_row, picks
        )
        keep_enc = {N_FEATS: feats, N_HIDDEN: hidden, N_NORMED: normed, N_INVERSE: inverse}
        edges, edges_low = edges0, edges0_low
        layers = []
        for l in range(LAYERS):
            halo = exchange(outgoing)
            first = layer_weights[l][0]
            local = layer_local(l, edges_low, node_low, first, vectors, send, recv)
            from_send = (first[0], N_W, (first[2][0] + D, D))
            before = edges_low
            edges, edges_low, nodes, node_low, outgoing, kept = layer_forward(
                l, local, edges, nodes, node_low, halo, (from_send,) + layer_weights[l][1:],
                vectors, send, recv_row, picks, l == LAYERS - 1,
            )
            kept[N_EDGES_LOW] = before
            layers.append(kept)
        state, loss, keep_dec = decoder_forward(
            step, state, target, latent, low, node_low, dec_weights, vectors,
            assign, delta, area, plan,
        )
        loss_local = loss_local + loss[0, 0]
        records.append((keep_enc, layers, keep_dec))

    class Sum:
        def __init__(self, parts, at_once=False):
            self.parts = list(parts)
            self.at_once = at_once
            self.stage = -2
            self.halves = None

        def job(self):
            p, count = self.parts, len(turns)
            if self.stage == -2:
                return (CORES, [p[0], partner(p[1], N_REP, 1), p[2], partner(p[3], N_REP, 1)], 0)
            if self.stage == -1:
                ways = 0 if self.at_once else 2 ** len(turns[0])
                return (OVER_X, [p[0], partner(p[1], N_REP, 2)], ways)
            if self.at_once:
                return (ALL, [self.all_turn()], 1)
            if self.stage < count:
                turn, last = turns[self.stage], self.stage == count - 1
                ways = 1 if last else 2 ** len(turns[self.stage + 1])
                got = [
                    partner(p[q], N_REGION, difference(q, turn)) for q in range(1, 2 ** len(turn))
                ]
                return (TURN, [p[0]] + got, ways)
            turn = turns[2 * count - 1 - self.stage]
            got = [partner(p[0], N_REGION, difference(q, turn)) for q in range(1, 2 ** len(turn))]
            return (JOIN, [p[0]] + got, 0)

        def summed(self):
            return self.stage >= (1 if self.at_once else len(turns))

        def all_turn(self):
            return lax.all_to_all(
                self.parts[0], N_REGION, split_axis=0, concat_axis=0, tiled=True
            )

        def done(self, parts):
            self.parts = parts
            self.stage += 1
            if self.at_once:
                if self.stage == 1:
                    self.halves = [self.all_turn()]
                return
            if self.stage == 2 * len(turns) - 1:
                self.halves = [parts[0], partner(parts[0], N_REGION, bits[0])]

    def over_all(value):
        for bit in bits:
            value = value + partner(value, N_REGION, bit)
        for bit in (1, 2):
            value = value + partner(value, N_REP, bit)
        return value

    all_squares = []
    on_way = {}
    arrived = []

    def advance(names, after):
        names = [name for name in names if on_way[name].halves is None]
        if not names:
            return after
        jobs = [on_way[name].job() for name in names]
        parts, squares = combine(jobs, bits, list(after) + arrived)
        arrived.clear()
        if squares is not None:
            all_squares.append(jnp.sum(squares, 0))
        for name, found in zip(names, parts):
            on_way[name].done(found)
            if on_way[name].halves is not None:
                arrived.append(on_way[name].halves[-1])
        return [parts[0][0]]

    d_state = None
    grads = {}
    d_embed = []
    for step in reversed(range(STEPS)):
        keep_enc, layers, keep_dec = records[step]
        final = step == 0
        d_nodes, d_grid, d_next, sums, grad = decoder_backward(
            step, regions, d_state, keep_dec, dec_weights, vectors, assign_row, delta, area, plan,
            inverse_total, *grads.get(N_DEC, (None, None)),
            (place, dec_rows, (0, dec_rows)) if final else None,
        )
        grads[N_DEC] = (grad if final else grad[0], sums)
        returned, d_edges = None, None
        after = []
        if final:
            on_way[N_DEC] = Sum(grad)
        for l in reversed(range(LAYERS)):
            old_grad, old_sums = grads.get(l, (None, None))
            found = layer_backward(
                l, d_nodes, returned, d_edges, layers[l], layer_weights[l], vectors,
                send_row, recv, picks_row, old_sums, after,
            )
            d_edges, sums = found[N_D_EDGES], found[N_SUMS]
            returned = exchange(found[N_D_HALO])
            after = advance(list(on_way), [sums]) + [returned] if final else []
            d_nodes, grad = layer_grads(
                found, layers[l], layer_weights[l][0], send_row, recv_row, layer_rows, old_grad,
                (place, layer_rows, (0, 4 * D, layer_rows)) if final else None, after,
            )
            grads[l] = (grad if final else grad[0], sums)
            after = advance([N_DEC, 2, 1], [d_nodes]) if final and l == 0 else []
            if final:
                on_way[l] = Sum(grad)
        d_embed.append(d_edges)
        others, swap = None, None
        if final:
            embed_sums, embed_grads = embed_backward(
                d_embed[0], d_embed[1], keep_embed, geometry, embed_inner, vectors, after
            )
            after = advance([0, 1, 2, N_DEC], [embed_sums])
            all_sums = {"embed": embed_sums}
            for name in [N_DEC] + list(range(LAYERS)):
                all_sums[name] = grads[name][1]
            others, swap = (embed_grads, all_sums), (place, start_rows, (0, start_rows))
        out = encoder_backward(
            step, d_grid, d_nodes, returned, d_next, keep_enc, (enc_first, enc_inner), vectors,
            assign, picks_row, scales, *grads.get(N_ENC, (None, None)), others, swap, after,
        )
        if not final:
            d_state, sums, grad = out
            grads[N_ENC] = (grad, sums)
    after = advance([N_DEC, 2, 1, 0], [out[0]])
    on_way["start"] = Sum(out, True)
    totals = None
    while any(item.halves is None for item in on_way.values()):
        after = advance(list(on_way), after)
        if totals is None and all(item.summed() for item in on_way.values()):
            squares_row = sum(all_squares)
            totals = over_all(jnp.stack([squares_row, jnp.broadcast_to(loss_local, (BLOCK,))]))
            arrived.append(totals)
    gradient_norm = jnp.sqrt(jnp.sum(totals[0]))
    loss_total = totals[1, 0]
    factor = jnp.minimum(1.0, clip_limit / gradient_norm)

    order = list(on_way)
    groups = [on_way[name].halves for name in order]
    last_group = len(groups) - 1
    chunks = []
    for l in reversed(range(LAYERS)):
        group = order.index(l)
        chunks += [(2, (l,), i * D, D, group, i * D) for i in range(3)]
        chunks.append((5, (2 + l,), 0, D, group, 3 * D))
        chunks += [(3, (l,), i * D, D, group, (4 + i) * D) for i in range(2)]
        chunks.append((5, (2 + LAYERS + l,), 0, D, group, 6 * D))
    chunks += [(4, (), i * D, D, 0, i * D) for i in range(2)]
    chunks.append((5, (last_block,), 0, D, 0, 2 * D))
    chunks.append((7, (), 0, variables, 0, 3 * D))
    chunks.append((0, (), 0, variables, last_group, 0))
    chunks.append((5, (0,), 0, D, last_group, depth))
    chunks.append((1, (), 0, features, last_group, depth + D))
    chunks.append((5, (1,), 0, D, last_group, depth + D + feature_rows))
    chunks.append((6, (), 0, vector_w.shape[0], last_group, at_vectors))
    *new, flat = update_weights(
        factor.reshape(1, 1), place, bits, groups, masters, moments, squares, chunks
    )
    weight_copies = flat.reshape(1, -1).astype(bf16)
    return (loss_total, weight_total, gradient_norm, *new, weight_copies)


def solution(mesh):
    two = P(None, N_REP)
    three = P(None, None, N_REP)
    weights = (two, two, three, three, two, three, two, two)
    placed = (
        P(N_REP, N_REGION, None),
        P(N_REP, None, N_REGION, None),
        P(),
        P(),
        P(),
        P(N_REGION, None),
        P(N_REGION),
        P(N_REGION),
        P(N_REGION),
        P(N_REGION),
        P(N_REGION, None, None),
        P(N_REGION),
        P(N_REGION),
        P(),
    ) + tuple(spec for spec in weights for _ in range(3))
    return jax.shard_map(
        body,
        mesh=mesh,
        in_specs=placed,
        out_specs=(P(), P(), P())
        + tuple(spec for spec in weights for _ in range(3))
        + (P(N_REP, None),),
        check_vma=False,
    )
```
